128 devices in a mesh: pool: 16 (over y, z), head: 8 (over x, core).
Axes of the slice: x: 4, y: 4, z: 4, core: 2. Of those that a mesh axis runs over, the one named last changes fastest.
Arguments:
- hidden: bfloat16 [16, 256, 5120], P('pool', None, 'head'), may hold values from -6 to 6
- snap_map: int32 [16], replicated, may hold values from 0 to 127
- pool_states: bfloat16 [128, 64, 64, 256], P('pool', 'head'), may hold values from -2.390625 to 2.390625
- w_zx: bfloat16 [5120, 2, 4096], P('pool', None, 'head'), may hold values from -0.078125 to 0.078125
- w_bc: bfloat16 [5120, 512], P('pool'), may hold values from -0.078125 to 0.078125
- w_dt: bfloat16 [5120, 64], P('pool', 'head'), may hold values from -0.078125 to 0.078125
- dt_bias: float32 [64], P('head'), may hold values from -6 to -2
- decay_rate: float32 [64], P('head'), may hold values from 0.05 to 2
- skip: float32 [64], P('head'), may hold values from 0.5 to 2
- norm_gain: float32 [4096], P('head'), may hold values from 0.1 to 1.9
- w_out: bfloat16 [4096, 5120], P('head', 'pool'), may hold values from -0.09375 to 0.09375
Outputs:
- mixed: bfloat16 [16, 256, 5120], P('pool', None, 'head')
- final_state: float32 [16, 64, 64, 256], P('pool', 'head')
The draws below stay inside these ranges and needn't reach their ends.
All inputs are finite; a program needn't handle non-finite values.
Results may differ from the reference program's by a relative error of at most 0.018.
Values may be sent and summed in bfloat16 or wider, within the bound.
A program may use at most 128 MiB of HBM per device.

```python
import math
import jax
import jax.numpy as jnp
import numpy as np
from jax import lax

D = 5120
HEADS = 64
HEAD_DIM = 64
STATE = 256
SPAN = 256
LENGTH = 256
REQS = 16
SNAPS = 128
INNER = 4096
N_HEAD = 8


def set_ends(values, stream_key, low, top_value):
    dims = values.shape
    spot = [jax.random.randint(jax.random.fold_in(stream_key, axis), (), 0, dims[axis]) for axis in range(len(dims))]
    values = values.at[tuple(spot)].set(low)
    longest = dims.index(max(dims))
    spot[longest] = (spot[longest] + 1) % dims[longest]
    return values.at[tuple(spot)].set(top_value)


def level_of(rng, dims, shards, least, top_value):
    factor_of = 1.0
    for axis_at, parts in shards:
        steps = jax.random.uniform(jax.random.fold_in(jax.random.fold_in(rng, 6), axis_at), (parts,), jnp.float32, least / len(shards), top_value / len(shards))
        factor_of = factor_of * jnp.repeat(jnp.exp(steps), dims[axis_at] // parts).reshape((-1,) + (1,) * (len(dims) - 1 - axis_at))
    return factor_of


def rank_table(amount, skew):
    loads = [(1 << 20) // math.isqrt(standing ** skew) + 1 for standing in range(1, amount + 1)]
    scale = 1 + sum(loads) // (1 << 30)
    return np.cumsum(np.array([max(1, weight // scale) for weight in loads]))


def ranked(rng, dims, number_of, slope):
    grid = rank_table(number_of, slope)
    ticket = jax.random.randint(jax.random.fold_in(rng, 1), dims, 0, int(grid[number_of - 1]))
    grade = jnp.searchsorted(jnp.asarray(grid, jnp.int32), ticket, side="right")
    return jax.random.permutation(jax.random.fold_in(rng, 2), number_of)[grade].astype(jnp.int32)


def scatter_about(stream_key, dims, width, limit, cuts=(), kind=jnp.bfloat16):
    entries = width * jax.random.normal(stream_key, dims, jnp.float32)
    if cuts:
        entries = entries * level_of(stream_key, dims, cuts, -0.22, 0.18)
    return jnp.clip(entries, -limit, limit).astype(kind)


def setup_inputs(seed: int = 0) -> dict:
    key_of = jax.random.split(jax.random.key(seed), 12)
    hidden = scatter_about(key_of[0], (REQS, LENGTH, D), 1.0, 6.0, ((0, 16), (2, 8)))
    snap_map = set_ends(ranked(key_of[1], (REQS,), SNAPS, 2), jax.random.fold_in(key_of[1], 3), 0, SNAPS - 1).astype(jnp.int32)
    pool_states = scatter_about(key_of[2], (SNAPS, HEADS, HEAD_DIM, STATE), 0.3, 2.390625, ((0, 16), (1, 8)))
    w_zx = scatter_about(key_of[3], (D, 2, INNER), D ** -0.5, 0.078125, ((0, 16), (2, 8)))
    w_bc = scatter_about(key_of[4], (D, 2 * STATE), D ** -0.5, 0.078125, ((0, 16),))
    w_dt = scatter_about(key_of[5], (D, HEADS), D ** -0.5, 0.078125, ((0, 16), (1, 8)))
    dt_bias = jnp.clip(-6.0 + 4.0 * jax.random.uniform(key_of[6], (HEADS,), jnp.float32) ** level_of(key_of[6], (HEADS,), ((0, 8),), -0.2, 0.2), -6.0, -2.0)
    decay_rate = jnp.clip(jnp.exp(math.log(2.0) - 3.6888794 * jax.random.uniform(key_of[7], (HEADS,), jnp.float32) ** level_of(key_of[7], (HEADS,), ((0, 8),), -0.2, 0.2)), 0.05, 2.0)
    skip = jnp.clip(0.5 + 1.5 * jax.random.uniform(key_of[8], (HEADS,), jnp.float32) ** level_of(key_of[8], (HEADS,), ((0, 8),), -0.2, 0.2), 0.5, 2.0)
    norm_gain = jnp.clip(1.0 + 0.18 * jax.random.normal(key_of[9], (INNER,), jnp.float32), 0.1, 1.9)
    w_out = scatter_about(key_of[10], (INNER, D), INNER ** -0.5, 0.09375, ((0, 8), (1, 16)))
    return dict(hidden=hidden, snap_map=snap_map, pool_states=pool_states, w_zx=w_zx, w_bc=w_bc, w_dt=w_dt, dt_bias=dt_bias, decay_rate=decay_rate, skip=skip, norm_gain=norm_gain, w_out=w_out)


def span_scan(values, steps_dt, bmat, cmat, rate, start_state):
    highest = lax.Precision.HIGHEST
    tokens_n, heads_n, head_dim = values.shape
    state_dim = bmat.shape[1]
    spans = tokens_n // SPAN
    cumlog = jnp.cumsum((-(rate[None, :] * steps_dt)).reshape(spans, SPAN, heads_n), axis=1)
    lower = (jnp.arange(SPAN)[:, None] >= jnp.arange(SPAN)[None, :])[None, :, :, None]
    spread = jnp.where(lower, cumlog[:, :, None, :] - cumlog[:, None, :, :], 0.0)
    decays = jnp.where(lower, jnp.exp(spread), 0.0)
    bsplit = bmat.reshape(spans, SPAN, state_dim)
    csplit = cmat.reshape(spans, SPAN, state_dim)
    scores = jnp.einsum('kin,kjn->kij', csplit, bsplit, precision=highest)
    weighted = (values * steps_dt[:, :, None]).reshape(spans, SPAN, heads_n, head_dim)
    within = jnp.einsum('kijh,kjhp->kihp', scores[:, :, :, None] * decays, weighted, precision=highest)
    tail_decay = jnp.exp(cumlog[:, -1:, :] - cumlog)
    states = jnp.einsum('kjhp,kjn->khpn', weighted * tail_decay[:, :, :, None], bsplit, precision=highest)
    span_decay = jnp.exp(cumlog[:, -1, :])

    def advance(carry, items):
        factor, added = items
        return (factor[:, None, None] * carry + added, carry)
    final, starts = lax.scan(advance, start_state, (span_decay, states))
    carried = jnp.exp(cumlog)[:, :, :, None] * jnp.einsum('kin,khpn->kihp', csplit, starts, precision=highest)
    return ((within + carried).reshape(tokens_n, heads_n, head_dim), final, cumlog)

def one_request(items, snap_map, pool_states, w_zx, w_bc, w_dt, dt_bias, decay_rate, skip, norm_gain, w_out):
    tokens, which = items
    proj_zx = jnp.dot(tokens, w_zx.reshape(D, 2 * INNER), preferred_element_type=jnp.float32)
    gate_part = proj_zx[:, :INNER].astype(jnp.bfloat16)
    inputs = proj_zx[:, INNER:].astype(jnp.bfloat16)
    maps = jnp.dot(tokens, w_bc, preferred_element_type=jnp.float32).astype(jnp.bfloat16)
    steps_dt = jax.nn.softplus(jnp.dot(tokens, w_dt, preferred_element_type=jnp.float32) + dt_bias[None, :])
    start_state = pool_states[which].astype(jnp.float32)
    values = inputs.astype(jnp.float32).reshape(LENGTH, HEADS, HEAD_DIM)
    bmat = maps[:, :STATE].astype(jnp.float32)
    cmat = maps[:, STATE:].astype(jnp.float32)
    scanned, final, cumlog = span_scan(values, steps_dt, bmat, cmat, decay_rate, start_state)
    gate_vals = gate_part.astype(jnp.float32).reshape(LENGTH, HEADS, HEAD_DIM)
    gated = (scanned + skip[None, :, None] * values) * jax.nn.silu(gate_vals)
    meansq = lax.optimization_barrier(jnp.mean(gated * gated, axis=-1, keepdims=True))
    normed = gated * lax.rsqrt(meansq + 1e-05) * norm_gain.reshape(HEADS, HEAD_DIM)[None, :, :]
    normed = normed.reshape(LENGTH, INNER).astype(jnp.bfloat16)
    group = INNER // N_HEAD
    total = jnp.zeros((LENGTH, D), jnp.float32)
    for index in range(N_HEAD):
        partial_term = jnp.dot(normed[:, index * group:(index + 1) * group], w_out[index * group:(index + 1) * group, :], preferred_element_type=jnp.float32)
        rounded = lax.optimization_barrier(partial_term.astype(jnp.bfloat16))
        total = total + rounded.astype(jnp.float32)
    return (total.astype(jnp.bfloat16), final)

def reference(hidden, snap_map, pool_states, w_zx, w_bc, w_dt, dt_bias, decay_rate, skip, norm_gain, w_out):

    def per_request(items):
        return one_request(items, snap_map, pool_states, w_zx, w_bc, w_dt, dt_bias, decay_rate, skip, norm_gain, w_out)
    mixed, final_state = lax.map(per_request, (hidden, snap_map))
    return (mixed, final_state)
```

```python
import jax
import jax.numpy as jnp
from jax import lax
from jax.experimental import pallas as pl
from jax.experimental.pallas import tpu as pltpu
from jax.sharding import PartitionSpec as P

F32 = jnp.float32
BF16 = jnp.bfloat16
MESH = pl.DeviceIdType.MESH
VMEM = pltpu.VMEM

HEADS_HERE = 8
N_SEM = 176
CH = 384


def dot_nn(a, b):
    return lax.dot_general(a, b, (((1,), (0,)), ((), ())), preferred_element_type=F32)


def dot_nt(a, b):
    return lax.dot_general(a, b, (((1,), (1,)), ((), ())), preferred_element_type=F32)


def dot_tn(a, b):
    return lax.dot_general(a, b, (((0,), (0,)), ((), ())), preferred_element_type=F32)


def body(
    snap,
    hid,
    wcat,
    wout_t,
    pool,
    small,
    mix_out,
    fin_out,
    xs_,
    ws_,
    p2,
    p1,
    p3,
    r2a,
    r2b,
    r1a,
    r1b,
    pz,
    maps,
    f2,
    f1,
    f3,
    tt,
    q2a,
    q2b,
    q1a,
    q1b,
    g1,
    g3,
    v2a,
    v2b,
    v1a,
    v1b,
    start,
    nb,
    wo,
    keep,
    cs,
    cr,
    o2,
    o1,
    o3,
    e2a,
    e2b,
    e1a,
    e1b,
    fs,
    mt,
    ss,
    rs,
):
    p = lax.axis_index("pool")
    h = lax.axis_index("head")
    y = p // 4
    z = lax.rem(p, 4)
    x = h // 2
    c = lax.rem(h, 2)
    sz = lax.rem(z, 2)
    zc = z // 2

    def m4(v):
        return lax.rem(v, 4)

    def dev(yy, zz, xx, cc):
        return (yy * 4 + zz, xx * 2 + cc)

    yp, ym = dev(m4(y + 1), z, x, c), dev(m4(y + 3), z, x, c)
    zp, zm = dev(y, m4(z + 1), x, c), dev(y, m4(z + 3), x, c)
    xp, xm = dev(y, z, m4(x + 1), c), dev(y, z, m4(x + 3), c)
    sib = dev(y, z, x, 1 - c)

    used = [0]
    sent = []

    def take(n=1):
        i = used[0]
        used[0] += n
        assert used[0] <= N_SEM
        return i

    def copy_of(src, dst, to, si, ri):
        return pltpu.make_async_remote_copy(
            src_ref=src, dst_ref=dst, send_sem=ss.at[si], recv_sem=rs.at[ri], device_id=to, device_id_type=MESH
        )

    def send(src, dst, to):
        i = take()
        cp = copy_of(src, dst, to, i, i)
        cp.start()
        sent.append(cp)
        return cp

    def mo(v, n):
        return pl.multiple_of(v, n)

    barrier = pltpu.get_barrier_semaphore()
    peers = [(p, lax.rem(h + i, 8)) for i in range(1, 8)]
    peers += [dev(y, m4(z + i), x, cc) for i in range(1, 4) for cc in range(2)]
    peers += [yp, ym]
    for peer in peers:
        pl.semaphore_signal(barrier, inc=1, device_id=peer, device_id_type=MESH)
    pl.semaphore_wait(barrier, len(peers))

    hs_sem = take(4)
    hr_sem = take(4)
    h0_local = []

    def x_block(req, half_off, rows, xx):
        return xs_.at[pl.ds(mo(req * 256 + half_off, 64), rows), pl.ds(mo(xx * 384, 128), 384)]

    def h0():
        for s in range(2):
            for d in range(2):
                local = (z == 2 * c + s) & (c == d)
                src = hid.at[pl.ds(d * 128, 128), pl.ds(256 * s, 384)]
                dst = x_block(z, d * 128, 128, x)
                cp = copy_of(src, dst, dev(y, 2 * c + s, x, d), hs_sem + 2 * s + d, hr_sem + z)
                h0_local.append((local, cp))

                @pl.when(jnp.logical_not(local))
                def _(cp=cp):
                    cp.start()

                @pl.when(local)
                def _(s=s, d=d):
                    xs_[pl.ds(mo(z * 256 + d * 128, 64), 128), pl.ds(mo(x * 384, 128), 384)] = hid[
                        d * 128 : d * 128 + 128, 256 * s : 256 * s + 384
                    ]

    hc = {}

    def hs(rr):
        zr = m4(z + rr)
        blk = x_block(zr, c * 128, 128, x)
        got = copy_of(blk, blk, sib, hs_sem, hr_sem + zr)
        if rr == 0:

            @pl.when(c != zc)
            def _():
                got.wait_recv()
        else:
            got.wait_recv()
        hc[rr, "p"] = send(blk, blk, xp)
        hc[rr, "m"] = send(blk, blk, xm)
        hc[rr, "s0"] = send(blk, blk, sib)

    def hf(rr):
        zr = m4(z + rr)
        hc[rr, "p"].wait_recv()
        fw = x_block(zr, c * 128, 64, m4(x + 3))
        hc[rr, "fp"] = send(fw, fw, xp)
        blk = x_block(zr, c * 128, 128, m4(x + 3))
        hc[rr, "s1"] = send(blk, blk, sib)
        hc[rr, "m"].wait_recv()
        fw = x_block(zr, c * 128 + 64, 64, m4(x + 1))
        hc[rr, "fm"] = send(fw, fw, xm)
        blk = x_block(zr, c * 128, 128, m4(x + 1))
        hc[rr, "s2"] = send(blk, blk, sib)

    def hg(rr):
        zr = m4(z + rr)
        hc[rr, "fp"].wait_recv()
        hc[rr, "fm"].wait_recv()
        blk = x_block(zr, c * 128, 128, m4(x + 2))
        hc[rr, "s3"] = send(blk, blk, sib)

    def hw(rr):
        for k in ("s0", "s1", "s2", "s3"):
            hc[rr, k].wait_recv()

    def w_block(i, off, rows, n):
        return ws_.at[pl.ds(mo(384 * i + 64 * sz + off, 32), rows), pl.ds(n * CH, CH)]

    wc = {}

    def w_init():
        for i in range(4):
            ws_[pl.ds(mo(384 * i + 320 * (1 - sz), 64), 64), :] = jnp.zeros((64, 3 * CH), BF16)
        ws_[pl.ds(mo(384 * y + 64 * sz, 64), 320), :] = wcat[...]

    def w0(n):
        src = wcat.at[:, pl.ds(n * CH, CH)]
        dst = w_block(y, 0, 320, n)
        wc[n, "p"] = send(src, dst, yp)
        wc[n, "m"] = send(src, dst, ym)

    def wf(n):
        wc[n, "p"].wait_recv()
        fw = w_block(m4(y + 3), 0, 160, n)
        wc[n, "fp"] = send(fw, fw, yp)
        wc[n, "m"].wait_recv()
        fw = w_block(m4(y + 1), 160, 160, n)
        wc[n, "fm"] = send(fw, fw, ym)

    def wg(n):
        wc[n, "fp"].wait_recv()
        wc[n, "fm"].wait_recv()

    pc = {}

    def part(n, rr):
        zr = m4(z + rr)
        return dot_nn(xs_[pl.ds(mo(zr * 256, 256), 256), :], ws_[:, n * CH : (n + 1) * CH])

    def pa(n):
        p2[n] = part(n, 2).astype(BF16)
        pc[n, "2a"] = send(p2.at[n, pl.ds(0, 128)], r2a.at[n], zp)
        pc[n, "2b"] = send(p2.at[n, pl.ds(128, 128)], r2b.at[n], zm)

    def pb(n):
        a = part(n, 1)
        p1[n, 128:] = a[128:].astype(BF16)
        pc[n, "1ah"] = send(p1.at[n, pl.ds(128, 128)], r1a.at[n, pl.ds(128, 128)], zp)
        b = part(n, 3)
        p3[n, :128] = b[:128].astype(BF16)
        pc[n, "1bl"] = send(p3.at[n, pl.ds(0, 128)], r1b.at[n, pl.ds(0, 128)], zm)
        pc[n, "2a"].wait_recv()
        p1[n, :128] = (a[:128] + r2a[n].astype(F32)).astype(BF16)
        pc[n, "1al"] = send(p1.at[n, pl.ds(0, 128)], r1a.at[n, pl.ds(0, 128)], zp)
        pc[n, "2b"].wait_recv()
        p3[n, 128:] = (b[128:] + r2b[n].astype(F32)).astype(BF16)
        pc[n, "1bh"] = send(p3.at[n, pl.ds(128, 128)], r1b.at[n, pl.ds(128, 128)], zm)

    def pd(n):
        own = part(n, 0)
        for k in ("1ah", "1al", "1bl", "1bh"):
            pc[n, k].wait_recv()
        pz[:, n * CH : (n + 1) * CH] = (own + r1a[n].astype(F32) + r1b[n].astype(F32)).astype(BF16)

    mr_sem = take(8)
    mc = []

    def m0():
        maps[h] = pz[:, :128]
        for i in range(1, 8):
            si = take()
            cp = copy_of(pz.at[:, pl.ds(0, 128)], maps.at[h], (p, lax.rem(h + i, 8)), si, mr_sem + h)
            cp.start()
            sent.append(cp)

    def mw():
        for i in range(1, 8):
            o = lax.rem(h + i, 8)
            copy_of(maps.at[o], maps.at[o], sib, mr_sem, mr_sem + o).wait_recv()

    sc = {}
    axes = (((y, yp, ym), (z, zp, zm)), ((z, zp, zm), (y, yp, ym)))

    def pick(half, a, b):
        r = a * 4 + b if half == 0 else b * 4 + a
        idx = snap[r]
        v = pool[lax.rem(idx, 8), half * 256 : half * 256 + 256, :]
        return jnp.where(idx // 8 == p, v, jnp.zeros_like(v))

    def s0(u):
        (a, ap, am), _ = axes[u]
        for b in range(4):
            f2[u, b] = pick(u, m4(a + 2), b)
            if b == 1:
                sc[u, "2a"] = send(f2.at[u, pl.ds(0, 2)], q2a.at[u], ap)
        sc[u, "2b"] = send(f2.at[u, pl.ds(2, 2)], q2b.at[u], am)
        for b in (2, 3):
            f1[u, b] = pick(u, m4(a + 1), b)
        sc[u, "1ah"] = send(f1.at[u, pl.ds(2, 2)], q1a.at[u, pl.ds(2, 2)], ap)
        for b in (0, 1):
            f3[u, b] = pick(u, m4(a + 3), b)
        sc[u, "1bl"] = send(f3.at[u, pl.ds(0, 2)], q1b.at[u, pl.ds(0, 2)], am)

    def s1(u):
        (a, ap, am), _ = axes[u]
        sc[u, "2a"].wait_recv()
        for b in (0, 1):
            f1[u, b] = pick(u, m4(a + 1), b) + q2a[u, b]
        sc[u, "1al"] = send(f1.at[u, pl.ds(0, 2)], q1a.at[u, pl.ds(0, 2)], ap)
        sc[u, "2b"].wait_recv()
        for b in (2, 3):
            f3[u, b] = pick(u, m4(a + 3), b) + q2b[u, b - 2]
        sc[u, "1bh"] = send(f3.at[u, pl.ds(2, 2)], q1b.at[u, pl.ds(2, 2)], am)

    def s2(u):
        (a, _, _), (b0, bp, bm) = axes[u]
        sc[u, "1ah"].wait_recv()
        sc[u, "1bl"].wait_recv()
        sc[u, "1al"].wait_recv()
        sc[u, "1bh"].wait_recv()
        for b in range(4):
            tt[u, b] = pick(u, a, b) + q1a[u, b] + q1b[u, b]
        far, nxt, prv = m4(b0 + 2), m4(b0 + 1), m4(b0 + 3)
        sc[u, "v2a"] = send(tt.at[u, far, pl.ds(0, 128)], v2a.at[u], bp)
        sc[u, "v2b"] = send(tt.at[u, far, pl.ds(128, 128)], v2b.at[u], bm)
        sc[u, "v1ah"] = send(tt.at[u, nxt, pl.ds(128, 128)], v1a.at[u, pl.ds(128, 128)], bp)
        sc[u, "v1bl"] = send(tt.at[u, prv, pl.ds(0, 128)], v1b.at[u, pl.ds(0, 128)], bm)

    def s3(u):
        _, (b0, bp, bm) = axes[u]
        nxt, prv = m4(b0 + 1), m4(b0 + 3)
        sc[u, "v2a"].wait_recv()
        g1[u] = tt[u, nxt, :128, :] + v2a[u]
        sc[u, "v1al"] = send(g1.at[u], v1a.at[u, pl.ds(0, 128)], bp)
        sc[u, "v2b"].wait_recv()
        g3[u] = tt[u, prv, 128:, :] + v2b[u]
        sc[u, "v1bh"] = send(g3.at[u], v1b.at[u, pl.ds(128, 128)], bm)

    def s4(u):
        _, (b0, _, _) = axes[u]
        for k in ("v1ah", "v1bl", "v1al", "v1bh"):
            sc[u, k].wait_recv()
        start[u * 256 : u * 256 + 256] = tt[u, b0] + v1a[u] + v1b[u]

    oc = {}

    def wo0():
        wo[y] = wout_t[...]
        oc["p"] = send(wout_t, wo.at[y], yp)
        oc["m"] = send(wout_t, wo.at[y], ym)

    def wof():
        oc["p"].wait_recv()
        fw = wo.at[m4(y + 3), pl.ds(0, 160)]
        oc["fp"] = send(fw, fw, yp)
        oc["m"].wait_recv()
        fw = wo.at[m4(y + 1), pl.ds(160, 160)]
        oc["fm"] = send(fw, fw, ym)

    def wog():
        oc["fp"].wait_recv()
        oc["fm"].wait_recv()

    nc = {}

    def scan():
        dtile = pz[:, :128].astype(F32)
        dtile = jnp.where(c == 0, pltpu.roll(dtile, 64, 1), dtile)
        v = dtile + small[0:1, :128]
        dt = jnp.maximum(v, 0.0) + jnp.log1p(jnp.exp(-jnp.abs(v)))
        rowi = lax.broadcasted_iota(jnp.int32, (256, 256), 0)
        coli = lax.broadcasted_iota(jnp.int32, (256, 256), 1)
        lower = rowi >= coli
        tri = jnp.where(lower, 1.0, 0.0).astype(F32)
        cum = lax.dot_general(
            tri,
            -(small[1:2, :128] * dt),
            (((1,), (0,)), ((), ())),
            precision=lax.Precision.HIGHEST,
            preferred_element_type=F32,
        )
        ecum = jnp.exp(cum)
        tail = jnp.exp(cum[255:256, :] - cum) * dt
        cum_t = cum.T
        dt_t = dt.T
        lane = lax.broadcasted_iota(jnp.int32, (256, 128), 1)
        first = lane < 64
        bmat = jnp.concatenate([jnp.where(first, maps[2 * i], maps[2 * i + 1]) for i in range(2)], axis=1)
        cmat = jnp.concatenate([jnp.where(first, maps[4 + 2 * i], maps[5 + 2 * i]) for i in range(2)], axis=1)
        scores = dot_nt(cmat, bmat)
        r128 = lax.broadcasted_iota(jnp.int32, (128, 128), 0) // 64
        c128 = lax.broadcasted_iota(jnp.int32, (128, 128), 1) // 64
        same = jnp.where(r128 == c128, 1.0 / 64.0, 0.0).astype(BF16)
        rows_first = lax.broadcasted_iota(jnp.int32, (128, 256), 0) < 64
        for k in range(4):
            lo, hi = 2 * k, 2 * k + 1
            cols = slice(128 * k, 128 * k + 128)
            xv = pz[:, 640 + 128 * k : 768 + 128 * k]
            gate = pz[:, 128 + 128 * k : 256 + 128 * k].astype(F32)
            xf = xv.astype(F32)

            def within(q):
                spread = jnp.where(lower, cum[:, q : q + 1] - cum_t[q : q + 1, :], -1e30)
                mix = jnp.exp(spread) * dt_t[q : q + 1, :] * scores
                return dot_nn(mix.astype(BF16), xv)

            def spread2(a):
                return jnp.where(first, a[:, lo : lo + 1], a[:, hi : hi + 1])

            s_in = start[128 * k : 128 * k + 128, :]
            carried = spread2(ecum) * dot_nt(cmat, s_in)
            scanned = jnp.where(first, within(lo), within(hi)) + carried
            gated = (scanned + small[2:3, cols] * xf) * (gate / (1.0 + jnp.exp(-gate)))
            sq = gated * gated
            sq_hi = sq.astype(BF16)
            sq_lo = (sq - sq_hi.astype(F32)).astype(BF16)
            meansq = dot_nn(sq_hi, same) + dot_nn(sq_lo, same)
            normed = gated * lax.rsqrt(meansq + 1e-05) * small[3:4, cols]
            nb[z, :, cols] = normed.astype(BF16)
            blk = nb.at[z, :, pl.ds(128 * k, 128)]
            nc[k, "p"] = send(blk, blk, zp)
            nc[k, "m"] = send(blk, blk, zm)
            weighted = (xf * spread2(tail)).astype(BF16)
            last = jnp.where(rows_first, ecum[255:256, lo : lo + 1], ecum[255:256, hi : hi + 1])
            fin_out[128 * k : 128 * k + 128, :] = last * s_in.astype(F32) + dot_tn(weighted, bmat)

    def nf():
        for k in range(4):
            nc[k, "p"].wait_recv()
            fw = nb.at[m4(z + 3), pl.ds(0, 128), pl.ds(128 * k, 128)]
            nc[k, "fp"] = send(fw, fw, zp)
            nc[k, "m"].wait_recv()
            fw = nb.at[m4(z + 1), pl.ds(128, 128), pl.ds(128 * k, 128)]
            nc[k, "fm"] = send(fw, fw, zm)

    def ng():
        for k in range(4):
            nc[k, "fp"].wait_recv()
            nc[k, "fm"].wait_recv()

    xc = {}
    fr_sem = take(4)
    fin_copies = []

    def oa(rr):
        n = nb[m4(z + rr)]
        for ii in (2, 1, 3, 0):
            o = dot_nt(wo[m4(x + ii)], n)
            left, right = o[:, :128], o[:, 128:]
            keep[rr, ii] = jnp.where(c == 0, left, right)
            cs[rr, ii] = jnp.where(c == 0, right, left).astype(BF16)
        xc[rr, "c"] = send(cs.at[rr], cr.at[rr], sib)

    def ob(rr):
        xc[rr, "c"].wait_recv()
        o2[rr] = (keep[rr, 2] + cr[rr, 2].astype(F32)).astype(BF16)
        xc[rr, "2a"] = send(o2.at[rr, pl.ds(0, 160)], e2a.at[rr], xp)
        xc[rr, "2b"] = send(o2.at[rr, pl.ds(160, 160)], e2b.at[rr], xm)
        o1[rr, 160:] = (keep[rr, 1, 160:] + cr[rr, 1, 160:].astype(F32)).astype(BF16)
        xc[rr, "1ah"] = send(o1.at[rr, pl.ds(160, 160)], e1a.at[rr, pl.ds(160, 160)], xp)
        o3[rr, :160] = (keep[rr, 3, :160] + cr[rr, 3, :160].astype(F32)).astype(BF16)
        xc[rr, "1bl"] = send(o3.at[rr, pl.ds(0, 160)], e1b.at[rr, pl.ds(0, 160)], xm)

    def od(rr):
        xc[rr, "2a"].wait_recv()
        o1[rr, :160] = (keep[rr, 1, :160] + cr[rr, 1, :160].astype(F32) + e2a[rr].astype(F32)).astype(BF16)
        xc[rr, "1al"] = send(o1.at[rr, pl.ds(0, 160)], e1a.at[rr, pl.ds(0, 160)], xp)
        xc[rr, "2b"].wait_recv()
        o3[rr, 160:] = (keep[rr, 3, 160:] + cr[rr, 3, 160:].astype(F32) + e2b[rr].astype(F32)).astype(BF16)
        xc[rr, "1bh"] = send(o3.at[rr, pl.ds(160, 160)], e1b.at[rr, pl.ds(160, 160)], xm)

    def oe(rr):
        for k in ("1ah", "1bl", "1al", "1bh"):
            xc[rr, k].wait_recv()
        total = keep[rr, 0] + cr[rr, 0].astype(F32) + e1a[rr].astype(F32) + e1b[rr].astype(F32)
        fs[rr] = total.astype(BF16)
        dst = mt.at[pl.ds(mo(sz * 320, 64), 320), pl.ds(mo(c * 128, 128), 128)]
        cp = copy_of(fs.at[rr], dst, dev(y, m4(z + rr), x, zc), take(), fr_sem + 2 * sz + c)
        if rr == 0:

            @pl.when(c != zc)
            def _():
                cp.start()

            @pl.when(c == zc)
            def _():
                mt[pl.ds(mo(sz * 320, 64), 320), pl.ds(mo(c * 128, 128), 128)] = fs[0]
        else:
            cp.start()
        fin_copies.append((rr, cp))

    def of():
        for s in range(2):
            for cc in range(2):
                dst = mt.at[pl.ds(s * 320, 320), pl.ds(cc * 128, 128)]
                got = copy_of(dst, dst, sib, hs_sem, fr_sem + 2 * s + cc)
                local = (z == 2 * c + s) & (c == cc)

                @pl.when(jnp.logical_not(local))
                def _(got=got):
                    got.wait_recv()

        mix_out[...] = mt[...]

    h0()
    w0(0)
    s0(1)
    w_init()
    hs(2)
    hs(1)
    hs(3)
    hs(0)
    hf(2)
    hf(1)
    wf(0)
    w0(1)
    hf(3)
    hg(2)
    hf(0)
    hg(1)
    hg(3)
    hg(0)
    wg(0)
    hw(2)
    pa(0)
    hw(1)
    hw(3)
    s1(1)
    pb(0)
    wf(1)
    w0(2)
    hw(0)
    wg(1)
    pa(1)
    pd(0)
    m0()
    wf(2)
    s0(0)
    pb(1)
    wg(2)
    pa(2)
    s2(1)
    pd(1)
    pb(2)
    s3(1)
    s1(0)
    pd(2)
    s4(1)
    wo0()
    s2(0)
    s3(0)
    wof()
    s4(0)
    mw()
    scan()
    wog()
    oa(0)
    nf()
    ob(0)
    oa(1)
    od(0)
    ob(1)
    oa(3)
    od(1)
    ob(3)
    oe(0)
    ng()
    oa(2)
    od(3)
    ob(2)
    oe(1)
    oe(3)
    od(2)
    oe(2)
    of()

    for cp in sent:
        cp.wait_send()
    for local, cp in h0_local:

        @pl.when(jnp.logical_not(local))
        def _(cp=cp):
            cp.wait_send()

    for rr, cp in fin_copies:
        if rr == 0:

            @pl.when(c != zc)
            def _(cp=cp):
                cp.wait_send()
        else:
            cp.wait_send()


def shards(hidden, snap_map, pool_states, w_zx, w_bc, w_dt, dt_bias, decay_rate, skip, norm_gain, w_out):
    h = lax.axis_index("head")
    c = lax.rem(h, 2)
    w_b = lax.dynamic_slice_in_dim(w_bc, h * 64, 64, axis=1)
    w_d = jnp.pad(w_dt, ((0, 0), (0, 56)))
    tile = jnp.where(c == 0, jnp.concatenate([w_b, w_d], 1), jnp.concatenate([w_d, w_b], 1))
    wcat = jnp.concatenate([tile, w_zx.reshape(320, 1024)], axis=1)
    small = jnp.stack(
        [
            jnp.pad(dt_bias, (0, 504)),
            jnp.pad(decay_rate, (0, 504)),
            jnp.repeat(skip, 64),
            norm_gain,
        ]
        + [jnp.zeros((512,), F32)] * 4
    )
    vm = pl.BlockSpec(memory_space=VMEM)
    scratch = [
        VMEM((1024, 1536), BF16),
        VMEM((1536, 3 * CH), BF16),
        *[VMEM((3, 256, CH), BF16)] * 3,
        *[VMEM((3, 128, CH), BF16)] * 2,
        *[VMEM((3, 256, CH), BF16)] * 2,
        VMEM((256, 3 * CH), BF16),
        VMEM((8, 256, 128), BF16),
        *[VMEM((2, 4, 256, 256), BF16)] * 4,
        *[VMEM((2, 2, 256, 256), BF16)] * 2,
        *[VMEM((2, 4, 256, 256), BF16)] * 2,
        *[VMEM((2, 128, 256), BF16)] * 4,
        *[VMEM((2, 256, 256), BF16)] * 2,
        VMEM((512, 256), BF16),
        VMEM((4, 256, 512), BF16),
        VMEM((4, 320, 512), BF16),
        VMEM((4, 4, 320, 128), F32),
        *[VMEM((4, 4, 320, 128), BF16)] * 2,
        *[VMEM((4, 320, 128), BF16)] * 3,
        *[VMEM((4, 160, 128), BF16)] * 2,
        *[VMEM((4, 320, 128), BF16)] * 3,
        VMEM((640, 256), BF16),
        pltpu.SemaphoreType.DMA((N_SEM,)),
        pltpu.SemaphoreType.DMA((N_SEM,)),
    ]
    mixed_t, final = pl.pallas_call(
        body,
        out_shape=(jax.ShapeDtypeStruct((640, 256), BF16), jax.ShapeDtypeStruct((512, 256), F32)),
        in_specs=[pl.BlockSpec(memory_space=pltpu.SMEM)] + [vm] * 5,
        out_specs=(vm, vm),
        scratch_shapes=scratch,
        compiler_params=pltpu.CompilerParams(
            collective_id=0, has_side_effects=True, vmem_limit_bytes=56 * 1024 * 1024
        ),
    )(snap_map, hidden.reshape(256, 640), wcat, w_out.T, pool_states.reshape(8, 512, 256), small)
    return mixed_t.T.reshape(1, 256, 640), final.reshape(1, 8, 64, 256)


def solution(mesh):
    in_specs = (
        P("pool", None, "head"),
        P(),
        P("pool", "head", None, None),
        P("pool", None, "head"),
        P("pool", None),
        P("pool", "head"),
        P("head"),
        P("head"),
        P("head"),
        P("head"),
        P("head", "pool"),
    )
    out_specs = (P("pool", None, "head"), P("pool", "head", None, None))
    return jax.shard_map(shards, mesh=mesh, in_specs=in_specs, out_specs=out_specs, check_vma=False)
```

```python
import jax
import jax.numpy as jnp
from jax import lax
from jax.experimental import pallas as pl
from jax.experimental.pallas import tpu as pltpu
from jax.sharding import PartitionSpec as P

F32 = jnp.float32
BF16 = jnp.bfloat16
MESH = pl.DeviceIdType.MESH
VMEM = pltpu.VMEM

N_SEM = 176
CH = 384


ORDER = (
    "h0",
    "w_cat",
    "w0 0",
    "s0 1",
    "w0 1",
    "w0 2",
    "w_init",
    "s0 0",
    "hs 2",
    "hs 1",
    "hs 3",
    "hs 0",
    "hf 2",
    "hf 1",
    "wf 0",
    "hf 3",
    "hg 2",
    "hf 0",
    "hg 1",
    "hg 3",
    "hg 0",
    "s1 1",
    "wf 1",
    "wg 0",
    "hw 2",
    "pa 0",
    "hw 1",
    "hw 3",
    "pb 0",
    "wf 2",
    "hw 0",
    "wg 1",
    "pa 1",
    "pd 0",
    "m0",
    "s1 0",
    "pb 1",
    "wg 2",
    "pa 2",
    "s2 1",
    "pd 1",
    "pb 2",
    "s3 1",
    "s2 0",
    "pd 2",
    "mw",
    "wo0",
    "scan_a",
    "s4 1",
    "s3 0",
    "wof",
    "s4 0",
    "scan_b 0",
    "scan_b 1",
    "scan_b 2",
    "scan_b 3",
    "wog",
    "nw",
    "wow",
    "oa 0",
    "nf 0",
    "nf 1",
    "od 0",
    "oa 1",
    "oa 3",
    "ng",
    "oe 0",
    "oa 2",
    "od 1",
    "od 3",
    "od 2",
    "oe 1",
    "oe 3",
    "oe 2",
    "final",
    "of",
)


class Sent:
    def __init__(self, copy):
        self.copy = copy
        self.got = False
        copy.start()

    def wait_recv(self):
        assert not self.got
        self.got = True
        self.copy.wait_recv()

    def finish(self):
        if not self.got:
            self.wait_recv()
        self.copy.wait_send()


def dot_nn(a, b):
    return lax.dot_general(a, b, (((1,), (0,)), ((), ())), preferred_element_type=F32)


def dot_nt(a, b):
    return lax.dot_general(a, b, (((1,), (1,)), ((), ())), preferred_element_type=F32)


def dot_tn(a, b):
    return lax.dot_general(a, b, (((0,), (0,)), ((), ())), preferred_element_type=F32)


def body(
    snap,
    bias,
    rate,
    skip,
    gain,
    hid,
    wzx,
    wbc,
    wdt,
    wout_t,
    pool,
    mix_out,
    fin_out,
    wcat,
    xs_,
    ws_,
    p2,
    p1,
    p3,
    r2a,
    r2b,
    r1a,
    r1b,
    pz,
    maps,
    f2,
    f1,
    f3,
    tt,
    q2a,
    q2b,
    q1a,
    q1b,
    g1,
    g3,
    v2a,
    v2b,
    v1a,
    v1b,
    start,
    wi,
    wt,
    bc,
    ns,
    nbuf,
    wo,
    k0,
    k1,
    k3,
    o2,
    o1,
    o3,
    e2a,
    e2b,
    e1a,
    e1b,
    fs,
    mt,
    ss,
    rs,
):
    p = lax.axis_index("pool")
    h = lax.axis_index("head")
    y = p // 4
    z = lax.rem(p, 4)
    x = h // 2
    c = lax.rem(h, 2)
    sz = lax.rem(z, 2)
    zc = z // 2

    def m4(v):
        return lax.rem(v, 4)

    def dev(yy, zz, xx, cc):
        return (yy * 4 + zz, xx * 2 + cc)

    yp, ym = dev(m4(y + 1), z, x, c), dev(m4(y + 3), z, x, c)
    zp, zm = dev(y, m4(z + 1), x, c), dev(y, m4(z + 3), x, c)
    xp, xm = dev(y, z, m4(x + 1), c), dev(y, z, m4(x + 3), c)
    sib = dev(y, z, x, 1 - c)

    used = [0]
    sent = []

    def take(n=1):
        i = used[0]
        used[0] += n
        assert used[0] <= N_SEM
        return i

    def copy_of(src, dst, to, si, ri):
        return pltpu.make_async_remote_copy(
            src_ref=src, dst_ref=dst, send_sem=ss.at[si], recv_sem=rs.at[ri], device_id=to, device_id_type=MESH
        )

    def send(src, dst, to):
        i = take()
        cp = Sent(copy_of(src, dst, to, i, i))
        sent.append(cp)
        return cp

    def mo(v, n):
        return pl.multiple_of(v, n)

    barrier = pltpu.get_barrier_semaphore()
    peers = [(p, lax.rem(h + i, 8)) for i in range(1, 8)]
    peers += [dev(y, m4(z + i), x, cc) for i in range(1, 4) for cc in range(2)]
    peers += [yp, ym]
    for peer in peers:
        pl.semaphore_signal(barrier, inc=1, device_id=peer, device_id_type=MESH)
    pl.semaphore_wait(barrier, len(peers))

    hs_sem = take(4)
    hr_sem = take(4)
    h0_local = []

    def x_block(req, half_off, rows, xx):
        return xs_.at[pl.ds(mo(req * 256 + half_off, 64), rows), pl.ds(mo(xx * 384, 128), 384)]

    def h0():
        for s in range(2):
            for d in range(2):
                local = (z == 2 * c + s) & (c == d)
                src = hid.at[pl.ds(d * 128, 128), pl.ds(256 * s, 384)]
                dst = x_block(z, d * 128, 128, x)
                cp = copy_of(src, dst, dev(y, 2 * c + s, x, d), hs_sem + 2 * s + d, hr_sem + z)
                h0_local.append((local, cp))

                @pl.when(jnp.logical_not(local))
                def _(cp=cp):
                    cp.start()

                @pl.when(local)
                def _(s=s, d=d):
                    xs_[pl.ds(mo(z * 256 + d * 128, 64), 128), pl.ds(mo(x * 384, 128), 384)] = hid[
                        d * 128 : d * 128 + 128, 256 * s : 256 * s + 384
                    ]

    hc = {}

    def hs(rr):
        zr = m4(z + rr)
        blk = x_block(zr, c * 128, 128, x)
        got = copy_of(blk, blk, sib, hs_sem, hr_sem + zr)
        if rr == 0:

            @pl.when(c != zc)
            def _():
                got.wait_recv()
        else:
            got.wait_recv()
        hc[rr, "p"] = send(blk, blk, xp)
        hc[rr, "m"] = send(blk, blk, xm)
        hc[rr, "s0"] = send(blk, blk, sib)

    def hf(rr):
        zr = m4(z + rr)
        hc[rr, "p"].wait_recv()
        fw = x_block(zr, c * 128, 64, m4(x + 3))
        hc[rr, "fp"] = send(fw, fw, xp)
        blk = x_block(zr, c * 128, 128, m4(x + 3))
        hc[rr, "s1"] = send(blk, blk, sib)
        hc[rr, "m"].wait_recv()
        fw = x_block(zr, c * 128 + 64, 64, m4(x + 1))
        hc[rr, "fm"] = send(fw, fw, xm)
        blk = x_block(zr, c * 128, 128, m4(x + 1))
        hc[rr, "s2"] = send(blk, blk, sib)

    def hg(rr):
        zr = m4(z + rr)
        hc[rr, "fp"].wait_recv()
        hc[rr, "fm"].wait_recv()
        blk = x_block(zr, c * 128, 128, m4(x + 2))
        hc[rr, "s3"] = send(blk, blk, sib)

    def hw(rr):
        for k in ("s0", "s1", "s2", "s3"):
            hc[rr, k].wait_recv()

    def w_block(i, off, rows, n):
        return ws_.at[pl.ds(mo(384 * i + 64 * sz + off, 32), rows), pl.ds(n * CH, CH)]

    wc = {}

    def w_cat():
        lane = lax.broadcasted_iota(jnp.int32, (320, 128), 1)
        er = lax.broadcasted_iota(jnp.int32, (8, 128), 0)
        el = lax.broadcasted_iota(jnp.int32, (8, 128), 1)
        place = jnp.where(el == er + 64 * (1 - c), 1.0, 0.0).astype(BF16)
        steps_w = dot_tn(wdt[...], place).astype(BF16)
        maps_w = wbc[:, pl.ds(mo(x * 128, 128), 128)]
        wcat[:, :128] = jnp.where(lane // 64 == c, maps_w, steps_w)
        wcat[:, 128:640] = wzx[:, 0, :]
        wcat[:, 640:] = wzx[:, 1, :]

    def w_init():
        for i in range(4):
            ws_[pl.ds(mo(384 * i + 320 * (1 - sz), 64), 64), :] = jnp.zeros((64, 3 * CH), BF16)
        ws_[pl.ds(mo(384 * y + 64 * sz, 64), 320), :] = wcat[...]

    def w0(n):
        src = wcat.at[:, pl.ds(n * CH, CH)]
        dst = w_block(y, 0, 320, n)
        wc[n, "p"] = send(src, dst, yp)
        wc[n, "m"] = send(src, dst, ym)

    def wf(n):
        wc[n, "p"].wait_recv()
        fw = w_block(m4(y + 3), 0, 160, n)
        wc[n, "fp"] = send(fw, fw, yp)
        wc[n, "m"].wait_recv()
        fw = w_block(m4(y + 1), 160, 160, n)
        wc[n, "fm"] = send(fw, fw, ym)

    def wg(n):
        wc[n, "fp"].wait_recv()
        wc[n, "fm"].wait_recv()

    pc = {}

    def part(n, rr):
        zr = m4(z + rr)
        return dot_nn(xs_[pl.ds(mo(zr * 256, 256), 256), :], ws_[:, n * CH : (n + 1) * CH])

    def pa(n):
        p2[n] = part(n, 2).astype(BF16)
        pc[n, "2a"] = send(p2.at[n, pl.ds(0, 128)], r2a.at[n], zp)
        pc[n, "2b"] = send(p2.at[n, pl.ds(128, 128)], r2b.at[n], zm)

    def pb(n):
        a = part(n, 1)
        p1[n, 128:] = a[128:].astype(BF16)
        pc[n, "1ah"] = send(p1.at[n, pl.ds(128, 128)], r1a.at[n, pl.ds(128, 128)], zp)
        b = part(n, 3)
        p3[n, :128] = b[:128].astype(BF16)
        pc[n, "1bl"] = send(p3.at[n, pl.ds(0, 128)], r1b.at[n, pl.ds(0, 128)], zm)
        pc[n, "2a"].wait_recv()
        p1[n, :128] = (a[:128] + r2a[n].astype(F32)).astype(BF16)
        pc[n, "1al"] = send(p1.at[n, pl.ds(0, 128)], r1a.at[n, pl.ds(0, 128)], zp)
        pc[n, "2b"].wait_recv()
        p3[n, 128:] = (b[128:] + r2b[n].astype(F32)).astype(BF16)
        pc[n, "1bh"] = send(p3.at[n, pl.ds(128, 128)], r1b.at[n, pl.ds(128, 128)], zm)

    def pd(n):
        own = part(n, 0)
        for k in ("1ah", "1al", "1bl", "1bh"):
            pc[n, k].wait_recv()
        pz[:, n * CH : (n + 1) * CH] = (own + r1a[n].astype(F32) + r1b[n].astype(F32)).astype(BF16)

    mr_sem = take(8)
    map_copies = []

    def m0():
        maps[h] = pz[:, :128]
        for i in range(1, 8):
            si = take()
            cp = copy_of(pz.at[:, pl.ds(0, 128)], maps.at[h], (p, lax.rem(h + i, 8)), si, mr_sem + h)
            cp.start()
            map_copies.append(cp)

    def mw():
        for i in range(1, 8):
            o = lax.rem(h + i, 8)
            copy_of(maps.at[o], maps.at[o], sib, mr_sem, mr_sem + o).wait_recv()

    sc = {}
    axes = (((y, yp, ym), (z, zp, zm)), ((z, zp, zm), (y, yp, ym)))

    def pick(half, a, b):
        r = a * 4 + b if half == 0 else b * 4 + a
        idx = snap[r]
        v = pool[lax.rem(idx, 8), half * 256 : half * 256 + 256, :]
        return jnp.where(idx // 8 == p, v, jnp.zeros_like(v))

    def s0(u):
        (a, ap, am), _ = axes[u]
        for b in range(4):
            f2[u, b] = pick(u, m4(a + 2), b)
            if b == 1:
                sc[u, "2a"] = send(f2.at[u, pl.ds(0, 2)], q2a.at[u], ap)
        sc[u, "2b"] = send(f2.at[u, pl.ds(2, 2)], q2b.at[u], am)
        for b in (2, 3):
            f1[u, b] = pick(u, m4(a + 1), b)
        sc[u, "1ah"] = send(f1.at[u, pl.ds(2, 2)], q1a.at[u, pl.ds(2, 2)], ap)
        for b in (0, 1):
            f3[u, b] = pick(u, m4(a + 3), b)
        sc[u, "1bl"] = send(f3.at[u, pl.ds(0, 2)], q1b.at[u, pl.ds(0, 2)], am)

    def s1(u):
        (a, ap, am), _ = axes[u]
        sc[u, "2a"].wait_recv()
        for b in (0, 1):
            f1[u, b] = pick(u, m4(a + 1), b) + q2a[u, b]
        sc[u, "1al"] = send(f1.at[u, pl.ds(0, 2)], q1a.at[u, pl.ds(0, 2)], ap)
        sc[u, "2b"].wait_recv()
        for b in (2, 3):
            f3[u, b] = pick(u, m4(a + 3), b) + q2b[u, b - 2]
        sc[u, "1bh"] = send(f3.at[u, pl.ds(2, 2)], q1b.at[u, pl.ds(2, 2)], am)

    def s2(u):
        (a, _, _), (b0, bp, bm) = axes[u]
        sc[u, "1ah"].wait_recv()
        sc[u, "1bl"].wait_recv()
        sc[u, "1al"].wait_recv()
        sc[u, "1bh"].wait_recv()
        for b in range(4):
            tt[u, b] = pick(u, a, b) + q1a[u, b] + q1b[u, b]
        far, nxt, prv = m4(b0 + 2), m4(b0 + 1), m4(b0 + 3)
        sc[u, "v2a"] = send(tt.at[u, far, pl.ds(0, 128)], v2a.at[u], bp)
        sc[u, "v2b"] = send(tt.at[u, far, pl.ds(128, 128)], v2b.at[u], bm)
        sc[u, "v1ah"] = send(tt.at[u, nxt, pl.ds(128, 128)], v1a.at[u, pl.ds(128, 128)], bp)
        sc[u, "v1bl"] = send(tt.at[u, prv, pl.ds(0, 128)], v1b.at[u, pl.ds(0, 128)], bm)

    def s3(u):
        _, (b0, bp, bm) = axes[u]
        nxt, prv = m4(b0 + 1), m4(b0 + 3)
        sc[u, "v2a"].wait_recv()
        g1[u] = tt[u, nxt, :128, :] + v2a[u]
        sc[u, "v1al"] = send(g1.at[u], v1a.at[u, pl.ds(0, 128)], bp)
        sc[u, "v2b"].wait_recv()
        g3[u] = tt[u, prv, 128:, :] + v2b[u]
        sc[u, "v1bh"] = send(g3.at[u], v1b.at[u, pl.ds(128, 128)], bm)

    def s4(u):
        _, (b0, _, _) = axes[u]
        for k in ("v1ah", "v1bl", "v1al", "v1bh"):
            sc[u, k].wait_recv()
        start[u * 256 : u * 256 + 256] = tt[u, b0] + v1a[u] + v1b[u]

    oc = {}
    half = pl.ds(mo(c * 128, 128), 128)

    def wo0():
        for k in range(4):
            wo[y, k, :, half] = wout_t[:, 128 * k : 128 * k + 128]
        blk = wo.at[y, :, :, half]
        oc["p"] = send(blk, blk, yp)
        oc["m"] = send(blk, blk, ym)
        oc["s0"] = send(blk, blk, sib)

    def wof():
        oc["p"].wait_recv()
        fw = wo.at[m4(y + 3), :, pl.ds(0, 160), half]
        oc["fp"] = send(fw, fw, yp)
        blk = wo.at[m4(y + 3), :, :, half]
        oc["s1"] = send(blk, blk, sib)
        oc["m"].wait_recv()
        fw = wo.at[m4(y + 1), :, pl.ds(160, 160), half]
        oc["fm"] = send(fw, fw, ym)
        blk = wo.at[m4(y + 1), :, :, half]
        oc["s2"] = send(blk, blk, sib)

    def wog():
        oc["fp"].wait_recv()
        oc["fm"].wait_recv()
        blk = wo.at[m4(y + 2), :, :, half]
        oc["s3"] = send(blk, blk, sib)

    def wow():
        for k in ("s0", "s1", "s2", "s3"):
            oc[k].wait_recv()

    nc = {}
    fa = {}

    def scan_a():
        lane1 = lax.broadcasted_iota(jnp.int32, (1, 128), 1)

        def row_of(ref):
            row = jnp.zeros((1, 128), F32)
            for q in range(8):
                row = jnp.where(lane1 == q, ref[q], row)
            return row

        dtile = pz[:, :128].astype(F32)
        dtile = jnp.where(c == 0, pltpu.roll(dtile, 64, 1), dtile)
        v = dtile + row_of(bias)
        dt = jnp.maximum(v, 0.0) + jnp.log1p(jnp.exp(-jnp.abs(v)))
        rowi = lax.broadcasted_iota(jnp.int32, (256, 256), 0)
        coli = lax.broadcasted_iota(jnp.int32, (256, 256), 1)
        lower = rowi >= coli
        tri = jnp.where(lower, 1.0, 0.0).astype(F32)
        cum = lax.dot_general(
            tri,
            -(row_of(rate) * dt),
            (((1,), (0,)), ((), ())),
            precision=lax.Precision.HIGHEST,
            preferred_element_type=F32,
        )
        ecum = jnp.exp(cum)
        tail = jnp.exp(cum[255:256, :] - cum) * dt
        cum_t = cum.T
        dt_t = dt.T
        first = lax.broadcasted_iota(jnp.int32, (256, 128), 1) < 64
        for i in range(2):
            bc[0, :, 128 * i : 128 * i + 128] = jnp.where(first, maps[2 * i], maps[2 * i + 1])
            bc[1, :, 128 * i : 128 * i + 128] = jnp.where(first, maps[4 + 2 * i], maps[5 + 2 * i])
        scores = dot_nt(bc[1], bc[0])
        for k in range(4):
            xv = pz[:, 640 + 128 * k : 768 + 128 * k]

            def within(q):
                spread = jnp.where(lower, cum[:, q : q + 1] - cum_t[q : q + 1, :], -1e30)
                mix = jnp.exp(spread) * dt_t[q : q + 1, :] * scores
                return dot_nn(mix.astype(BF16), xv)

            cols = slice(128 * k, 128 * k + 128)
            wi[:, cols] = jnp.where(first, within(2 * k), within(2 * k + 1))
            w = jnp.where(first, tail[:, 2 * k : 2 * k + 1], tail[:, 2 * k + 1 : 2 * k + 2])
            wt[:, cols] = (xv.astype(F32) * w).astype(BF16)
        fa["ecum"] = ecum

    def scan_b(k):
        ecum = fa["ecum"]
        lo, hi = 2 * k, 2 * k + 1
        cols = slice(128 * k, 128 * k + 128)
        first = lax.broadcasted_iota(jnp.int32, (256, 128), 1) < 64
        r128 = lax.broadcasted_iota(jnp.int32, (128, 128), 0) // 64
        c128 = lax.broadcasted_iota(jnp.int32, (128, 128), 1) // 64
        same = jnp.where(r128 == c128, 1.0 / 64.0, 0.0).astype(BF16)
        xf = pz[:, 640 + 128 * k : 768 + 128 * k].astype(F32)
        gate = pz[:, 128 + 128 * k : 256 + 128 * k].astype(F32)
        s_in = start[cols, :]
        decay = jnp.where(first, ecum[:, lo : lo + 1], ecum[:, hi : hi + 1])
        scanned = wi[:, cols] + decay * dot_nt(bc[1], s_in)
        skips = jnp.where(first, skip[lo], skip[hi])
        gated = (scanned + skips * xf) * (gate / (1.0 + jnp.exp(-gate)))
        sq = gated * gated
        sq_hi = sq.astype(BF16)
        sq_lo = (sq - sq_hi.astype(F32)).astype(BF16)
        meansq = dot_nn(sq_hi, same) + dot_nn(sq_lo, same)
        normed = (gated * lax.rsqrt(meansq + 1e-05) * gain[:, cols]).astype(BF16)
        upper, under = normed[:128], normed[128:]
        nbuf[z, k, :, half] = jnp.where(c == 0, upper, under)
        ns[k] = jnp.where(c == 0, under, upper)
        dst = nbuf.at[z, k, :, half]
        nc[k, "pd"] = send(ns.at[k], dst, dev(y, m4(z + 1), x, 1 - c))
        nc[k, "md"] = send(ns.at[k], dst, dev(y, m4(z + 3), x, 1 - c))
        nc[k, "pc"] = send(dst, dst, zp)
        nc[k, "mc"] = send(dst, dst, zm)
        nc[k, "s"] = send(ns.at[k], dst, sib)

    def final():
        ecum = fa["ecum"]
        rows_first = lax.broadcasted_iota(jnp.int32, (128, 256), 0) < 64
        for k in range(4):
            cols = slice(128 * k, 128 * k + 128)
            lo, hi = 2 * k, 2 * k + 1
            last = jnp.where(rows_first, ecum[255:256, lo : lo + 1], ecum[255:256, hi : hi + 1])
            fin_out[cols, :] = last * start[cols, :].astype(F32) + dot_tn(wt[:, cols], bc[0])

    def nf(j):
        for k in (2 * j, 2 * j + 1):
            nc[k, "pc"].wait_recv()
            nc[k, "pd"].wait_recv()
        fw = nbuf.at[m4(z + 3), pl.ds(2 * j, 2), pl.ds(0, 64)]
        nc[j, "fp"] = send(fw, fw, zp)
        for k in (2 * j, 2 * j + 1):
            nc[k, "mc"].wait_recv()
            nc[k, "md"].wait_recv()
        fw = nbuf.at[m4(z + 1), pl.ds(2 * j, 2), pl.ds(64, 64)]
        nc[j, "fm"] = send(fw, fw, zm)

    def ng():
        for j in range(2):
            nc[j, "fp"].wait_recv()
            nc[j, "fm"].wait_recv()

    def nw():
        for k in range(4):
            nc[k, "s"].wait_recv()

    xc = {}
    fr_sem = take(4)
    fin_copies = []

    def oa(rr):
        zr = m4(z + rr)

        def prod(ii):
            i = m4(x + ii)
            o = dot_nt(wo[i, 0], nbuf[zr, 0])
            for k in range(1, 4):
                o = o + dot_nt(wo[i, k], nbuf[zr, k])
            return o

        o2[rr] = prod(2).astype(BF16)
        xc[rr, "2a"] = send(o2.at[rr, pl.ds(0, 160)], e2a.at[rr], xp)
        xc[rr, "2b"] = send(o2.at[rr, pl.ds(160, 160)], e2b.at[rr], xm)
        o = prod(1)
        k1[rr] = o[:160]
        o1[rr, 160:] = o[160:].astype(BF16)
        xc[rr, "1ah"] = send(o1.at[rr, pl.ds(160, 160)], e1a.at[rr, pl.ds(160, 160)], xp)
        o = prod(3)
        k3[rr] = o[160:]
        o3[rr, :160] = o[:160].astype(BF16)
        xc[rr, "1bl"] = send(o3.at[rr, pl.ds(0, 160)], e1b.at[rr, pl.ds(0, 160)], xm)
        k0[rr] = prod(0)

    def od(rr):
        xc[rr, "2a"].wait_recv()
        o1[rr, :160] = (k1[rr] + e2a[rr].astype(F32)).astype(BF16)
        xc[rr, "1al"] = send(o1.at[rr, pl.ds(0, 160)], e1a.at[rr, pl.ds(0, 160)], xp)
        xc[rr, "2b"].wait_recv()
        o3[rr, 160:] = (k3[rr] + e2b[rr].astype(F32)).astype(BF16)
        xc[rr, "1bh"] = send(o3.at[rr, pl.ds(160, 160)], e1b.at[rr, pl.ds(160, 160)], xm)

    def oe(rr):
        for k in ("1ah", "1bl", "1al", "1bh"):
            xc[rr, k].wait_recv()
        total = k0[rr] + e1a[rr].astype(F32) + e1b[rr].astype(F32)
        fs[rr] = total.astype(BF16)
        dst = mt.at[pl.ds(mo(sz * 320, 64), 320), pl.ds(mo(c * 128, 128), 128)]
        cp = copy_of(fs.at[rr], dst, dev(y, m4(z + rr), x, zc), take(), fr_sem + 2 * sz + c)
        if rr == 0:

            @pl.when(c != zc)
            def _():
                cp.start()

            @pl.when(c == zc)
            def _():
                mt[pl.ds(mo(sz * 320, 64), 320), pl.ds(mo(c * 128, 128), 128)] = fs[0]
        else:
            cp.start()
        fin_copies.append((rr, cp))

    def of():
        for s in range(2):
            for cc in range(2):
                dst = mt.at[pl.ds(s * 320, 320), pl.ds(cc * 128, 128)]
                got = copy_of(dst, dst, sib, hs_sem, fr_sem + 2 * s + cc)
                local = (z == 2 * c + s) & (c == cc)

                @pl.when(jnp.logical_not(local))
                def _(got=got):
                    got.wait_recv()

        mix_out[...] = mt[...]

    steps = dict(
        h0=h0,
        hf=hf,
        hg=hg,
        hs=hs,
        hw=hw,
        m0=m0,
        mw=mw,
        nf=nf,
        ng=ng,
        nw=nw,
        oa=oa,
        od=od,
        oe=oe,
        of=of,
        pa=pa,
        pb=pb,
        pd=pd,
        s0=s0,
        s1=s1,
        s2=s2,
        s3=s3,
        s4=s4,
        scan_a=scan_a,
        scan_b=scan_b,
        final=final,
        w0=w0,
        w_cat=w_cat,
        w_init=w_init,
        wf=wf,
        wg=wg,
        wo0=wo0,
        wof=wof,
        wog=wog,
        wow=wow,
    )
    for step in ORDER:
        name, *args = step.split()
        steps[name](*map(int, args))

    for cp in sent:
        cp.finish()
    for cp in map_copies:
        cp.wait_send()
    for local, cp in h0_local:

        @pl.when(jnp.logical_not(local))
        def _(cp=cp):
            cp.wait_send()

    for rr, cp in fin_copies:
        if rr == 0:

            @pl.when(c != zc)
            def _(cp=cp):
                cp.wait_send()
        else:
            cp.wait_send()


def finish_body(mixed_t, final, mixed_out, final_out):
    mixed_out[...] = mixed_t[...].T
    final_out[...] = final[...]


def shards(hidden, snap_map, pool_states, w_zx, w_bc, w_dt, dt_bias, decay_rate, skip, norm_gain, w_out):
    vm = pl.BlockSpec(memory_space=VMEM)
    sm = pl.BlockSpec(memory_space=pltpu.SMEM)
    scratch = [
        VMEM((320, 3 * CH), BF16),
        VMEM((1024, 1536), BF16),
        VMEM((1536, 3 * CH), BF16),
        *[VMEM((3, 256, CH), BF16)] * 3,
        *[VMEM((3, 128, CH), BF16)] * 2,
        *[VMEM((3, 256, CH), BF16)] * 2,
        VMEM((256, 3 * CH), BF16),
        VMEM((8, 256, 128), BF16),
        *[VMEM((2, 4, 256, 256), BF16)] * 4,
        *[VMEM((2, 2, 256, 256), BF16)] * 2,
        *[VMEM((2, 4, 256, 256), BF16)] * 2,
        *[VMEM((2, 128, 256), BF16)] * 4,
        *[VMEM((2, 256, 256), BF16)] * 2,
        VMEM((512, 256), BF16),
        VMEM((256, 512), F32),
        VMEM((256, 512), BF16),
        VMEM((2, 256, 256), BF16),
        VMEM((4, 128, 128), BF16),
        VMEM((4, 4, 128, 256), BF16),
        VMEM((4, 4, 320, 256), BF16),
        VMEM((4, 320, 128), F32),
        *[VMEM((4, 160, 128), F32)] * 2,
        *[VMEM((4, 320, 128), BF16)] * 3,
        *[VMEM((4, 160, 128), BF16)] * 2,
        *[VMEM((4, 320, 128), BF16)] * 3,
        VMEM((640, 256), BF16),
        pltpu.SemaphoreType.DMA((N_SEM,)),
        pltpu.SemaphoreType.DMA((N_SEM,)),
    ]
    mixed_t, final = pl.pallas_call(
        body,
        out_shape=(jax.ShapeDtypeStruct((640, 256), BF16), jax.ShapeDtypeStruct((512, 256), F32)),
        in_specs=[sm] * 4 + [vm] * 7,
        out_specs=(vm, vm),
        scratch_shapes=scratch,
        compiler_params=pltpu.CompilerParams(
            collective_id=0, has_side_effects=True, vmem_limit_bytes=56 * 1024 * 1024
        ),
    )(
        snap_map,
        dt_bias,
        decay_rate,
        skip,
        norm_gain.reshape(1, 512),
        hidden.reshape(256, 640),
        w_zx,
        w_bc,
        w_dt.T,
        w_out.T,
        pool_states.reshape(8, 512, 256),
    )
    mixed, final = pl.pallas_call(
        finish_body,
        out_shape=(jax.ShapeDtypeStruct((256, 640), BF16), jax.ShapeDtypeStruct((512, 256), F32)),
        in_specs=[vm, vm],
        out_specs=(vm, vm),
    )(mixed_t, final)
    return mixed.reshape(1, 256, 640), final.reshape(1, 8, 64, 256)


def solution(mesh):
    in_specs = (
        P("pool", None, "head"),
        P(),
        P("pool", "head", None, None),
        P("pool", None, "head"),
        P("pool", None),
        P("pool", "head"),
        P("head"),
        P("head"),
        P("head"),
        P("head"),
        P("head", "pool"),
    )
    out_specs = (P("pool", None, "head"), P("pool", "head", None, None))
    return jax.shard_map(shards, mesh=mesh, in_specs=in_specs, out_specs=out_specs, check_vma=False)
```

```python
import jax
import jax.numpy as jnp
from jax import lax
from jax.experimental import pallas as pl
from jax.experimental.pallas import tpu as pltpu
from jax.sharding import PartitionSpec as P

F32 = jnp.float32
BF16 = jnp.bfloat16
MESH = pl.DeviceIdType.MESH
VMEM = pltpu.VMEM

N_SEM = 176
ROWS = (192, 320)
FIRST_ROW = (0, 192)
CH = 384


ORDER = (
    "h0",
    "w_cat",
    "w0 1",
    "w0 2",
    "s0 1",
    "hs 3",
    "hs 1",
    "wf 1",
    "w0 0",
    "hs 2",
    "hs 0",
    "wf 2",
    "s1 1",
    "hf 3",
    "hf 2",
    "hf 0",
    "hf 1",
    "hg 2",
    "wg 1",
    "wf 0",
    "hw 2",
    "s0 0",
    "hg 3",
    "w_init",
    "pa 1",
    "hg 1",
    "hw 3",
    "wg 2",
    "hw 1",
    "wg 0",
    "hg 0",
    "pa 0",
    "pb1 0",
    "pa 2",
    "s1 0",
    "s2 1",
    "pb2 0",
    "pb1 1",
    "pb1 2",
    "pb2 1",
    "hw 0",
    "wo0",
    "pd 0",
    "m0",
    "s2 0",
    "pb2 2",
    "s3 1",
    "pd 1",
    "mw",
    "scan_a",
    "wof",
    "pd 2",
    "s4 0",
    "s4 1",
    "scan_b 0",
    "scan_b 1",
    "scan_b 2",
    "scan_b 3",
    "wog",
    "nf 0",
    "nw",
    "wow",
    "oa 0",
    "nf 1",
    "oa 1",
    "oa 3",
    "od 1",
    "final",
    "ng",
    "o_far",
    "od 3",
    "od 0",
    "oe 1",
    "oe 3",
    "far_in",
    "oe 0",
    "of",
)


class Sent:
    def __init__(self, copy):
        self.copy = copy
        self.got = False
        copy.start()

    def wait_recv(self):
        assert not self.got
        self.got = True
        self.copy.wait_recv()

    def finish(self):
        if not self.got:
            self.wait_recv()
        self.copy.wait_send()


def dot_nn(a, b):
    return lax.dot_general(a, b, (((1,), (0,)), ((), ())), preferred_element_type=F32)


def dot_nt(a, b):
    return lax.dot_general(a, b, (((1,), (1,)), ((), ())), preferred_element_type=F32)


def dot_tn(a, b):
    return lax.dot_general(a, b, (((0,), (0,)), ((), ())), preferred_element_type=F32)


def body(
    snap,
    bias,
    rate,
    skip,
    gain,
    hid,
    wzx,
    wbc,
    wdt,
    wout_t,
    pool,
    mix_out,
    fin_out,
    wcat,
    xs_,
    ws_,
    p2,
    p1,
    p3,
    r2a,
    r2b,
    r1a,
    r1b,
    ka,
    kb,
    pz,
    maps,
    f2,
    f1,
    f3,
    tt,
    q2a,
    q2b,
    q1a,
    q1b,
    v2,
    v1a,
    v1b,
    g1,
    g3,
    start,
    wi,
    wt,
    bc,
    ns,
    nbuf,
    wo,
    d2,
    h2,
    k0,
    k1,
    k3,
    o2,
    o1,
    o3,
    e2a,
    e2b,
    e1a,
    e1b,
    fs,
    mt,
    ss,
    rs,
):
    p = lax.axis_index("pool")
    h = lax.axis_index("head")
    y = p // 4
    z = lax.rem(p, 4)
    x = h // 2
    c = lax.rem(h, 2)
    sz = lax.rem(z, 2)
    zc = z // 2

    def m4(v):
        return lax.rem(v, 4)

    def dev(yy, zz, xx, cc):
        return (yy * 4 + zz, xx * 2 + cc)

    yp, ym = dev(m4(y + 1), z, x, c), dev(m4(y + 3), z, x, c)
    zp, zm = dev(y, m4(z + 1), x, c), dev(y, m4(z + 3), x, c)
    xp, xm = dev(y, z, m4(x + 1), c), dev(y, z, m4(x + 3), c)
    sib = dev(y, z, x, 1 - c)

    used = [0]
    sent = []

    def take(n=1):
        i = used[0]
        used[0] += n
        assert used[0] <= N_SEM
        return i

    def copy_of(src, dst, to, si, ri):
        return pltpu.make_async_remote_copy(
            src_ref=src, dst_ref=dst, send_sem=ss.at[si], recv_sem=rs.at[ri], device_id=to, device_id_type=MESH
        )

    def send(src, dst, to):
        i = take()
        cp = Sent(copy_of(src, dst, to, i, i))
        sent.append(cp)
        return cp

    def mo(v, n):
        return pl.multiple_of(v, n)

    barrier = pltpu.get_barrier_semaphore()
    peers = [(p, lax.rem(h + i, 8)) for i in range(1, 8)]
    peers += [dev(y, m4(z + i), x, cc) for i in range(1, 4) for cc in range(2)]
    peers += [yp, ym]
    peers += [dev(y, m4(z + 2), m4(x + i), cc) for i in range(1, 4) for cc in range(2)]
    for peer in peers:
        pl.semaphore_signal(barrier, inc=1, device_id=peer, device_id_type=MESH)
    pl.semaphore_wait(barrier, len(peers))

    hs_sem = take(4)
    hr_sem = take(4)
    h0_local = []

    def x_block(req, half_off, rows, xx):
        return xs_.at[pl.ds(mo(req * 256 + half_off, 64), rows), pl.ds(mo(xx * 384, 128), 384)]

    def h0():
        for s in range(2):
            for d in range(2):
                local = (z == 2 * c + s) & (c == d)
                src = hid.at[pl.ds(d * 128, 128), pl.ds(256 * s, 384)]
                dst = x_block(z, d * 128, 128, x)
                cp = copy_of(src, dst, dev(y, 2 * c + s, x, d), hs_sem + 2 * s + d, hr_sem + z)
                h0_local.append((local, cp))

                @pl.when(jnp.logical_not(local))
                def _(cp=cp):
                    cp.start()

                @pl.when(local)
                def _(s=s, d=d):
                    xs_[pl.ds(mo(z * 256 + d * 128, 64), 128), pl.ds(mo(x * 384, 128), 384)] = hid[
                        d * 128 : d * 128 + 128, 256 * s : 256 * s + 384
                    ]

    hc = {}

    def hs(rr):
        zr = m4(z + rr)
        blk = x_block(zr, c * 128, 128, x)
        got = copy_of(blk, blk, sib, hs_sem, hr_sem + zr)
        if rr == 0:

            @pl.when(c != zc)
            def _():
                got.wait_recv()
        else:
            got.wait_recv()
        hc[rr, "p"] = send(blk, blk, xp)
        hc[rr, "m"] = send(blk, blk, xm)
        hc[rr, "s0"] = send(blk, blk, sib)

    def hf(rr):
        zr = m4(z + rr)
        hc[rr, "p"].wait_recv()
        fw = x_block(zr, c * 128, 64, m4(x + 3))
        hc[rr, "fp"] = send(fw, fw, xp)
        blk = x_block(zr, c * 128, 128, m4(x + 3))
        hc[rr, "s1"] = send(blk, blk, sib)
        hc[rr, "m"].wait_recv()
        fw = x_block(zr, c * 128 + 64, 64, m4(x + 1))
        hc[rr, "fm"] = send(fw, fw, xm)
        blk = x_block(zr, c * 128, 128, m4(x + 1))
        hc[rr, "s2"] = send(blk, blk, sib)

    def hg(rr):
        zr = m4(z + rr)
        hc[rr, "fp"].wait_recv()
        hc[rr, "fm"].wait_recv()
        blk = x_block(zr, c * 128, 128, m4(x + 2))
        hc[rr, "s3"] = send(blk, blk, sib)

    def hw(rr):
        for k in ("s0", "s1", "s2", "s3"):
            hc[rr, k].wait_recv()

    def w_block(i, off, rows, n):
        return ws_.at[pl.ds(mo(384 * i + 64 * sz + off, 32), rows), pl.ds(n * CH, CH)]

    wc = {}

    def w_cat():
        lane = lax.broadcasted_iota(jnp.int32, (320, 128), 1)
        er = lax.broadcasted_iota(jnp.int32, (8, 128), 0)
        el = lax.broadcasted_iota(jnp.int32, (8, 128), 1)
        place = jnp.where(el == er + 64 * (1 - c), 1.0, 0.0).astype(BF16)
        steps_w = dot_tn(wdt[...], place).astype(BF16)
        maps_w = wbc[:, pl.ds(mo(x * 128, 128), 128)]
        wcat[:, :128] = jnp.where(lane // 64 == c, maps_w, steps_w)
        wcat[:, 128:640] = wzx[:, 1, :]
        wcat[:, 640:] = wzx[:, 0, :]

    def w_init():
        for i in range(4):
            ws_[pl.ds(mo(384 * i + 320 * (1 - sz), 64), 64), :] = jnp.zeros((64, 3 * CH), BF16)
        ws_[pl.ds(mo(384 * y + 64 * sz, 64), 320), :] = wcat[...]

    def w0(n):
        src = wcat.at[:, pl.ds(n * CH, CH)]
        dst = w_block(y, 0, 320, n)
        wc[n, "p"] = send(src, dst, yp)
        wc[n, "m"] = send(src, dst, ym)

    def wf(n):
        wc[n, "p"].wait_recv()
        fw = w_block(m4(y + 3), 0, 160, n)
        wc[n, "fp"] = send(fw, fw, yp)
        wc[n, "m"].wait_recv()
        fw = w_block(m4(y + 1), 160, 160, n)
        wc[n, "fm"] = send(fw, fw, ym)

    def wg(n):
        wc[n, "fp"].wait_recv()
        wc[n, "fm"].wait_recv()

    pc = {}

    def part(n, rr):
        zr = m4(z + rr)
        return dot_nn(xs_[pl.ds(mo(zr * 256, 256), 256), :], ws_[:, n * CH : (n + 1) * CH])

    def pa(n):
        p2[n] = part(n, 2).astype(BF16)
        pc[n, "2a"] = send(p2.at[n, pl.ds(0, 128)], r2a.at[n], zp)
        pc[n, "2b"] = send(p2.at[n, pl.ds(128, 128)], r2b.at[n], zm)

    def pb1(n):
        a = part(n, 1)
        p1[n, 128:] = a[128:].astype(BF16)
        pc[n, "1ah"] = send(p1.at[n, pl.ds(128, 128)], r1a.at[n, pl.ds(128, 128)], zp)
        ka[n] = a[:128]
        b = part(n, 3)
        p3[n, :128] = b[:128].astype(BF16)
        pc[n, "1bl"] = send(p3.at[n, pl.ds(0, 128)], r1b.at[n, pl.ds(0, 128)], zm)
        kb[n] = b[128:]

    def pb2(n):
        pc[n, "2a"].wait_recv()
        p1[n, :128] = (ka[n] + r2a[n].astype(F32)).astype(BF16)
        pc[n, "1al"] = send(p1.at[n, pl.ds(0, 128)], r1a.at[n, pl.ds(0, 128)], zp)
        pc[n, "2b"].wait_recv()
        p3[n, 128:] = (kb[n] + r2b[n].astype(F32)).astype(BF16)
        pc[n, "1bh"] = send(p3.at[n, pl.ds(128, 128)], r1b.at[n, pl.ds(128, 128)], zm)

    def pd(n):
        own = part(n, 0)
        for k in ("1ah", "1al", "1bl", "1bh"):
            pc[n, k].wait_recv()
        pz[:, n * CH : (n + 1) * CH] = (own + r1a[n].astype(F32) + r1b[n].astype(F32)).astype(BF16)

    mr_sem = take(8)
    map_copies = []

    def m0():
        maps[h] = pz[:, :128]
        for i in range(1, 8):
            si = take()
            cp = copy_of(pz.at[:, pl.ds(0, 128)], maps.at[h], (p, lax.rem(h + i, 8)), si, mr_sem + h)
            cp.start()
            map_copies.append(cp)

    def mw():
        for i in range(1, 8):
            o = lax.rem(h + i, 8)
            copy_of(maps.at[o], maps.at[o], sib, mr_sem, mr_sem + o).wait_recv()

    sc = {}
    axes = (((y, yp, ym), (z, zp, zm)), ((z, zp, zm), (y, yp, ym)))
    far2 = (dev(y, m4(z + 2), x, c), None)

    def pick(u, a, b):
        r = a * 4 + b if u == 0 else b * 4 + a
        idx = snap[r]
        v = pool[lax.rem(idx, 8), FIRST_ROW[u] : FIRST_ROW[u] + ROWS[u], :]
        return jnp.where(idx // 8 == p, v, jnp.zeros_like(v))

    def s0(u):
        (a, ap, am), _ = axes[u]
        for b in range(4):
            f2[u][b] = pick(u, m4(a + 2), b)
            if b == 1:
                sc[u, "2a"] = send(f2[u].at[pl.ds(0, 2)], q2a[u], ap)
        sc[u, "2b"] = send(f2[u].at[pl.ds(2, 2)], q2b[u], am)
        for b in (2, 3):
            f1[u][b] = pick(u, m4(a + 1), b)
        sc[u, "1ah"] = send(f1[u].at[pl.ds(2, 2)], q1a[u].at[pl.ds(2, 2)], ap)
        for b in (0, 1):
            f3[u][b] = pick(u, m4(a + 3), b)
        sc[u, "1bl"] = send(f3[u].at[pl.ds(0, 2)], q1b[u].at[pl.ds(0, 2)], am)

    def s1(u):
        (a, ap, am), _ = axes[u]
        sc[u, "2a"].wait_recv()
        for b in (0, 1):
            f1[u][b] = pick(u, m4(a + 1), b) + q2a[u][b]
        sc[u, "1al"] = send(f1[u].at[pl.ds(0, 2)], q1a[u].at[pl.ds(0, 2)], ap)
        sc[u, "2b"].wait_recv()
        for b in (2, 3):
            f3[u][b] = pick(u, m4(a + 3), b) + q2b[u][b - 2]
        sc[u, "1bh"] = send(f3[u].at[pl.ds(2, 2)], q1b[u].at[pl.ds(2, 2)], am)

    def s2(u):
        (a, _, _), (b0, bp, bm) = axes[u]
        sc[u, "1ah"].wait_recv()
        sc[u, "1bl"].wait_recv()
        sc[u, "1al"].wait_recv()
        sc[u, "1bh"].wait_recv()
        for b in range(4):
            tt[u][b] = pick(u, a, b) + q1a[u][b] + q1b[u][b]
        far, nxt, prv = m4(b0 + 2), m4(b0 + 1), m4(b0 + 3)
        if far2[u] is not None:
            sc[u, "v2"] = send(tt[u].at[far], v2[u], far2[u])
            sc[u, "v1a"] = send(tt[u].at[nxt], v1a[u], bp)
            sc[u, "v1b"] = send(tt[u].at[prv], v1b[u], bm)
            return
        n = ROWS[u] // 2
        sc[u, "v2a"] = send(tt[u].at[far, pl.ds(0, n)], v2[u].at[pl.ds(0, n)], bp)
        sc[u, "v2b"] = send(tt[u].at[far, pl.ds(n, n)], v2[u].at[pl.ds(n, n)], bm)
        sc[u, "v1ah"] = send(tt[u].at[nxt, pl.ds(n, n)], v1a[u].at[pl.ds(n, n)], bp)
        sc[u, "v1bl"] = send(tt[u].at[prv, pl.ds(0, n)], v1b[u].at[pl.ds(0, n)], bm)

    def s3(u):
        _, (b0, bp, bm) = axes[u]
        nxt, prv = m4(b0 + 1), m4(b0 + 3)
        n = ROWS[u] // 2
        sc[u, "v2a"].wait_recv()
        g1[...] = tt[u][nxt, :n, :] + v2[u][:n]
        sc[u, "v1al"] = send(g1, v1a[u].at[pl.ds(0, n)], bp)
        sc[u, "v2b"].wait_recv()
        g3[...] = tt[u][prv, n:, :] + v2[u][n:]
        sc[u, "v1bh"] = send(g3, v1b[u].at[pl.ds(n, n)], bm)

    def s4(u):
        _, (b0, _, _) = axes[u]
        rows = slice(FIRST_ROW[u], FIRST_ROW[u] + ROWS[u])
        if far2[u] is not None:
            for k in ("v2", "v1a", "v1b"):
                sc[u, k].wait_recv()
            start[rows] = tt[u][b0] + v1a[u][...] + v1b[u][...] + v2[u][...]
            return
        for k in ("v1ah", "v1bl", "v1al", "v1bh"):
            sc[u, k].wait_recv()
        start[rows] = tt[u][b0] + v1a[u][...] + v1b[u][...]

    oc = {}
    half = pl.ds(mo(c * 128, 128), 128)

    def wo0():
        for k in range(4):
            wo[y, k, :, half] = wout_t[:, 128 * k : 128 * k + 128]
        blk = wo.at[y, :, :, half]
        oc["p"] = send(blk, blk, yp)
        oc["m"] = send(blk, blk, ym)
        oc["s0"] = send(blk, blk, sib)

    def wof():
        oc["p"].wait_recv()
        fw = wo.at[m4(y + 3), :, pl.ds(0, 160), half]
        oc["fp"] = send(fw, fw, yp)
        blk = wo.at[m4(y + 3), :, :, half]
        oc["s1"] = send(blk, blk, sib)
        oc["m"].wait_recv()
        fw = wo.at[m4(y + 1), :, pl.ds(160, 160), half]
        oc["fm"] = send(fw, fw, ym)
        blk = wo.at[m4(y + 1), :, :, half]
        oc["s2"] = send(blk, blk, sib)

    def wog():
        oc["fp"].wait_recv()
        oc["fm"].wait_recv()
        blk = wo.at[m4(y + 2), :, :, half]
        oc["s3"] = send(blk, blk, sib)

    def wow():
        for k in ("s0", "s1", "s2", "s3"):
            oc[k].wait_recv()

    nc = {}
    fa = {}

    def scan_a():
        lane1 = lax.broadcasted_iota(jnp.int32, (1, 128), 1)

        def row_of(ref):
            row = jnp.zeros((1, 128), F32)
            for q in range(8):
                row = jnp.where(lane1 == q, ref[q], row)
            return row

        dtile = pz[:, :128].astype(F32)
        dtile = jnp.where(c == 0, pltpu.roll(dtile, 64, 1), dtile)
        v = dtile + row_of(bias)
        dt = jnp.maximum(v, 0.0) + jnp.log1p(jnp.exp(-jnp.abs(v)))
        rowi = lax.broadcasted_iota(jnp.int32, (256, 256), 0)
        coli = lax.broadcasted_iota(jnp.int32, (256, 256), 1)
        lower = rowi >= coli
        tri = jnp.where(lower, 1.0, 0.0).astype(F32)
        cum = lax.dot_general(
            tri,
            -(row_of(rate) * dt),
            (((1,), (0,)), ((), ())),
            precision=lax.Precision.HIGHEST,
            preferred_element_type=F32,
        )
        ecum = jnp.exp(cum)
        tail = jnp.exp(cum[255:256, :] - cum) * dt
        cum_t = cum.T
        dt_t = dt.T
        first = lax.broadcasted_iota(jnp.int32, (256, 128), 1) < 64
        for i in range(2):
            bc[0, :, 128 * i : 128 * i + 128] = jnp.where(first, maps[2 * i], maps[2 * i + 1])
            bc[1, :, 128 * i : 128 * i + 128] = jnp.where(first, maps[4 + 2 * i], maps[5 + 2 * i])
        scores = dot_nt(bc[1], bc[0])
        for k in range(4):
            xv = pz[:, 128 + 128 * k : 256 + 128 * k]

            def within(q):
                spread = jnp.where(lower, cum[:, q : q + 1] - cum_t[q : q + 1, :], -1e30)
                mix = jnp.exp(spread) * dt_t[q : q + 1, :] * scores
                return dot_nn(mix.astype(BF16), xv)

            cols = slice(128 * k, 128 * k + 128)
            wi[:, cols] = jnp.where(first, within(2 * k), within(2 * k + 1))
            w = jnp.where(first, tail[:, 2 * k : 2 * k + 1], tail[:, 2 * k + 1 : 2 * k + 2])
            wt[:, cols] = (xv.astype(F32) * w).astype(BF16)
        fa["ecum"] = ecum

    def scan_b(k):
        ecum = fa["ecum"]
        lo, hi = 2 * k, 2 * k + 1
        cols = slice(128 * k, 128 * k + 128)
        first = lax.broadcasted_iota(jnp.int32, (256, 128), 1) < 64
        r128 = lax.broadcasted_iota(jnp.int32, (128, 128), 0) // 64
        c128 = lax.broadcasted_iota(jnp.int32, (128, 128), 1) // 64
        same = jnp.where(r128 == c128, 1.0 / 64.0, 0.0).astype(BF16)
        xf = pz[:, 128 + 128 * k : 256 + 128 * k].astype(F32)
        gate = pz[:, 640 + 128 * k : 768 + 128 * k].astype(F32)
        s_in = start[cols, :]
        decay = jnp.where(first, ecum[:, lo : lo + 1], ecum[:, hi : hi + 1])
        scanned = wi[:, cols] + decay * dot_nt(bc[1], s_in)
        skips = jnp.where(first, skip[lo], skip[hi])
        gated = (scanned + skips * xf) * (gate / (1.0 + jnp.exp(-gate)))
        sq = gated * gated
        sq_hi = sq.astype(BF16)
        sq_lo = (sq - sq_hi.astype(F32)).astype(BF16)
        meansq = dot_nn(sq_hi, same) + dot_nn(sq_lo, same)
        normed = (gated * lax.rsqrt(meansq + 1e-05) * gain[:, cols]).astype(BF16)
        upper, under = normed[:128], normed[128:]
        nbuf[z, k, :, half] = jnp.where(c == 0, upper, under)
        ns[k] = jnp.where(c == 0, under, upper)
        dst = nbuf.at[z, k, :, half]
        nc[k, "pd"] = send(ns.at[k], dst, dev(y, m4(z + 1), x, 1 - c))
        nc[k, "md"] = send(ns.at[k], dst, dev(y, m4(z + 3), x, 1 - c))
        nc[k, "pc"] = send(dst, dst, zp)
        nc[k, "mc"] = send(dst, dst, zm)
        nc[k, "s"] = send(ns.at[k], dst, sib)

    def final():
        ecum = fa["ecum"]
        rows_first = lax.broadcasted_iota(jnp.int32, (128, 256), 0) < 64
        for k in range(4):
            cols = slice(128 * k, 128 * k + 128)
            lo, hi = 2 * k, 2 * k + 1
            last = jnp.where(rows_first, ecum[255:256, lo : lo + 1], ecum[255:256, hi : hi + 1])
            fin_out[cols, :] = last * start[cols, :].astype(F32) + dot_tn(wt[:, cols], bc[0])

    def nf(j):
        for k in (2 * j, 2 * j + 1):
            nc[k, "pc"].wait_recv()
            nc[k, "pd"].wait_recv()
        fw = nbuf.at[m4(z + 3), pl.ds(2 * j, 2), pl.ds(0, 64)]
        nc[j, "fp"] = send(fw, fw, zp)
        for k in (2 * j, 2 * j + 1):
            nc[k, "mc"].wait_recv()
            nc[k, "md"].wait_recv()
        fw = nbuf.at[m4(z + 1), pl.ds(2 * j, 2), pl.ds(64, 64)]
        nc[j, "fm"] = send(fw, fw, zm)

    def ng():
        for j in range(2):
            nc[j, "fp"].wait_recv()
            nc[j, "fm"].wait_recv()

    def nw():
        for k in range(4):
            nc[k, "s"].wait_recv()

    xc = {}
    fr_sem = take(4)
    fin_copies = []

    def out_prod(zr, i):
        o = dot_nt(wo[i, 0], nbuf[zr, 0])
        for k in range(1, 4):
            o = o + dot_nt(wo[i, k], nbuf[zr, k])
        return o

    d_sem = take(8)
    direct = []

    def o_far():
        for ii in (2, 1, 3, 0):
            i = m4(x + ii)
            d2[ii] = out_prod(m4(z + 2), i).astype(BF16)
            cp = copy_of(d2.at[ii], h2.at[2 * ii + c], dev(y, m4(z + 2), i, zc), take(), d_sem + 2 * ii + c)
            cp.start()
            direct.append(cp)

    def far_in():
        @pl.when(c == m4(z + 2) // 2)
        def _():
            for cc in range(2):
                total = jnp.zeros((320, 128), F32)
                for ii in (0, 1, 3, 2):
                    q = 2 * ii + cc
                    copy_of(h2.at[q], h2.at[q], sib, hs_sem, d_sem + q).wait_recv()
                    total = total + h2[q].astype(F32)
                mt[pl.ds(mo(sz * 320, 64), 320), 128 * cc : 128 * cc + 128] = total.astype(BF16)

    def oa(rr):
        zr = m4(z + rr)

        def prod(ii):
            return out_prod(zr, m4(x + ii))

        o2[rr] = prod(2).astype(BF16)
        xc[rr, "2a"] = send(o2.at[rr, pl.ds(0, 160)], e2a.at[rr], xp)
        xc[rr, "2b"] = send(o2.at[rr, pl.ds(160, 160)], e2b.at[rr], xm)
        o = prod(1)
        k1[rr] = o[:160]
        o1[rr, 160:] = o[160:].astype(BF16)
        xc[rr, "1ah"] = send(o1.at[rr, pl.ds(160, 160)], e1a.at[rr, pl.ds(160, 160)], xp)
        o = prod(3)
        k3[rr] = o[160:]
        o3[rr, :160] = o[:160].astype(BF16)
        xc[rr, "1bl"] = send(o3.at[rr, pl.ds(0, 160)], e1b.at[rr, pl.ds(0, 160)], xm)
        k0[rr] = prod(0)

    def od(rr):
        xc[rr, "2a"].wait_recv()
        o1[rr, :160] = (k1[rr] + e2a[rr].astype(F32)).astype(BF16)
        xc[rr, "1al"] = send(o1.at[rr, pl.ds(0, 160)], e1a.at[rr, pl.ds(0, 160)], xp)
        xc[rr, "2b"].wait_recv()
        o3[rr, 160:] = (k3[rr] + e2b[rr].astype(F32)).astype(BF16)
        xc[rr, "1bh"] = send(o3.at[rr, pl.ds(160, 160)], e1b.at[rr, pl.ds(160, 160)], xm)

    def oe(rr):
        for k in ("1ah", "1bl", "1al", "1bh"):
            xc[rr, k].wait_recv()
        total = k0[rr] + e1a[rr].astype(F32) + e1b[rr].astype(F32)
        fs[rr] = total.astype(BF16)
        dst = mt.at[pl.ds(mo(sz * 320, 64), 320), pl.ds(mo(c * 128, 128), 128)]
        cp = copy_of(fs.at[rr], dst, dev(y, m4(z + rr), x, zc), take(), fr_sem + 2 * sz + c)
        if rr == 0:

            @pl.when(c != zc)
            def _():
                cp.start()

            @pl.when(c == zc)
            def _():
                mt[pl.ds(mo(sz * 320, 64), 320), pl.ds(mo(c * 128, 128), 128)] = fs[0]
        else:
            cp.start()
        fin_copies.append((rr, cp))

    def of():
        for s in range(2):
            for cc in range(2):
                dst = mt.at[pl.ds(s * 320, 320), pl.ds(cc * 128, 128)]
                got = copy_of(dst, dst, sib, hs_sem, fr_sem + 2 * s + cc)
                local = ((z == 2 * c + s) & (c == cc)) | (m4(z + 2) == 2 * c + s)

                @pl.when(jnp.logical_not(local))
                def _(got=got):
                    got.wait_recv()

        mix_out[...] = mt[...]

    steps = dict(
        h0=h0,
        hf=hf,
        hg=hg,
        hs=hs,
        hw=hw,
        m0=m0,
        mw=mw,
        nf=nf,
        ng=ng,
        nw=nw,
        oa=oa,
        od=od,
        oe=oe,
        of=of,
        o_far=o_far,
        far_in=far_in,
        pa=pa,
        pb1=pb1,
        pb2=pb2,
        pd=pd,
        s0=s0,
        s1=s1,
        s2=s2,
        s3=s3,
        s4=s4,
        scan_a=scan_a,
        scan_b=scan_b,
        final=final,
        w0=w0,
        w_cat=w_cat,
        w_init=w_init,
        wf=wf,
        wg=wg,
        wo0=wo0,
        wof=wof,
        wog=wog,
        wow=wow,
    )
    for step in ORDER:
        name, *args = step.split()
        steps[name](*map(int, args))

    for cp in sent:
        cp.finish()
    for cp in map_copies + direct:
        cp.wait_send()
    for local, cp in h0_local:

        @pl.when(jnp.logical_not(local))
        def _(cp=cp):
            cp.wait_send()

    for rr, cp in fin_copies:
        if rr == 0:

            @pl.when(c != zc)
            def _(cp=cp):
                cp.wait_send()
        else:
            cp.wait_send()


def finish_body(mixed_t, final, mixed_out, final_out):
    mixed_out[...] = mixed_t[...].T
    final_out[...] = final[...]


def shards(hidden, snap_map, pool_states, w_zx, w_bc, w_dt, dt_bias, decay_rate, skip, norm_gain, w_out):
    vm = pl.BlockSpec(memory_space=VMEM)
    sm = pl.BlockSpec(memory_space=pltpu.SMEM)
    scratch = [
        VMEM((320, 3 * CH), BF16),
        VMEM((1024, 1536), BF16),
        VMEM((1536, 3 * CH), BF16),
        *[VMEM((3, 256, CH), BF16)] * 3,
        *[VMEM((3, 128, CH), BF16)] * 2,
        *[VMEM((3, 256, CH), BF16)] * 2,
        *[VMEM((3, 128, CH), F32)] * 2,
        VMEM((256, 3 * CH), BF16),
        VMEM((8, 256, 128), BF16),
        *[tuple(VMEM((4, n, 256), BF16) for n in ROWS)] * 4,
        *[tuple(VMEM((2, n, 256), BF16) for n in ROWS)] * 2,
        *[tuple(VMEM((4, n, 256), BF16) for n in ROWS)] * 2,
        *[tuple(VMEM((n, 256), BF16) for n in ROWS)] * 3,
        *[VMEM((ROWS[1] // 2, 256), BF16)] * 2,
        VMEM((512, 256), BF16),
        VMEM((256, 512), F32),
        VMEM((256, 512), BF16),
        VMEM((2, 256, 256), BF16),
        VMEM((4, 128, 128), BF16),
        VMEM((4, 4, 128, 256), BF16),
        VMEM((4, 4, 320, 256), BF16),
        VMEM((4, 320, 128), BF16),
        VMEM((8, 320, 128), BF16),
        VMEM((4, 320, 128), F32),
        *[VMEM((4, 160, 128), F32)] * 2,
        *[VMEM((4, 320, 128), BF16)] * 3,
        *[VMEM((4, 160, 128), BF16)] * 2,
        *[VMEM((4, 320, 128), BF16)] * 3,
        VMEM((640, 256), BF16),
        pltpu.SemaphoreType.DMA((N_SEM,)),
        pltpu.SemaphoreType.DMA((N_SEM,)),
    ]
    mixed_t, final = pl.pallas_call(
        body,
        out_shape=(jax.ShapeDtypeStruct((640, 256), BF16), jax.ShapeDtypeStruct((512, 256), F32)),
        in_specs=[sm] * 4 + [vm] * 7,
        out_specs=(vm, vm),
        scratch_shapes=scratch,
        compiler_params=pltpu.CompilerParams(
            collective_id=0, has_side_effects=True, vmem_limit_bytes=56 * 1024 * 1024
        ),
    )(
        snap_map,
        dt_bias,
        decay_rate,
        skip,
        norm_gain.reshape(1, 512),
        hidden.reshape(256, 640),
        w_zx,
        w_bc,
        w_dt.T,
        w_out.T,
        pool_states.reshape(8, 512, 256),
    )
    mixed, final = pl.pallas_call(
        finish_body,
        out_shape=(jax.ShapeDtypeStruct((256, 640), BF16), jax.ShapeDtypeStruct((512, 256), F32)),
        in_specs=[vm, vm],
        out_specs=(vm, vm),
    )(mixed_t, final)
    return mixed.reshape(1, 256, 640), final.reshape(1, 8, 64, 256)


def solution(mesh):
    in_specs = (
        P("pool", None, "head"),
        P(),
        P("pool", "head", None, None),
        P("pool", None, "head"),
        P("pool", None),
        P("pool", "head"),
        P("head"),
        P("head"),
        P("head"),
        P("head"),
        P("head", "pool"),
    )
    out_specs = (P("pool", None, "head"), P("pool", "head", None, None))
    return jax.shard_map(shards, mesh=mesh, in_specs=in_specs, out_specs=out_specs, check_vma=False)
```

```python
import jax
import jax.numpy as jnp
from jax import lax
from jax.experimental import pallas as pl
from jax.experimental.pallas import tpu as pltpu
from jax.sharding import PartitionSpec as P

F32 = jnp.float32
BF16 = jnp.bfloat16
MESH = pl.DeviceIdType.MESH
VMEM = pltpu.VMEM

N_SEM = 176
ROWS = (192, 320)
FIRST_ROW = (0, 192)
CH = 384


ORDER = (
    "h0",
    "w0 1",
    "w0 2",
    "s0 1",
    "hs 3",
    "hs 1",
    "wf 1",
    "w0 0",
    "hs 2",
    "hs 0",
    "wf 2",
    "s1 1",
    "hf 3",
    "hf 2",
    "hf 0",
    "hf 1",
    "hg 2",
    "wg 1",
    "wf 0",
    "hw 2",
    "s0 0",
    "hg 3",
    "pa 1",
    "hg 1",
    "hw 3",
    "wg 2",
    "hw 1",
    "wg 0",
    "hg 0",
    "pa 0",
    "pb1 0",
    "pa 2",
    "s1 0",
    "s2 1",
    "pb2 0",
    "pb1 1",
    "pb1 2",
    "pb2 1",
    "hw 0",
    "wo0",
    "pd 0",
    "m0",
    "s2 0",
    "pb2 2",
    "s3 1",
    "pd 1",
    "mw",
    "scan_a",
    "wof",
    "pd 2",
    "s4 0",
    "s4 1",
    "scan_b 0",
    "scan_b 1",
    "scan_b 2",
    "scan_b 3",
    "wog",
    "nf 0",
    "nw",
    "wow",
    "oa 0",
    "nf 1",
    "oa 1",
    "oa 3",
    "od 1",
    "final",
    "ng",
    "o_far",
    "od 3",
    "od 0",
    "oe 1",
    "oe 3",
    "far_in",
    "oe 0",
    "of",
)


class Sent:
    def __init__(self, copy):
        self.copy = copy
        self.got = False
        copy.start()

    def wait_recv(self):
        assert not self.got
        self.got = True
        self.copy.wait_recv()

    def finish(self):
        if not self.got:
            self.wait_recv()
        self.copy.wait_send()


def dot_nn(a, b):
    return lax.dot_general(a, b, (((1,), (0,)), ((), ())), preferred_element_type=F32)


def dot_nt(a, b):
    return lax.dot_general(a, b, (((1,), (1,)), ((), ())), preferred_element_type=F32)


def dot_tn(a, b):
    return lax.dot_general(a, b, (((0,), (0,)), ((), ())), preferred_element_type=F32)


def body(
    snap,
    bias,
    rate,
    skip,
    gain,
    wdt,
    hid_in,
    wzx_in,
    wbc_in,
    wout_in,
    pool_in,
    mix_out,
    fin_out,
    hid,
    wzx,
    wbc,
    wout_t,
    pool,
    wcat,
    xs_,
    ws_,
    p2,
    p1,
    p3,
    r2a,
    r2b,
    r1a,
    r1b,
    ka,
    kb,
    pz,
    maps,
    f2,
    f1,
    f3,
    tt,
    q2a,
    q2b,
    q1a,
    q1b,
    v2,
    v1a,
    v1b,
    g1,
    g3,
    start,
    wi,
    wt,
    bc,
    ns,
    nbuf,
    wo,
    d2,
    h2,
    k0,
    k1,
    k3,
    o2,
    o1,
    o3,
    e2a,
    e2b,
    e1a,
    e1b,
    fs,
    mt,
    ss,
    rs,
    ls,
):
    p = lax.axis_index("pool")
    h = lax.axis_index("head")
    y = p // 4
    z = lax.rem(p, 4)
    x = h // 2
    c = lax.rem(h, 2)
    sz = lax.rem(z, 2)
    zc = z // 2

    def m4(v):
        return lax.rem(v, 4)

    def dev(yy, zz, xx, cc):
        return (yy * 4 + zz, xx * 2 + cc)

    yp, ym = dev(m4(y + 1), z, x, c), dev(m4(y + 3), z, x, c)
    zp, zm = dev(y, m4(z + 1), x, c), dev(y, m4(z + 3), x, c)
    xp, xm = dev(y, z, m4(x + 1), c), dev(y, z, m4(x + 3), c)
    sib = dev(y, z, x, 1 - c)

    used = [0]
    sent = []

    def take(n=1):
        i = used[0]
        used[0] += n
        assert used[0] <= N_SEM
        return i

    def copy_of(src, dst, to, si, ri):
        return pltpu.make_async_remote_copy(
            src_ref=src, dst_ref=dst, send_sem=ss.at[si], recv_sem=rs.at[ri], device_id=to, device_id_type=MESH
        )

    def send(src, dst, to):
        i = take()
        cp = Sent(copy_of(src, dst, to, i, i))
        sent.append(cp)
        return cp

    def mo(v, n):
        return pl.multiple_of(v, n)

    barrier = pltpu.get_barrier_semaphore()
    peers = [(p, lax.rem(h + i, 8)) for i in range(1, 8)]
    peers += [dev(y, m4(z + i), x, cc) for i in range(1, 4) for cc in range(2)]
    peers += [yp, ym]
    for peer in peers:
        pl.semaphore_signal(barrier, inc=1, device_id=peer, device_id_type=MESH)

    loads = [
        pltpu.make_async_copy(src, dst, ls.at[i])
        for i, (src, dst) in enumerate(
            ((wzx_in, wzx), (wbc_in, wbc), (pool_in, pool), (hid_in, hid), (wout_in, wout_t))
        )
    ]
    for load in loads:
        load.start()

    hs_sem = take(4)
    hr_sem = take(4)
    h0_local = []

    def x_block(req, half_off, rows, xx):
        return xs_.at[pl.ds(mo(req * 256 + half_off, 64), rows), pl.ds(mo(xx * 384, 128), 384)]

    def h0():
        for s in range(2):
            for d in range(2):
                local = (z == 2 * c + s) & (c == d)
                src = hid.at[pl.ds(d * 128, 128), pl.ds(256 * s, 384)]
                dst = x_block(z, d * 128, 128, x)
                cp = copy_of(src, dst, dev(y, 2 * c + s, x, d), hs_sem + 2 * s + d, hr_sem + z)
                h0_local.append((local, cp))

                @pl.when(jnp.logical_not(local))
                def _(cp=cp):
                    cp.start()

                @pl.when(local)
                def _(s=s, d=d):
                    xs_[pl.ds(mo(z * 256 + d * 128, 64), 128), pl.ds(mo(x * 384, 128), 384)] = hid[
                        d * 128 : d * 128 + 128, 256 * s : 256 * s + 384
                    ]

    hc = {}

    def hs(rr):
        zr = m4(z + rr)
        blk = x_block(zr, c * 128, 128, x)
        got = copy_of(blk, blk, sib, hs_sem, hr_sem + zr)
        if rr == 0:

            @pl.when(c != zc)
            def _():
                got.wait_recv()
        else:
            got.wait_recv()
        hc[rr, "p"] = send(blk, blk, xp)
        hc[rr, "m"] = send(blk, blk, xm)
        hc[rr, "s0"] = send(blk, blk, sib)

    def hf(rr):
        zr = m4(z + rr)
        hc[rr, "p"].wait_recv()
        fw = x_block(zr, c * 128, 64, m4(x + 3))
        hc[rr, "fp"] = send(fw, fw, xp)
        blk = x_block(zr, c * 128, 128, m4(x + 3))
        hc[rr, "s1"] = send(blk, blk, sib)
        hc[rr, "m"].wait_recv()
        fw = x_block(zr, c * 128 + 64, 64, m4(x + 1))
        hc[rr, "fm"] = send(fw, fw, xm)
        blk = x_block(zr, c * 128, 128, m4(x + 1))
        hc[rr, "s2"] = send(blk, blk, sib)

    def hg(rr):
        zr = m4(z + rr)
        hc[rr, "fp"].wait_recv()
        hc[rr, "fm"].wait_recv()
        blk = x_block(zr, c * 128, 128, m4(x + 2))
        hc[rr, "s3"] = send(blk, blk, sib)

    def hw(rr):
        for k in ("s0", "s1", "s2", "s3"):
            hc[rr, k].wait_recv()

    def w_block(i, off, rows, n):
        return ws_.at[pl.ds(mo(384 * i + 64 * sz + off, 32), rows), pl.ds(n * CH, CH)]

    wc = {}

    def w_cat():
        lane = lax.broadcasted_iota(jnp.int32, (320, 128), 1)
        er = lax.broadcasted_iota(jnp.int32, (8, 128), 0)
        el = lax.broadcasted_iota(jnp.int32, (8, 128), 1)
        place = jnp.where(el == er + 64 * (1 - c), 1.0, 0.0).astype(BF16)
        steps_w = dot_tn(wdt[...], place).astype(BF16)
        maps_w = wbc[:, pl.ds(mo(x * 128, 128), 128)]
        wcat[:, :128] = jnp.where(lane // 64 == c, maps_w, steps_w)
        wcat[:, 128:640] = wzx[:, 1, :]
        wcat[:, 640:] = wzx[:, 0, :]

    def w_init():
        for i in range(4):
            ws_[pl.ds(mo(384 * i + 320 * (1 - sz), 64), 64), :] = jnp.zeros((64, 3 * CH), BF16)
        ws_[pl.ds(mo(384 * y + 64 * sz, 64), 320), :] = wcat[...]

    def w0(n):
        src = wcat.at[:, pl.ds(n * CH, CH)]
        dst = w_block(y, 0, 320, n)
        wc[n, "p"] = send(src, dst, yp)
        wc[n, "m"] = send(src, dst, ym)

    def wf(n):
        wc[n, "p"].wait_recv()
        fw = w_block(m4(y + 3), 0, 160, n)
        wc[n, "fp"] = send(fw, fw, yp)
        wc[n, "m"].wait_recv()
        fw = w_block(m4(y + 1), 160, 160, n)
        wc[n, "fm"] = send(fw, fw, ym)

    def wg(n):
        wc[n, "fp"].wait_recv()
        wc[n, "fm"].wait_recv()

    pc = {}

    def part(n, rr):
        zr = m4(z + rr)
        return dot_nn(xs_[pl.ds(mo(zr * 256, 256), 256), :], ws_[:, n * CH : (n + 1) * CH])

    def pa(n):
        p2[n] = part(n, 2).astype(BF16)
        pc[n, "2a"] = send(p2.at[n, pl.ds(0, 128)], r2a.at[n], zp)
        pc[n, "2b"] = send(p2.at[n, pl.ds(128, 128)], r2b.at[n], zm)

    def pb1(n):
        a = part(n, 1)
        p1[n, 128:] = a[128:].astype(BF16)
        pc[n, "1ah"] = send(p1.at[n, pl.ds(128, 128)], r1a.at[n, pl.ds(128, 128)], zp)
        ka[n] = a[:128]
        b = part(n, 3)
        p3[n, :128] = b[:128].astype(BF16)
        pc[n, "1bl"] = send(p3.at[n, pl.ds(0, 128)], r1b.at[n, pl.ds(0, 128)], zm)
        kb[n] = b[128:]

    def pb2(n):
        pc[n, "2a"].wait_recv()
        p1[n, :128] = (ka[n] + r2a[n].astype(F32)).astype(BF16)
        pc[n, "1al"] = send(p1.at[n, pl.ds(0, 128)], r1a.at[n, pl.ds(0, 128)], zp)
        pc[n, "2b"].wait_recv()
        p3[n, 128:] = (kb[n] + r2b[n].astype(F32)).astype(BF16)
        pc[n, "1bh"] = send(p3.at[n, pl.ds(128, 128)], r1b.at[n, pl.ds(128, 128)], zm)

    def pd(n):
        own = part(n, 0)
        for k in ("1ah", "1al", "1bl", "1bh"):
            pc[n, k].wait_recv()
        pz[:, n * CH : (n + 1) * CH] = (own + r1a[n].astype(F32) + r1b[n].astype(F32)).astype(BF16)

    mr_sem = take(8)
    map_copies = []

    def m0():
        maps[h] = pz[:, :128]
        for i in range(1, 8):
            si = take()
            cp = copy_of(pz.at[:, pl.ds(0, 128)], maps.at[h], (p, lax.rem(h + i, 8)), si, mr_sem + h)
            cp.start()
            map_copies.append(cp)

    def mw():
        for i in range(1, 8):
            o = lax.rem(h + i, 8)
            copy_of(maps.at[o], maps.at[o], sib, mr_sem, mr_sem + o).wait_recv()

    sc = {}
    axes = (((y, yp, ym), (z, zp, zm)), ((z, zp, zm), (y, yp, ym)))
    far2 = (dev(y, m4(z + 2), x, c), None)

    def pick(u, a, b):
        r = a * 4 + b if u == 0 else b * 4 + a
        idx = snap[r]
        v = pool[lax.rem(idx, 8), FIRST_ROW[u] : FIRST_ROW[u] + ROWS[u], :]
        return jnp.where(idx // 8 == p, v, jnp.zeros_like(v))

    def s_pick(u):
        a = axes[u][0][0]
        for b in range(4):
            f2[u][b] = pick(u, m4(a + 2), b)
        for b in (2, 3):
            f1[u][b] = pick(u, m4(a + 1), b)
        for b in (0, 1):
            f3[u][b] = pick(u, m4(a + 3), b)

    def s0(u):
        (a, ap, am), _ = axes[u]
        sc[u, "2a"] = send(f2[u].at[pl.ds(0, 2)], q2a[u], ap)
        sc[u, "2b"] = send(f2[u].at[pl.ds(2, 2)], q2b[u], am)
        sc[u, "1ah"] = send(f1[u].at[pl.ds(2, 2)], q1a[u].at[pl.ds(2, 2)], ap)
        sc[u, "1bl"] = send(f3[u].at[pl.ds(0, 2)], q1b[u].at[pl.ds(0, 2)], am)

    def s1(u):
        (a, ap, am), _ = axes[u]
        sc[u, "2a"].wait_recv()
        for b in (0, 1):
            f1[u][b] = pick(u, m4(a + 1), b) + q2a[u][b]
        sc[u, "1al"] = send(f1[u].at[pl.ds(0, 2)], q1a[u].at[pl.ds(0, 2)], ap)
        sc[u, "2b"].wait_recv()
        for b in (2, 3):
            f3[u][b] = pick(u, m4(a + 3), b) + q2b[u][b - 2]
        sc[u, "1bh"] = send(f3[u].at[pl.ds(2, 2)], q1b[u].at[pl.ds(2, 2)], am)

    def s2(u):
        (a, _, _), (b0, bp, bm) = axes[u]
        sc[u, "1ah"].wait_recv()
        sc[u, "1bl"].wait_recv()
        sc[u, "1al"].wait_recv()
        sc[u, "1bh"].wait_recv()
        for b in range(4):
            tt[u][b] = pick(u, a, b) + q1a[u][b] + q1b[u][b]
        far, nxt, prv = m4(b0 + 2), m4(b0 + 1), m4(b0 + 3)
        if far2[u] is not None:
            sc[u, "v2"] = send(tt[u].at[far], v2[u], far2[u])
            sc[u, "v1a"] = send(tt[u].at[nxt], v1a[u], bp)
            sc[u, "v1b"] = send(tt[u].at[prv], v1b[u], bm)
            return
        n = ROWS[u] // 2
        sc[u, "v2a"] = send(tt[u].at[far, pl.ds(0, n)], v2[u].at[pl.ds(0, n)], bp)
        sc[u, "v2b"] = send(tt[u].at[far, pl.ds(n, n)], v2[u].at[pl.ds(n, n)], bm)
        sc[u, "v1ah"] = send(tt[u].at[nxt, pl.ds(n, n)], v1a[u].at[pl.ds(n, n)], bp)
        sc[u, "v1bl"] = send(tt[u].at[prv, pl.ds(0, n)], v1b[u].at[pl.ds(0, n)], bm)

    def s3(u):
        _, (b0, bp, bm) = axes[u]
        nxt, prv = m4(b0 + 1), m4(b0 + 3)
        n = ROWS[u] // 2
        sc[u, "v2a"].wait_recv()
        g1[...] = tt[u][nxt, :n, :] + v2[u][:n]
        sc[u, "v1al"] = send(g1, v1a[u].at[pl.ds(0, n)], bp)
        sc[u, "v2b"].wait_recv()
        g3[...] = tt[u][prv, n:, :] + v2[u][n:]
        sc[u, "v1bh"] = send(g3, v1b[u].at[pl.ds(n, n)], bm)

    def s4(u):
        _, (b0, _, _) = axes[u]
        rows = slice(FIRST_ROW[u], FIRST_ROW[u] + ROWS[u])
        if far2[u] is not None:
            for k in ("v2", "v1a", "v1b"):
                sc[u, k].wait_recv()
            start[rows] = tt[u][b0] + v1a[u][...] + v1b[u][...] + v2[u][...]
            return
        for k in ("v1ah", "v1bl", "v1al", "v1bh"):
            sc[u, k].wait_recv()
        start[rows] = tt[u][b0] + v1a[u][...] + v1b[u][...]

    oc = {}
    half = pl.ds(mo(c * 128, 128), 128)

    def wo0():
        for k in range(4):
            wo[y, k, :, half] = wout_t[:, 128 * k : 128 * k + 128]
        blk = wo.at[y, :, :, half]
        oc["p"] = send(blk, blk, yp)
        oc["m"] = send(blk, blk, ym)
        oc["s0"] = send(blk, blk, sib)

    def wof():
        oc["p"].wait_recv()
        fw = wo.at[m4(y + 3), :, pl.ds(0, 160), half]
        oc["fp"] = send(fw, fw, yp)
        blk = wo.at[m4(y + 3), :, :, half]
        oc["s1"] = send(blk, blk, sib)
        oc["m"].wait_recv()
        fw = wo.at[m4(y + 1), :, pl.ds(160, 160), half]
        oc["fm"] = send(fw, fw, ym)
        blk = wo.at[m4(y + 1), :, :, half]
        oc["s2"] = send(blk, blk, sib)

    def wog():
        oc["fp"].wait_recv()
        oc["fm"].wait_recv()
        blk = wo.at[m4(y + 2), :, :, half]
        oc["s3"] = send(blk, blk, sib)

    def wow():
        for k in ("s0", "s1", "s2", "s3"):
            oc[k].wait_recv()

    nc = {}
    fa = {}

    def scan_a():
        lane1 = lax.broadcasted_iota(jnp.int32, (1, 128), 1)

        def row_of(ref):
            row = jnp.zeros((1, 128), F32)
            for q in range(8):
                row = jnp.where(lane1 == q, ref[q], row)
            return row

        dtile = pz[:, :128].astype(F32)
        dtile = jnp.where(c == 0, pltpu.roll(dtile, 64, 1), dtile)
        v = dtile + row_of(bias)
        dt = jnp.maximum(v, 0.0) + jnp.log1p(jnp.exp(-jnp.abs(v)))
        rowi = lax.broadcasted_iota(jnp.int32, (256, 256), 0)
        coli = lax.broadcasted_iota(jnp.int32, (256, 256), 1)
        lower = rowi >= coli
        tri = jnp.where(lower, 1.0, 0.0).astype(F32)
        cum = lax.dot_general(
            tri,
            -(row_of(rate) * dt),
            (((1,), (0,)), ((), ())),
            precision=lax.Precision.HIGHEST,
            preferred_element_type=F32,
        )
        ecum = jnp.exp(cum)
        tail = jnp.exp(cum[255:256, :] - cum) * dt
        cum_t = cum.T
        dt_t = dt.T
        first = lax.broadcasted_iota(jnp.int32, (256, 128), 1) < 64
        for i in range(2):
            bc[0, :, 128 * i : 128 * i + 128] = jnp.where(first, maps[2 * i], maps[2 * i + 1])
            bc[1, :, 128 * i : 128 * i + 128] = jnp.where(first, maps[4 + 2 * i], maps[5 + 2 * i])
        scores = dot_nt(bc[1], bc[0])
        for k in range(4):
            xv = pz[:, 128 + 128 * k : 256 + 128 * k]

            def within(q):
                spread = jnp.where(lower, cum[:, q : q + 1] - cum_t[q : q + 1, :], -1e30)
                mix = jnp.exp(spread) * dt_t[q : q + 1, :] * scores
                return dot_nn(mix.astype(BF16), xv)

            cols = slice(128 * k, 128 * k + 128)
            wi[:, cols] = jnp.where(first, within(2 * k), within(2 * k + 1))
            w = jnp.where(first, tail[:, 2 * k : 2 * k + 1], tail[:, 2 * k + 1 : 2 * k + 2])
            wt[:, cols] = (xv.astype(F32) * w).astype(BF16)
        fa["ecum"] = ecum

    def scan_b(k):
        ecum = fa["ecum"]
        lo, hi = 2 * k, 2 * k + 1
        cols = slice(128 * k, 128 * k + 128)
        first = lax.broadcasted_iota(jnp.int32, (256, 128), 1) < 64
        r128 = lax.broadcasted_iota(jnp.int32, (128, 128), 0) // 64
        c128 = lax.broadcasted_iota(jnp.int32, (128, 128), 1) // 64
        same = jnp.where(r128 == c128, 1.0 / 64.0, 0.0).astype(BF16)
        xf = pz[:, 128 + 128 * k : 256 + 128 * k].astype(F32)
        gate = pz[:, 640 + 128 * k : 768 + 128 * k].astype(F32)
        s_in = start[cols, :]
        decay = jnp.where(first, ecum[:, lo : lo + 1], ecum[:, hi : hi + 1])
        scanned = wi[:, cols] + decay * dot_nt(bc[1], s_in)
        skips = jnp.where(first, skip[lo], skip[hi])
        gated = (scanned + skips * xf) * (gate / (1.0 + jnp.exp(-gate)))
        sq = gated * gated
        sq_hi = sq.astype(BF16)
        sq_lo = (sq - sq_hi.astype(F32)).astype(BF16)
        meansq = dot_nn(sq_hi, same) + dot_nn(sq_lo, same)
        normed = (gated * lax.rsqrt(meansq + 1e-05) * gain[:, cols]).astype(BF16)
        upper, under = normed[:128], normed[128:]
        nbuf[z, k, :, half] = jnp.where(c == 0, upper, under)
        ns[k] = jnp.where(c == 0, under, upper)
        dst = nbuf.at[z, k, :, half]
        nc[k, "pd"] = send(ns.at[k], dst, dev(y, m4(z + 1), x, 1 - c))
        nc[k, "md"] = send(ns.at[k], dst, dev(y, m4(z + 3), x, 1 - c))
        nc[k, "pc"] = send(dst, dst, zp)
        nc[k, "mc"] = send(dst, dst, zm)
        nc[k, "s"] = send(ns.at[k], dst, sib)

    def final():
        ecum = fa["ecum"]
        rows_first = lax.broadcasted_iota(jnp.int32, (128, 256), 0) < 64
        for k in range(4):
            cols = slice(128 * k, 128 * k + 128)
            lo, hi = 2 * k, 2 * k + 1
            last = jnp.where(rows_first, ecum[255:256, lo : lo + 1], ecum[255:256, hi : hi + 1])
            fin_out[cols, :] = last * start[cols, :].astype(F32) + dot_tn(wt[:, cols], bc[0])

    def nf(j):
        for k in (2 * j, 2 * j + 1):
            nc[k, "pc"].wait_recv()
            nc[k, "pd"].wait_recv()
        fw = nbuf.at[m4(z + 3), pl.ds(2 * j, 2), pl.ds(0, 64)]
        nc[j, "fp"] = send(fw, fw, zp)
        for k in (2 * j, 2 * j + 1):
            nc[k, "mc"].wait_recv()
            nc[k, "md"].wait_recv()
        fw = nbuf.at[m4(z + 1), pl.ds(2 * j, 2), pl.ds(64, 64)]
        nc[j, "fm"] = send(fw, fw, zm)

    def ng():
        for j in range(2):
            nc[j, "fp"].wait_recv()
            nc[j, "fm"].wait_recv()

    def nw():
        for k in range(4):
            nc[k, "s"].wait_recv()

    xc = {}
    fr_sem = take(4)
    fin_copies = []

    def out_prod(zr, i):
        o = dot_nt(wo[i, 0], nbuf[zr, 0])
        for k in range(1, 4):
            o = o + dot_nt(wo[i, k], nbuf[zr, k])
        return o

    d_sem = take(8)
    direct = []

    def o_far():
        for ii in (2, 1, 3, 0):
            i = m4(x + ii)
            d2[ii] = out_prod(m4(z + 2), i).astype(BF16)
            cp = copy_of(d2.at[ii], h2.at[2 * ii + c], dev(y, m4(z + 2), i, zc), take(), d_sem + 2 * ii + c)
            cp.start()
            direct.append(cp)

    def far_in():
        @pl.when(c == m4(z + 2) // 2)
        def _():
            for cc in range(2):
                total = jnp.zeros((320, 128), F32)
                for ii in (0, 1, 3, 2):
                    q = 2 * ii + cc
                    copy_of(h2.at[q], h2.at[q], sib, hs_sem, d_sem + q).wait_recv()
                    total = total + h2[q].astype(F32)
                mt[pl.ds(mo(sz * 320, 64), 320), 128 * cc : 128 * cc + 128] = total.astype(BF16)

    def oa(rr):
        zr = m4(z + rr)

        def prod(ii):
            return out_prod(zr, m4(x + ii))

        o2[rr] = prod(2).astype(BF16)
        xc[rr, "2a"] = send(o2.at[rr, pl.ds(0, 160)], e2a.at[rr], xp)
        xc[rr, "2b"] = send(o2.at[rr, pl.ds(160, 160)], e2b.at[rr], xm)
        o = prod(1)
        k1[rr] = o[:160]
        o1[rr, 160:] = o[160:].astype(BF16)
        xc[rr, "1ah"] = send(o1.at[rr, pl.ds(160, 160)], e1a.at[rr, pl.ds(160, 160)], xp)
        o = prod(3)
        k3[rr] = o[160:]
        o3[rr, :160] = o[:160].astype(BF16)
        xc[rr, "1bl"] = send(o3.at[rr, pl.ds(0, 160)], e1b.at[rr, pl.ds(0, 160)], xm)
        k0[rr] = prod(0)

    def od(rr):
        xc[rr, "2a"].wait_recv()
        o1[rr, :160] = (k1[rr] + e2a[rr].astype(F32)).astype(BF16)
        xc[rr, "1al"] = send(o1.at[rr, pl.ds(0, 160)], e1a.at[rr, pl.ds(0, 160)], xp)
        xc[rr, "2b"].wait_recv()
        o3[rr, 160:] = (k3[rr] + e2b[rr].astype(F32)).astype(BF16)
        xc[rr, "1bh"] = send(o3.at[rr, pl.ds(160, 160)], e1b.at[rr, pl.ds(160, 160)], xm)

    def oe(rr):
        for k in ("1ah", "1bl", "1al", "1bh"):
            xc[rr, k].wait_recv()
        total = k0[rr] + e1a[rr].astype(F32) + e1b[rr].astype(F32)
        fs[rr] = total.astype(BF16)
        dst = mt.at[pl.ds(mo(sz * 320, 64), 320), pl.ds(mo(c * 128, 128), 128)]
        cp = copy_of(fs.at[rr], dst, dev(y, m4(z + rr), x, zc), take(), fr_sem + 2 * sz + c)
        if rr == 0:

            @pl.when(c != zc)
            def _():
                cp.start()

            @pl.when(c == zc)
            def _():
                mt[pl.ds(mo(sz * 320, 64), 320), pl.ds(mo(c * 128, 128), 128)] = fs[0]
        else:
            cp.start()
        fin_copies.append((rr, cp))

    def of():
        for s in range(2):
            for cc in range(2):
                dst = mt.at[pl.ds(s * 320, 320), pl.ds(cc * 128, 128)]
                got = copy_of(dst, dst, sib, hs_sem, fr_sem + 2 * s + cc)
                local = ((z == 2 * c + s) & (c == cc)) | (m4(z + 2) == 2 * c + s)

                @pl.when(jnp.logical_not(local))
                def _(got=got):
                    got.wait_recv()

        mix_out[...] = mt[...]

    steps = dict(
        h0=h0,
        hf=hf,
        hg=hg,
        hs=hs,
        hw=hw,
        m0=m0,
        mw=mw,
        nf=nf,
        ng=ng,
        nw=nw,
        oa=oa,
        od=od,
        oe=oe,
        of=of,
        o_far=o_far,
        far_in=far_in,
        pa=pa,
        pb1=pb1,
        pb2=pb2,
        pd=pd,
        s0=s0,
        s1=s1,
        s2=s2,
        s3=s3,
        s4=s4,
        scan_a=scan_a,
        scan_b=scan_b,
        final=final,
        w0=w0,
        wf=wf,
        wg=wg,
        wo0=wo0,
        wof=wof,
        wog=wog,
        wow=wow,
    )
    loads[0].wait()
    loads[1].wait()
    w_cat()
    w_init()
    loads[2].wait()
    s_pick(1)
    s_pick(0)
    loads[3].wait()
    loads[4].wait()
    pl.semaphore_wait(barrier, len(peers))

    for step in ORDER:
        name, *args = step.split()
        steps[name](*map(int, args))

    for cp in sent:
        cp.finish()
    for cp in map_copies + direct:
        cp.wait_send()
    for local, cp in h0_local:

        @pl.when(jnp.logical_not(local))
        def _(cp=cp):
            cp.wait_send()

    for rr, cp in fin_copies:
        if rr == 0:

            @pl.when(c != zc)
            def _(cp=cp):
                cp.wait_send()
        else:
            cp.wait_send()


def finish_body(mixed_t, final, mixed_out, final_out):
    mixed_out[...] = mixed_t[...].T
    final_out[...] = final[...]


def shards(hidden, snap_map, pool_states, w_zx, w_bc, w_dt, dt_bias, decay_rate, skip, norm_gain, w_out):
    vm = pl.BlockSpec(memory_space=VMEM)
    sm = pl.BlockSpec(memory_space=pltpu.SMEM)
    scratch = [
        VMEM((256, 640), BF16),
        VMEM((320, 2, 512), BF16),
        VMEM((320, 512), BF16),
        VMEM((320, 512), BF16),
        VMEM((8, 512, 256), BF16),
        VMEM((320, 3 * CH), BF16),
        VMEM((1024, 1536), BF16),
        VMEM((1536, 3 * CH), BF16),
        *[VMEM((3, 256, CH), BF16)] * 3,
        *[VMEM((3, 128, CH), BF16)] * 2,
        *[VMEM((3, 256, CH), BF16)] * 2,
        *[VMEM((3, 128, CH), F32)] * 2,
        VMEM((256, 3 * CH), BF16),
        VMEM((8, 256, 128), BF16),
        *[tuple(VMEM((4, n, 256), BF16) for n in ROWS)] * 4,
        *[tuple(VMEM((2, n, 256), BF16) for n in ROWS)] * 2,
        *[tuple(VMEM((4, n, 256), BF16) for n in ROWS)] * 2,
        *[tuple(VMEM((n, 256), BF16) for n in ROWS)] * 3,
        *[VMEM((ROWS[1] // 2, 256), BF16)] * 2,
        VMEM((512, 256), BF16),
        VMEM((256, 512), F32),
        VMEM((256, 512), BF16),
        VMEM((2, 256, 256), BF16),
        VMEM((4, 128, 128), BF16),
        VMEM((4, 4, 128, 256), BF16),
        VMEM((4, 4, 320, 256), BF16),
        VMEM((4, 320, 128), BF16),
        VMEM((8, 320, 128), BF16),
        VMEM((4, 320, 128), F32),
        *[VMEM((4, 160, 128), F32)] * 2,
        *[VMEM((4, 320, 128), BF16)] * 3,
        *[VMEM((4, 160, 128), BF16)] * 2,
        *[VMEM((4, 320, 128), BF16)] * 3,
        VMEM((640, 256), BF16),
        pltpu.SemaphoreType.DMA((N_SEM,)),
        pltpu.SemaphoreType.DMA((N_SEM,)),
        pltpu.SemaphoreType.DMA((5,)),
    ]
    mixed_t, final = pl.pallas_call(
        body,
        out_shape=(jax.ShapeDtypeStruct((640, 256), BF16), jax.ShapeDtypeStruct((512, 256), F32)),
        in_specs=[sm] * 4 + [vm] * 2 + [pl.BlockSpec(memory_space=pl.ANY)] * 5,
        out_specs=(vm, vm),
        scratch_shapes=scratch,
        compiler_params=pltpu.CompilerParams(
            collective_id=0, has_side_effects=True, vmem_limit_bytes=56 * 1024 * 1024
        ),
    )(
        snap_map,
        dt_bias,
        decay_rate,
        skip,
        norm_gain.reshape(1, 512),
        w_dt.T,
        hidden.reshape(256, 640),
        w_zx,
        w_bc,
        w_out.T,
        pool_states.reshape(8, 512, 256),
    )
    mixed, final = pl.pallas_call(
        finish_body,
        out_shape=(jax.ShapeDtypeStruct((256, 640), BF16), jax.ShapeDtypeStruct((512, 256), F32)),
        in_specs=[vm, vm],
        out_specs=(vm, vm),
    )(mixed_t, final)
    return mixed.reshape(1, 256, 640), final.reshape(1, 8, 64, 256)


def solution(mesh):
    in_specs = (
        P("pool", None, "head"),
        P(),
        P("pool", "head", None, None),
        P("pool", None, "head"),
        P("pool", None),
        P("pool", "head"),
        P("head"),
        P("head"),
        P("head"),
        P("head"),
        P("head", "pool"),
    )
    out_specs = (P("pool", None, "head"), P("pool", "head", None, None))
    return jax.shard_map(shards, mesh=mesh, in_specs=in_specs, out_specs=out_specs, check_vma=False)
```

```python
import jax
import jax.numpy as jnp
from jax import lax
from jax.experimental import pallas as pl
from jax.experimental.pallas import tpu as pltpu
from jax.sharding import PartitionSpec as P

F32 = jnp.float32
BF16 = jnp.bfloat16
MESH = pl.DeviceIdType.MESH
VMEM = pltpu.VMEM

N_SEM = 176
ROWS = (160, 352)
FIRST_ROW = (0, 160)
CH = 384


ORDER = (
    "s_pick 1",
    "h0",
    "w0 2",
    "s0 1",
    "w_init",
    "s_pick 0",
    "hs 2",
    "hs 0",
    "hs 3",
    "w0 1",
    "hf 2",
    "wf 0",
    "hf 3",
    "hg 2",
    "hs 1",
    "wf 1",
    "s1 1",
    "hw 2",
    "s0 0",
    "wg 0",
    "hf 1",
    "hg 3",
    "hw 3",
    "pa 0",
    "wf 2",
    "wg 1",
    "pa 1",
    "s1 0",
    "hg 1",
    "wo0",
    "hw 1",
    "hf 0",
    "pb1 0",
    "pb1 1",
    "pb2 0",
    "pb2 1",
    "wg 2",
    "s2 1",
    "pa 2",
    "hg 0",
    "hw 0",
    "s2 0",
    "pd 0",
    "m0",
    "pb1 2",
    "pd 1",
    "s3 1",
    "pb2 2",
    "s4 0",
    "mw",
    "wof",
    "scan_a",
    "s4 1",
    "pd 2",
    "scan_b 2",
    "scan_b 1",
    "scan_b 0",
    "wog",
    "scan_b 3",
    "nw",
    "wow",
    "oa 0",
    "nf 0",
    "nf 1",
    "oa 1",
    "final",
    "oa 3",
    "od 1",
    "ng",
    "o_far",
    "od 3",
    "oe 1",
    "od 0",
    "oe 3",
    "far_in",
    "oe 0",
    "of",
)


class Sent:
    def __init__(self, copy):
        self.copy = copy
        self.got = False
        copy.start()

    def wait_recv(self):
        assert not self.got
        self.got = True
        self.copy.wait_recv()

    def finish(self):
        if not self.got:
            self.wait_recv()
        self.copy.wait_send()


def dot_nn(a, b):
    return lax.dot_general(a, b, (((1,), (0,)), ((), ())), preferred_element_type=F32)


def dot_nt(a, b):
    return lax.dot_general(a, b, (((1,), (1,)), ((), ())), preferred_element_type=F32)


def dot_tn(a, b):
    return lax.dot_general(a, b, (((0,), (0,)), ((), ())), preferred_element_type=F32)


def body(
    snap,
    bias,
    rate,
    skip,
    gain,
    wdt,
    hid_in,
    wzx_in,
    wbc_in,
    wout_in,
    pool_in,
    mix_out,
    fin_out,
    hid,
    wzx,
    wbc,
    wout_t,
    pool,
    wcat,
    xs_,
    ws_,
    p2,
    p1,
    p3,
    r2a,
    r2b,
    r1a,
    r1b,
    ka,
    kb,
    pz,
    maps,
    f2,
    f1,
    f3,
    tt,
    q2a,
    q2b,
    q1a,
    q1b,
    v2,
    v1a,
    v1b,
    g1,
    g3,
    start,
    wi,
    wt,
    bc,
    ns,
    nbuf,
    wo,
    d2,
    h2,
    k0,
    k1,
    k3,
    o2,
    o1,
    o3,
    e2a,
    e2b,
    e2,
    e1a,
    e1b,
    fs,
    mt,
    fin,
    ss,
    rs,
    ls,
    tier,
):
    p = lax.axis_index("pool")
    h = lax.axis_index("head")
    y = p // 4
    z = lax.rem(p, 4)
    x = h // 2
    c = lax.rem(h, 2)
    sz = lax.rem(z, 2)
    zc = z // 2

    def m4(v):
        return lax.rem(v, 4)

    def dev(yy, zz, xx, cc):
        return (yy * 4 + zz, xx * 2 + cc)

    yp, ym = dev(m4(y + 1), z, x, c), dev(m4(y + 3), z, x, c)
    zp, zm = dev(y, m4(z + 1), x, c), dev(y, m4(z + 3), x, c)
    xp, xm = dev(y, z, m4(x + 1), c), dev(y, z, m4(x + 3), c)
    sib = dev(y, z, x, 1 - c)

    used = [0]
    sent = []

    def take(n=1):
        i = used[0]
        used[0] += n
        assert used[0] <= N_SEM
        return i

    def copy_of(src, dst, to, si, ri):
        return pltpu.make_async_remote_copy(
            src_ref=src, dst_ref=dst, send_sem=ss.at[si], recv_sem=rs.at[ri], device_id=to, device_id_type=MESH
        )

    def send(src, dst, to):
        i = take()
        cp = Sent(copy_of(src, dst, to, i, i))
        sent.append(cp)
        return cp

    def mo(v, n):
        return pl.multiple_of(v, n)

    barrier = pltpu.get_barrier_semaphore()
    peers = [sib, xp, xm, yp, ym]
    peers += [dev(y, m4(z + i), x, cc) for i in (1, 3) for cc in range(2)]
    for peer in peers:
        pl.semaphore_signal(barrier, inc=1, device_id=peer, device_id_type=MESH)

    loads = [
        pltpu.make_async_copy(src, dst, ls.at[i])
        for i, (src, dst) in enumerate(
            ((wzx_in, wzx), (wbc_in, wbc), (pool_in, pool), (hid_in, hid), (wout_in, wout_t))
        )
    ]
    for load in loads:
        load.start()

    hs_sem = take(4)
    hr_sem = take(4)
    h0_local = []

    def x_block(req, half_off, rows, xx):
        return xs_.at[pl.ds(mo(req * 256 + half_off, 64), rows), pl.ds(mo(xx * 384, 128), 384)]

    def h0_near():
        for s in range(2):
            for d in range(2):
                zq = 2 * c + s
                local = (z == zq) & (c == d)
                far = m4(zq + 4 - z) == 2
                src = hid.at[pl.ds(d * 128, 128), pl.ds(256 * s, 384)]
                dst = x_block(z, d * 128, 128, x)
                cp = copy_of(src, dst, dev(y, zq, x, d), hs_sem + 2 * s + d, hr_sem + z)
                h0_local.append((local, far, cp))

                @pl.when(jnp.logical_not(local | far))
                def _(cp=cp):
                    cp.start()

                @pl.when(local)
                def _(s=s, d=d):
                    xs_[pl.ds(mo(z * 256 + d * 128, 64), 128), pl.ds(mo(x * 384, 128), 384)] = hid[
                        d * 128 : d * 128 + 128, 256 * s : 256 * s + 384
                    ]

    def h0():
        pl.semaphore_wait(tier, 1)
        for _, far, cp in h0_local:

            @pl.when(far)
            def _(cp=cp):
                cp.start()

    hc = {}

    def hs(rr):
        zr = m4(z + rr)
        blk = x_block(zr, c * 128, 128, x)
        got = copy_of(blk, blk, sib, hs_sem, hr_sem + zr)
        if rr == 0:

            @pl.when(c != zc)
            def _():
                got.wait_recv()
        else:
            got.wait_recv()
        hc[rr, "p"] = send(blk, blk, xp)
        hc[rr, "m"] = send(blk, blk, xm)
        hc[rr, "s0"] = send(blk, blk, sib)

    def hf(rr):
        zr = m4(z + rr)
        hc[rr, "p"].wait_recv()
        fw = x_block(zr, c * 128, 64, m4(x + 3))
        hc[rr, "fp"] = send(fw, fw, xp)
        blk = x_block(zr, c * 128, 128, m4(x + 3))
        hc[rr, "s1"] = send(blk, blk, sib)
        hc[rr, "m"].wait_recv()
        fw = x_block(zr, c * 128 + 64, 64, m4(x + 1))
        hc[rr, "fm"] = send(fw, fw, xm)
        blk = x_block(zr, c * 128, 128, m4(x + 1))
        hc[rr, "s2"] = send(blk, blk, sib)

    def hg(rr):
        zr = m4(z + rr)
        hc[rr, "fp"].wait_recv()
        hc[rr, "fm"].wait_recv()
        blk = x_block(zr, c * 128, 128, m4(x + 2))
        hc[rr, "s3"] = send(blk, blk, sib)

    def hw(rr):
        for k in ("s0", "s1", "s2", "s3"):
            hc[rr, k].wait_recv()

    def w_block(i, off, rows, n):
        return ws_.at[pl.ds(mo(384 * i + 64 * sz + off, 32), rows), pl.ds(n * CH, CH)]

    wc = {}

    def w_cat():
        lane = lax.broadcasted_iota(jnp.int32, (320, 128), 1)
        er = lax.broadcasted_iota(jnp.int32, (8, 128), 0)
        el = lax.broadcasted_iota(jnp.int32, (8, 128), 1)
        place = jnp.where(el == er + 64 * (1 - c), 1.0, 0.0).astype(BF16)
        steps_w = dot_tn(wdt[...], place).astype(BF16)
        maps_w = wbc[:, pl.ds(mo(x * 128, 128), 128)]
        wcat[:, :128] = jnp.where(lane // 64 == c, maps_w, steps_w)
        wcat[:, 128:640] = wzx[:, 1, :]
        wcat[:, 640:] = wzx[:, 0, :]

    def w_init():
        for i in range(4):
            ws_[pl.ds(mo(384 * i + 320 * (1 - sz), 64), 64), :] = jnp.zeros((64, 3 * CH), BF16)
        ws_[pl.ds(mo(384 * y + 64 * sz, 64), 320), :] = wcat[...]

    def w0(n):
        src = wcat.at[:, pl.ds(n * CH, CH)]
        dst = w_block(y, 0, 320, n)
        wc[n, "p"] = send(src, dst, yp)
        wc[n, "m"] = send(src, dst, ym)

    def wf(n):
        wc[n, "p"].wait_recv()
        fw = w_block(m4(y + 3), 0, 160, n)
        wc[n, "fp"] = send(fw, fw, yp)
        wc[n, "m"].wait_recv()
        fw = w_block(m4(y + 1), 160, 160, n)
        wc[n, "fm"] = send(fw, fw, ym)

    def wg(n):
        wc[n, "fp"].wait_recv()
        wc[n, "fm"].wait_recv()

    pc = {}

    def part(n, rr):
        zr = m4(z + rr)
        return dot_nn(xs_[pl.ds(mo(zr * 256, 256), 256), :], ws_[:, n * CH : (n + 1) * CH])

    def pa(n):
        p2[n] = part(n, 2).astype(BF16)
        pc[n, "2a"] = send(p2.at[n, pl.ds(0, 128)], r2a.at[n], zp)
        pc[n, "2b"] = send(p2.at[n, pl.ds(128, 128)], r2b.at[n], zm)

    def pb1(n):
        a = part(n, 1)
        p1[n, 128:] = a[128:].astype(BF16)
        pc[n, "1ah"] = send(p1.at[n, pl.ds(128, 128)], r1a.at[n, pl.ds(128, 128)], zp)
        ka[n] = a[:128]
        b = part(n, 3)
        p3[n, :128] = b[:128].astype(BF16)
        pc[n, "1bl"] = send(p3.at[n, pl.ds(0, 128)], r1b.at[n, pl.ds(0, 128)], zm)
        kb[n] = b[128:]

    def pb2(n):
        pc[n, "2a"].wait_recv()
        p1[n, :128] = (ka[n] + r2a[n].astype(F32)).astype(BF16)
        pc[n, "1al"] = send(p1.at[n, pl.ds(0, 128)], r1a.at[n, pl.ds(0, 128)], zp)
        pc[n, "2b"].wait_recv()
        p3[n, 128:] = (kb[n] + r2b[n].astype(F32)).astype(BF16)
        pc[n, "1bh"] = send(p3.at[n, pl.ds(128, 128)], r1b.at[n, pl.ds(128, 128)], zm)

    def pd(n):
        own = part(n, 0)
        for k in ("1ah", "1al", "1bl", "1bh"):
            pc[n, k].wait_recv()
        pz[:, n * CH : (n + 1) * CH] = (own + r1a[n].astype(F32) + r1b[n].astype(F32)).astype(BF16)

    mr_sem = take(8)
    map_copies = []

    def m0():
        maps[h] = pz[:, :128]
        for i in range(1, 8):
            si = take()
            cp = copy_of(pz.at[:, pl.ds(0, 128)], maps.at[h], (p, lax.rem(h + i, 8)), si, mr_sem + h)
            cp.start()
            map_copies.append(cp)

    def mw():
        for i in range(1, 8):
            o = lax.rem(h + i, 8)
            copy_of(maps.at[o], maps.at[o], sib, mr_sem, mr_sem + o).wait_recv()

    sc = {}
    axes = (((y, yp, ym), (z, zp, zm)), ((z, zp, zm), (y, yp, ym)))
    far2 = (dev(y, m4(z + 2), x, c), None)

    def pick(u, a, b):
        r = a * 4 + b if u == 0 else b * 4 + a
        idx = snap[r]
        v = pool[lax.rem(idx, 8), FIRST_ROW[u] : FIRST_ROW[u] + ROWS[u], :]
        return jnp.where(idx // 8 == p, v, jnp.zeros_like(v))

    def s_pick(u):
        if u == 1:
            loads[2].wait()
        a = axes[u][0][0]
        for b in range(4):
            f2[u][b] = pick(u, m4(a + 2), b)
        for b in (2, 3):
            f1[u][b] = pick(u, m4(a + 1), b)
        for b in (0, 1):
            f3[u][b] = pick(u, m4(a + 3), b)

    def s0(u):
        (a, ap, am), _ = axes[u]
        sc[u, "2a"] = send(f2[u].at[pl.ds(0, 2)], q2a[u], ap)
        sc[u, "2b"] = send(f2[u].at[pl.ds(2, 2)], q2b[u], am)
        sc[u, "1ah"] = send(f1[u].at[pl.ds(2, 2)], q1a[u].at[pl.ds(2, 2)], ap)
        sc[u, "1bl"] = send(f3[u].at[pl.ds(0, 2)], q1b[u].at[pl.ds(0, 2)], am)

    def s1(u):
        (a, ap, am), _ = axes[u]
        sc[u, "2a"].wait_recv()
        for b in (0, 1):
            f1[u][b] = pick(u, m4(a + 1), b) + q2a[u][b]
        sc[u, "1al"] = send(f1[u].at[pl.ds(0, 2)], q1a[u].at[pl.ds(0, 2)], ap)
        sc[u, "2b"].wait_recv()
        for b in (2, 3):
            f3[u][b] = pick(u, m4(a + 3), b) + q2b[u][b - 2]
        sc[u, "1bh"] = send(f3[u].at[pl.ds(2, 2)], q1b[u].at[pl.ds(2, 2)], am)

    def s2(u):
        (a, _, _), (b0, bp, bm) = axes[u]
        sc[u, "1ah"].wait_recv()
        sc[u, "1bl"].wait_recv()
        sc[u, "1al"].wait_recv()
        sc[u, "1bh"].wait_recv()
        for b in range(4):
            tt[u][b] = pick(u, a, b) + q1a[u][b] + q1b[u][b]
        far, nxt, prv = m4(b0 + 2), m4(b0 + 1), m4(b0 + 3)
        if far2[u] is not None:
            sc[u, "v2"] = send(tt[u].at[far], v2[u], far2[u])
            sc[u, "v1a"] = send(tt[u].at[nxt], v1a[u], bp)
            sc[u, "v1b"] = send(tt[u].at[prv], v1b[u], bm)
            return
        n = ROWS[u] // 2
        sc[u, "v2a"] = send(tt[u].at[far, pl.ds(0, n)], v2[u].at[pl.ds(0, n)], bp)
        sc[u, "v2b"] = send(tt[u].at[far, pl.ds(n, n)], v2[u].at[pl.ds(n, n)], bm)
        sc[u, "v1ah"] = send(tt[u].at[nxt, pl.ds(n, n)], v1a[u].at[pl.ds(n, n)], bp)
        sc[u, "v1bl"] = send(tt[u].at[prv, pl.ds(0, n)], v1b[u].at[pl.ds(0, n)], bm)

    def s3(u):
        _, (b0, bp, bm) = axes[u]
        nxt, prv = m4(b0 + 1), m4(b0 + 3)
        n = ROWS[u] // 2
        sc[u, "v2a"].wait_recv()
        g1[...] = tt[u][nxt, :n, :] + v2[u][:n]
        sc[u, "v1al"] = send(g1, v1a[u].at[pl.ds(0, n)], bp)
        sc[u, "v2b"].wait_recv()
        g3[...] = tt[u][prv, n:, :] + v2[u][n:]
        sc[u, "v1bh"] = send(g3, v1b[u].at[pl.ds(n, n)], bm)

    def s4(u):
        _, (b0, _, _) = axes[u]
        rows = slice(FIRST_ROW[u], FIRST_ROW[u] + ROWS[u])
        if far2[u] is not None:
            for k in ("v2", "v1a", "v1b"):
                sc[u, k].wait_recv()
            start[rows] = tt[u][b0] + v1a[u][...] + v1b[u][...] + v2[u][...]
            return
        for k in ("v1ah", "v1bl", "v1al", "v1bh"):
            sc[u, k].wait_recv()
        start[rows] = tt[u][b0] + v1a[u][...] + v1b[u][...]

    oc = {}
    half = pl.ds(mo(c * 128, 128), 128)

    def wo0():
        loads[4].wait()
        for k in range(4):
            wo[y, k, :, half] = wout_t[:, 128 * k : 128 * k + 128]
        blk = wo.at[y, :, :, half]
        oc["p"] = send(blk, blk, yp)
        oc["m"] = send(blk, blk, ym)
        oc["s0"] = send(blk, blk, sib)

    def wof():
        oc["p"].wait_recv()
        fw = wo.at[m4(y + 3), :, pl.ds(0, 160), half]
        oc["fp"] = send(fw, fw, yp)
        blk = wo.at[m4(y + 3), :, :, half]
        oc["s1"] = send(blk, blk, sib)
        oc["m"].wait_recv()
        fw = wo.at[m4(y + 1), :, pl.ds(160, 160), half]
        oc["fm"] = send(fw, fw, ym)
        blk = wo.at[m4(y + 1), :, :, half]
        oc["s2"] = send(blk, blk, sib)

    def wog():
        oc["fp"].wait_recv()
        oc["fm"].wait_recv()
        blk = wo.at[m4(y + 2), :, :, half]
        oc["s3"] = send(blk, blk, sib)

    def wow():
        for k in ("s0", "s1", "s2", "s3"):
            oc[k].wait_recv()

    nc = {}
    fa = {}
    stores = []

    def scan_a():
        lane1 = lax.broadcasted_iota(jnp.int32, (1, 128), 1)

        def row_of(ref):
            row = jnp.zeros((1, 128), F32)
            for q in range(8):
                row = jnp.where(lane1 == q, ref[q], row)
            return row

        dtile = pz[:, :128].astype(F32)
        dtile = jnp.where(c == 0, pltpu.roll(dtile, 64, 1), dtile)
        v = dtile + row_of(bias)
        dt = jnp.maximum(v, 0.0) + jnp.log1p(jnp.exp(-jnp.abs(v)))
        rowi = lax.broadcasted_iota(jnp.int32, (256, 256), 0)
        coli = lax.broadcasted_iota(jnp.int32, (256, 256), 1)
        lower = rowi >= coli
        tri = jnp.where(lower, 1.0, 0.0).astype(F32)
        cum = lax.dot_general(
            tri,
            -(row_of(rate) * dt),
            (((1,), (0,)), ((), ())),
            precision=lax.Precision.HIGHEST,
            preferred_element_type=F32,
        )
        ecum = jnp.exp(cum)
        tail = jnp.exp(cum[255:256, :] - cum) * dt
        cum_t = cum.T
        dt_t = dt.T
        first = lax.broadcasted_iota(jnp.int32, (256, 128), 1) < 64
        for i in range(2):
            bc[0, :, 128 * i : 128 * i + 128] = jnp.where(first, maps[2 * i], maps[2 * i + 1])
            bc[1, :, 128 * i : 128 * i + 128] = jnp.where(first, maps[4 + 2 * i], maps[5 + 2 * i])
        scores = dot_nt(bc[1], bc[0])
        for k in range(4):
            xv = pz[:, 128 + 128 * k : 256 + 128 * k]

            def within(q):
                spread = jnp.where(lower, cum[:, q : q + 1] - cum_t[q : q + 1, :], -1e30)
                mix = jnp.exp(spread) * dt_t[q : q + 1, :] * scores
                return dot_nn(mix.astype(BF16), xv)

            cols = slice(128 * k, 128 * k + 128)
            wi[:, cols] = jnp.where(first, within(2 * k), within(2 * k + 1))
            w = jnp.where(first, tail[:, 2 * k : 2 * k + 1], tail[:, 2 * k + 1 : 2 * k + 2])
            wt[:, cols] = (xv.astype(F32) * w).astype(BF16)
        fa["ecum"] = ecum

    def scan_b(k):
        ecum = fa["ecum"]
        lo, hi = 2 * k, 2 * k + 1
        cols = slice(128 * k, 128 * k + 128)
        first = lax.broadcasted_iota(jnp.int32, (256, 128), 1) < 64
        r128 = lax.broadcasted_iota(jnp.int32, (128, 128), 0) // 64
        c128 = lax.broadcasted_iota(jnp.int32, (128, 128), 1) // 64
        same = jnp.where(r128 == c128, 1.0 / 64.0, 0.0).astype(BF16)
        xf = pz[:, 128 + 128 * k : 256 + 128 * k].astype(F32)
        gate = pz[:, 640 + 128 * k : 768 + 128 * k].astype(F32)
        s_in = start[cols, :]
        decay = jnp.where(first, ecum[:, lo : lo + 1], ecum[:, hi : hi + 1])
        scanned = wi[:, cols] + decay * dot_nt(bc[1], s_in)
        skips = jnp.where(first, skip[lo], skip[hi])
        gated = (scanned + skips * xf) * (gate / (1.0 + jnp.exp(-gate)))
        sq = gated * gated
        sq_hi = sq.astype(BF16)
        sq_lo = (sq - sq_hi.astype(F32)).astype(BF16)
        meansq = dot_nn(sq_hi, same) + dot_nn(sq_lo, same)
        normed = (gated * lax.rsqrt(meansq + 1e-05) * gain[:, cols]).astype(BF16)
        upper, under = normed[:128], normed[128:]
        nbuf[z, k, :, half] = jnp.where(c == 0, upper, under)
        ns[k] = jnp.where(c == 0, under, upper)
        dst = nbuf.at[z, k, :, half]
        nc[k, "pd"] = send(ns.at[k], dst, dev(y, m4(z + 1), x, 1 - c))
        nc[k, "md"] = send(ns.at[k], dst, dev(y, m4(z + 3), x, 1 - c))
        nc[k, "pc"] = send(dst, dst, zp)
        nc[k, "mc"] = send(dst, dst, zm)
        nc[k, "s"] = send(ns.at[k], dst, sib)

    def final():
        ecum = fa["ecum"]
        rows_first = lax.broadcasted_iota(jnp.int32, (128, 256), 0) < 64
        for k in range(4):
            cols = slice(128 * k, 128 * k + 128)
            lo, hi = 2 * k, 2 * k + 1
            last = jnp.where(rows_first, ecum[255:256, lo : lo + 1], ecum[255:256, hi : hi + 1])
            fin[cols, :] = last * start[cols, :].astype(F32) + dot_tn(wt[:, cols], bc[0])

        stores.append(pltpu.make_async_copy(fin, fin_out, ls.at[5]))
        stores[-1].start()

    def nf(j):
        for k in (2 * j, 2 * j + 1):
            nc[k, "pc"].wait_recv()
            nc[k, "pd"].wait_recv()
        fw = nbuf.at[m4(z + 3), pl.ds(2 * j, 2), pl.ds(0, 64)]
        nc[j, "fp"] = send(fw, fw, zp)
        for k in (2 * j, 2 * j + 1):
            nc[k, "mc"].wait_recv()
            nc[k, "md"].wait_recv()
        fw = nbuf.at[m4(z + 1), pl.ds(2 * j, 2), pl.ds(64, 64)]
        nc[j, "fm"] = send(fw, fw, zm)

    def ng():
        for j in range(2):
            nc[j, "fp"].wait_recv()
            nc[j, "fm"].wait_recv()

    def nw():
        for k in range(4):
            nc[k, "s"].wait_recv()

    xc = {}
    fr_sem = take(4)
    fin_copies = []

    def out_prod(zr, i):
        o = dot_nt(wo[i, 0], nbuf[zr, 0])
        for k in range(1, 4):
            o = o + dot_nt(wo[i, k], nbuf[zr, k])
        return o

    d_sem = take(8)
    direct = []

    def o_far():
        for ii in (2, 1, 3, 0):
            i = m4(x + ii)
            d2[ii] = out_prod(m4(z + 2), i).astype(BF16)
            cp = copy_of(d2.at[ii], h2.at[2 * ii + c], dev(y, m4(z + 2), i, zc), take(), d_sem + 2 * ii + c)
            cp.start()
            direct.append(cp)

    def far_in():
        @pl.when(c == m4(z + 2) // 2)
        def _():
            for cc in range(2):
                total = jnp.zeros((320, 128), F32)
                for ii in (0, 1, 3, 2):
                    q = 2 * ii + cc
                    copy_of(h2.at[q], h2.at[q], sib, hs_sem, d_sem + q).wait_recv()
                    total = total + h2[q].astype(F32)
                mt[pl.ds(mo(sz * 320, 64), 320), 128 * cc : 128 * cc + 128] = total.astype(BF16)

    def oa(rr):
        zr = m4(z + rr)

        def prod(ii):
            return out_prod(zr, m4(x + ii))

        o2[rr] = prod(2).astype(BF16)
        xc[rr, "2a"] = send(o2.at[rr, pl.ds(0, 160)], e2a.at[rr], xp)
        xc[rr, "2b"] = send(o2.at[rr, pl.ds(160, 160)], e2b.at[rr], xm)
        o = prod(1)
        k1[rr] = o[:160]
        o1[rr, 160:] = o[160:].astype(BF16)
        xc[rr, "1ah"] = send(o1.at[rr, pl.ds(160, 160)], e1a.at[rr, pl.ds(160, 160)], xp)
        o = prod(3)
        k3[rr] = o[160:]
        o3[rr, :160] = o[:160].astype(BF16)
        xc[rr, "1bl"] = send(o3.at[rr, pl.ds(0, 160)], e1b.at[rr, pl.ds(0, 160)], xm)
        k0[rr] = prod(0)

    def od(rr):
        xc[rr, "2a"].wait_recv()
        o1[rr, :160] = (k1[rr] + e2a[rr].astype(F32)).astype(BF16)
        xc[rr, "1al"] = send(o1.at[rr, pl.ds(0, 160)], e1a.at[rr, pl.ds(0, 160)], xp)
        xc[rr, "2b"].wait_recv()
        o3[rr, 160:] = (k3[rr] + e2b[rr].astype(F32)).astype(BF16)
        xc[rr, "1bh"] = send(o3.at[rr, pl.ds(160, 160)], e1b.at[rr, pl.ds(160, 160)], xm)

    def ox(rr):
        zr = m4(z + rr)
        o2[rr] = out_prod(zr, m4(x + 2)).astype(BF16)
        xc[rr, "2"] = send(o2.at[rr], e2.at[rr], dev(y, z, m4(x + 2), c))
        o1[rr] = out_prod(zr, m4(x + 1)).astype(BF16)
        xc[rr, "1a"] = send(o1.at[rr], e1a.at[rr], xp)
        o3[rr] = out_prod(zr, m4(x + 3)).astype(BF16)
        xc[rr, "1b"] = send(o3.at[rr], e1b.at[rr], xm)
        k0[rr] = out_prod(zr, x)

    def oxe(rr):
        for k in ("2", "1a", "1b"):
            xc[rr, k].wait_recv()
        home(rr, k0[rr] + e1a[rr].astype(F32) + e1b[rr].astype(F32) + e2[rr].astype(F32))

    def oe(rr):
        for k in ("1ah", "1bl", "1al", "1bh"):
            xc[rr, k].wait_recv()
        home(rr, k0[rr] + e1a[rr].astype(F32) + e1b[rr].astype(F32))

    def home(rr, total):
        fs[rr] = total.astype(BF16)
        dst = mt.at[pl.ds(mo(sz * 320, 64), 320), pl.ds(mo(c * 128, 128), 128)]
        cp = copy_of(fs.at[rr], dst, dev(y, m4(z + rr), x, zc), take(), fr_sem + 2 * sz + c)
        if rr == 0:

            @pl.when(c != zc)
            def _():
                cp.start()

            @pl.when(c == zc)
            def _():
                mt[pl.ds(mo(sz * 320, 64), 320), pl.ds(mo(c * 128, 128), 128)] = fs[0]
        else:
            cp.start()
        fin_copies.append((rr, cp))

    def of():
        for s in range(2):
            for cc in range(2):
                dst = mt.at[pl.ds(s * 320, 320), pl.ds(cc * 128, 128)]
                got = copy_of(dst, dst, sib, hs_sem, fr_sem + 2 * s + cc)
                local = ((z == 2 * c + s) & (c == cc)) | (m4(z + 2) == 2 * c + s)

                @pl.when(jnp.logical_not(local))
                def _(got=got):
                    got.wait_recv()

        stores.append(pltpu.make_async_copy(mt, mix_out, ls.at[6]))
        stores[-1].start()

    steps = dict(
        h0=h0,
        hf=hf,
        hg=hg,
        hs=hs,
        hw=hw,
        m0=m0,
        mw=mw,
        nf=nf,
        ng=ng,
        nw=nw,
        oa=oa,
        od=od,
        oe=oe,
        ox=ox,
        oxe=oxe,
        of=of,
        o_far=o_far,
        far_in=far_in,
        pa=pa,
        pb1=pb1,
        pb2=pb2,
        pd=pd,
        s0=s0,
        s1=s1,
        s2=s2,
        s3=s3,
        s4=s4,
        scan_a=scan_a,
        scan_b=scan_b,
        final=final,
        w0=w0,
        s_pick=s_pick,
        w_init=w_init,
        wf=wf,
        wg=wg,
        wo0=wo0,
        wof=wof,
        wog=wog,
        wow=wow,
    )
    loads[0].wait()
    loads[1].wait()
    w_cat()
    loads[3].wait()
    pl.semaphore_wait(barrier, len(peers))
    pl.semaphore_signal(tier, inc=1, device_id=zm, device_id_type=MESH)
    w0(0)
    h0_near()

    for step in ORDER:
        name, *args = step.split()
        steps[name](*map(int, args))

    for cp in sent:
        cp.finish()
    for cp in stores:
        cp.wait()
    for cp in map_copies + direct:
        cp.wait_send()
    for local, _, cp in h0_local:

        @pl.when(jnp.logical_not(local))
        def _(cp=cp):
            cp.wait_send()

    for rr, cp in fin_copies:
        if rr == 0:

            @pl.when(c != zc)
            def _(cp=cp):
                cp.wait_send()
        else:
            cp.wait_send()


def finish_body(mixed_t, final, mixed_out, final_out, mixed, sems):
    copies = [
        pltpu.make_async_copy(final, final_out, sems.at[0]),
        pltpu.make_async_copy(mixed, mixed_out, sems.at[1]),
    ]
    copies[0].start()
    mixed[...] = mixed_t[...].T
    copies[1].start()
    for cp in copies:
        cp.wait()


def shards(hidden, snap_map, pool_states, w_zx, w_bc, w_dt, dt_bias, decay_rate, skip, norm_gain, w_out):
    vm = pl.BlockSpec(memory_space=VMEM)
    sm = pl.BlockSpec(memory_space=pltpu.SMEM)
    hbm = pl.BlockSpec(memory_space=pl.ANY)
    scratch = [
        VMEM((256, 640), BF16),
        VMEM((320, 2, 512), BF16),
        VMEM((320, 512), BF16),
        VMEM((320, 512), BF16),
        VMEM((8, 512, 256), BF16),
        VMEM((320, 3 * CH), BF16),
        VMEM((1024, 1536), BF16),
        VMEM((1536, 3 * CH), BF16),
        *[VMEM((3, 256, CH), BF16)] * 3,
        *[VMEM((3, 128, CH), BF16)] * 2,
        *[VMEM((3, 256, CH), BF16)] * 2,
        *[VMEM((3, 128, CH), F32)] * 2,
        VMEM((256, 3 * CH), BF16),
        VMEM((8, 256, 128), BF16),
        *[tuple(VMEM((4, n, 256), BF16) for n in ROWS)] * 4,
        *[tuple(VMEM((2, n, 256), BF16) for n in ROWS)] * 2,
        *[tuple(VMEM((4, n, 256), BF16) for n in ROWS)] * 2,
        *[tuple(VMEM((n, 256), BF16) for n in ROWS)] * 3,
        *[VMEM((ROWS[1] // 2, 256), BF16)] * 2,
        VMEM((512, 256), BF16),
        VMEM((256, 512), F32),
        VMEM((256, 512), BF16),
        VMEM((2, 256, 256), BF16),
        VMEM((4, 128, 128), BF16),
        VMEM((4, 4, 128, 256), BF16),
        VMEM((4, 4, 320, 256), BF16),
        VMEM((4, 320, 128), BF16),
        VMEM((8, 320, 128), BF16),
        VMEM((4, 320, 128), F32),
        *[VMEM((4, 160, 128), F32)] * 2,
        *[VMEM((4, 320, 128), BF16)] * 3,
        *[VMEM((4, 160, 128), BF16)] * 2,
        *[VMEM((4, 320, 128), BF16)] * 4,
        VMEM((640, 256), BF16),
        VMEM((512, 256), F32),
        pltpu.SemaphoreType.DMA((N_SEM,)),
        pltpu.SemaphoreType.DMA((N_SEM,)),
        pltpu.SemaphoreType.DMA((7,)),
        pltpu.SemaphoreType.REGULAR,
    ]
    mixed_t, final = pl.pallas_call(
        body,
        out_shape=(jax.ShapeDtypeStruct((640, 256), BF16), jax.ShapeDtypeStruct((512, 256), F32)),
        in_specs=[sm] * 4 + [vm] * 2 + [hbm] * 5,
        out_specs=(hbm, hbm),
        scratch_shapes=scratch,
        compiler_params=pltpu.CompilerParams(
            collective_id=0, has_side_effects=True, vmem_limit_bytes=56 * 1024 * 1024
        ),
    )(
        snap_map,
        dt_bias,
        decay_rate,
        skip,
        norm_gain.reshape(1, 512),
        w_dt.T,
        hidden.reshape(256, 640),
        w_zx,
        w_bc,
        w_out.T,
        pool_states.reshape(8, 512, 256),
    )
    mixed, final = pl.pallas_call(
        finish_body,
        out_shape=(jax.ShapeDtypeStruct((256, 640), BF16), jax.ShapeDtypeStruct((512, 256), F32)),
        in_specs=[vm, vm],
        out_specs=(hbm, hbm),
        scratch_shapes=[VMEM((256, 640), BF16), pltpu.SemaphoreType.DMA((2,))],
    )(mixed_t, final)
    return mixed.reshape(1, 256, 640), final.reshape(1, 8, 64, 256)


def solution(mesh):
    in_specs = (
        P("pool", None, "head"),
        P(),
        P("pool", "head", None, None),
        P("pool", None, "head"),
        P("pool", None),
        P("pool", "head"),
        P("head"),
        P("head"),
        P("head"),
        P("head"),
        P("head", "pool"),
    )
    out_specs = (P("pool", None, "head"), P("pool", "head", None, None))
    return jax.shard_map(shards, mesh=mesh, in_specs=in_specs, out_specs=out_specs, check_vma=False)
```

```python
import jax
import jax.numpy as jnp
from jax import lax
from jax.experimental import pallas as pl
from jax.experimental.pallas import tpu as pltpu
from jax.sharding import PartitionSpec as P

F32 = jnp.float32
BF16 = jnp.bfloat16
MESH = pl.DeviceIdType.MESH
VMEM = pltpu.VMEM

N_SEM = 176
ROWS = (160, 352)
FIRST_ROW = (0, 160)
CH = 384


ORDER = (
    "s_pick 1",
    "h0",
    "w0 2",
    "s0 1",
    "w_init",
    "s_pick 0",
    "hs 2",
    "hs 0",
    "hs 3",
    "w0 1",
    "hf 2",
    "wf 0",
    "hf 3",
    "hg 2",
    "hs 1",
    "wf 1",
    "s1 1",
    "hw 2",
    "s0 0",
    "wg 0",
    "hf 1",
    "hg 3",
    "hw 3",
    "pa 0",
    "wf 2",
    "wg 1",
    "pa 1",
    "s1 0",
    "hg 1",
    "hw 1",
    "hf 0",
    "pb1 0",
    "pb1 1",
    "pb2 0",
    "pb2 1",
    "wg 2",
    "s2 1",
    "wo0",
    "pa 2",
    "hg 0",
    "hw 0",
    "s2 0",
    "pd 0",
    "m0",
    "pb1 2",
    "pd 1",
    "s3 1",
    "pb2 2",
    "s4 0",
    "mw",
    "wof",
    "scan_a",
    "s4 1",
    "pd 2",
    "scan_b 0",
    "scan_b 1",
    "scan_b 2",
    "scan_b 3",
    "wog",
    "nw",
    "wow",
    "oa 0",
    "nf 0",
    "nf 1",
    "oa 1",
    "final",
    "oa 3",
    "od 1",
    "ng",
    "o_far",
    "od 3",
    "oe 1",
    "od 0",
    "oe 3",
    "far_in",
    "oe 0",
    "of",
)


class Sent:
    def __init__(self, copy):
        self.copy = copy
        self.got = False
        copy.start()

    def wait_recv(self):
        assert not self.got
        self.got = True
        self.copy.wait_recv()

    def finish(self):
        if not self.got:
            self.wait_recv()
        self.copy.wait_send()


def dot_nn(a, b):
    return lax.dot_general(a, b, (((1,), (0,)), ((), ())), preferred_element_type=F32)


def dot_nt(a, b):
    return lax.dot_general(a, b, (((1,), (1,)), ((), ())), preferred_element_type=F32)


def dot_tn(a, b):
    return lax.dot_general(a, b, (((0,), (0,)), ((), ())), preferred_element_type=F32)


def body(
    snap,
    bias,
    rate,
    skip,
    gain,
    wdt,
    hid_in,
    wzx_in,
    wbc_in,
    wout_in,
    pool_in,
    mix_out,
    fin_out,
    hid,
    wzx,
    wbc,
    wout_t,
    pool,
    wcat,
    xs_,
    ws_,
    p2,
    p1,
    p3,
    r2a,
    r2b,
    r1a,
    r1b,
    ka,
    kb,
    pz,
    maps,
    f2,
    f1,
    f3,
    tt,
    q2a,
    q2b,
    q1a,
    q1b,
    v2,
    v1a,
    v1b,
    g1,
    g3,
    start,
    wi,
    wt,
    bc,
    ns,
    nbuf,
    wo,
    d2,
    h2,
    k0,
    k1,
    k3,
    o2,
    o1,
    o3,
    e2a,
    e2b,
    e2,
    e1a,
    e1b,
    fs,
    mt,
    fin,
    ss,
    rs,
    ls,
    tier,
):
    p = lax.axis_index("pool")
    h = lax.axis_index("head")
    y = p // 4
    z = lax.rem(p, 4)
    x = h // 2
    c = lax.rem(h, 2)
    sz = lax.rem(z, 2)
    zc = z // 2

    def m4(v):
        return lax.rem(v, 4)

    def dev(yy, zz, xx, cc):
        return (yy * 4 + zz, xx * 2 + cc)

    yp, ym = dev(m4(y + 1), z, x, c), dev(m4(y + 3), z, x, c)
    zp, zm = dev(y, m4(z + 1), x, c), dev(y, m4(z + 3), x, c)
    xp, xm = dev(y, z, m4(x + 1), c), dev(y, z, m4(x + 3), c)
    sib = dev(y, z, x, 1 - c)

    used = [0]
    sent = []

    def take(n=1):
        i = used[0]
        used[0] += n
        assert used[0] <= N_SEM
        return i

    def copy_of(src, dst, to, si, ri):
        return pltpu.make_async_remote_copy(
            src_ref=src, dst_ref=dst, send_sem=ss.at[si], recv_sem=rs.at[ri], device_id=to, device_id_type=MESH
        )

    def send(src, dst, to):
        i = take()
        cp = Sent(copy_of(src, dst, to, i, i))
        sent.append(cp)
        return cp

    def mo(v, n):
        return pl.multiple_of(v, n)

    barrier = pltpu.get_barrier_semaphore()
    peers = [sib, xp, xm, yp, ym]
    peers += [dev(y, m4(z + i), x, cc) for i in (1, 3) for cc in range(2)]
    for peer in peers:
        pl.semaphore_signal(barrier, inc=1, device_id=peer, device_id_type=MESH)

    loads = [
        pltpu.make_async_copy(src, dst, ls.at[i])
        for i, (src, dst) in enumerate(
            ((wzx_in, wzx), (wbc_in, wbc), (pool_in, pool), (hid_in, hid), (wout_in, wout_t))
        )
    ]
    for load in loads:
        load.start()

    hs_sem = take(4)
    hr_sem = take(4)
    h0_local = []

    def x_block(req, half_off, rows, xx):
        return xs_.at[pl.ds(mo(req * 256 + half_off, 64), rows), pl.ds(mo(xx * 384, 128), 384)]

    def h0_near():
        for s in range(2):
            for d in range(2):
                zq = 2 * c + s
                local = (z == zq) & (c == d)
                far = m4(zq + 4 - z) == 2
                src = hid.at[pl.ds(d * 128, 128), pl.ds(256 * s, 384)]
                dst = x_block(z, d * 128, 128, x)
                cp = copy_of(src, dst, dev(y, zq, x, d), hs_sem + 2 * s + d, hr_sem + z)
                h0_local.append((local, far, cp))

                @pl.when(jnp.logical_not(local | far))
                def _(cp=cp):
                    cp.start()

                @pl.when(local)
                def _(s=s, d=d):
                    xs_[pl.ds(mo(z * 256 + d * 128, 64), 128), pl.ds(mo(x * 384, 128), 384)] = hid[
                        d * 128 : d * 128 + 128, 256 * s : 256 * s + 384
                    ]

    def h0():
        pl.semaphore_wait(tier, 1)
        for _, far, cp in h0_local:

            @pl.when(far)
            def _(cp=cp):
                cp.start()

    hc = {}

    def hs(rr):
        zr = m4(z + rr)
        blk = x_block(zr, c * 128, 128, x)
        got = copy_of(blk, blk, sib, hs_sem, hr_sem + zr)
        if rr == 0:

            @pl.when(c != zc)
            def _():
                got.wait_recv()
        else:
            got.wait_recv()
        hc[rr, "p"] = send(blk, blk, xp)
        hc[rr, "m"] = send(blk, blk, xm)
        hc[rr, "s0"] = send(blk, blk, sib)

    def hf(rr):
        zr = m4(z + rr)
        hc[rr, "p"].wait_recv()
        fw = x_block(zr, c * 128, 64, m4(x + 3))
        hc[rr, "fp"] = send(fw, fw, xp)
        blk = x_block(zr, c * 128, 128, m4(x + 3))
        hc[rr, "s1"] = send(blk, blk, sib)
        hc[rr, "m"].wait_recv()
        fw = x_block(zr, c * 128 + 64, 64, m4(x + 1))
        hc[rr, "fm"] = send(fw, fw, xm)
        blk = x_block(zr, c * 128, 128, m4(x + 1))
        hc[rr, "s2"] = send(blk, blk, sib)

    def hg(rr):
        zr = m4(z + rr)
        hc[rr, "fp"].wait_recv()
        hc[rr, "fm"].wait_recv()
        blk = x_block(zr, c * 128, 128, m4(x + 2))
        hc[rr, "s3"] = send(blk, blk, sib)

    def hw(rr):
        for k in ("s0", "s1", "s2", "s3"):
            hc[rr, k].wait_recv()

    def w_block(i, off, rows, n):
        return ws_.at[pl.ds(mo(384 * i + 64 * sz + off, 32), rows), pl.ds(n * CH, CH)]

    wc = {}

    def w_cat():
        lane = lax.broadcasted_iota(jnp.int32, (320, 128), 1)
        er = lax.broadcasted_iota(jnp.int32, (8, 128), 0)
        el = lax.broadcasted_iota(jnp.int32, (8, 128), 1)
        place = jnp.where(el == er + 64 * (1 - c), 1.0, 0.0).astype(BF16)
        steps_w = dot_tn(wdt[...], place).astype(BF16)
        maps_w = wbc[:, pl.ds(mo(x * 128, 128), 128)]
        wcat[:, :128] = jnp.where(lane // 64 == c, maps_w, steps_w)
        wcat[:, 128:640] = wzx[:, 1, :]
        wcat[:, 640:] = wzx[:, 0, :]

    def w_init():
        for i in range(4):
            ws_[pl.ds(mo(384 * i + 320 * (1 - sz), 64), 64), :] = jnp.zeros((64, 3 * CH), BF16)
        ws_[pl.ds(mo(384 * y + 64 * sz, 64), 320), :] = wcat[...]

    def w0(n):
        src = wcat.at[:, pl.ds(n * CH, CH)]
        dst = w_block(y, 0, 320, n)
        wc[n, "p"] = send(src, dst, yp)
        wc[n, "m"] = send(src, dst, ym)

    def wf(n):
        wc[n, "p"].wait_recv()
        fw = w_block(m4(y + 3), 0, 160, n)
        wc[n, "fp"] = send(fw, fw, yp)
        wc[n, "m"].wait_recv()
        fw = w_block(m4(y + 1), 160, 160, n)
        wc[n, "fm"] = send(fw, fw, ym)

    def wg(n):
        wc[n, "fp"].wait_recv()
        wc[n, "fm"].wait_recv()

    pc = {}

    def part(n, rr):
        zr = m4(z + rr)
        return dot_nn(xs_[pl.ds(mo(zr * 256, 256), 256), :], ws_[:, n * CH : (n + 1) * CH])

    def pa(n):
        p2[n] = part(n, 2).astype(BF16)
        pc[n, "2a"] = send(p2.at[n, pl.ds(0, 128)], r2a.at[n], zp)
        pc[n, "2b"] = send(p2.at[n, pl.ds(128, 128)], r2b.at[n], zm)

    def pb1(n):
        a = part(n, 1)
        p1[n, 128:] = a[128:].astype(BF16)
        pc[n, "1ah"] = send(p1.at[n, pl.ds(128, 128)], r1a.at[n, pl.ds(128, 128)], zp)
        ka[n] = a[:128]
        b = part(n, 3)
        p3[n, :128] = b[:128].astype(BF16)
        pc[n, "1bl"] = send(p3.at[n, pl.ds(0, 128)], r1b.at[n, pl.ds(0, 128)], zm)
        kb[n] = b[128:]

    def pb2(n):
        pc[n, "2a"].wait_recv()
        p1[n, :128] = (ka[n] + r2a[n].astype(F32)).astype(BF16)
        pc[n, "1al"] = send(p1.at[n, pl.ds(0, 128)], r1a.at[n, pl.ds(0, 128)], zp)
        pc[n, "2b"].wait_recv()
        p3[n, 128:] = (kb[n] + r2b[n].astype(F32)).astype(BF16)
        pc[n, "1bh"] = send(p3.at[n, pl.ds(128, 128)], r1b.at[n, pl.ds(128, 128)], zm)

    def pd(n):
        own = part(n, 0)
        for k in ("1ah", "1al", "1bl", "1bh"):
            pc[n, k].wait_recv()
        pz[:, n * CH : (n + 1) * CH] = (own + r1a[n].astype(F32) + r1b[n].astype(F32)).astype(BF16)

    mr_sem = take(8)
    map_copies = []

    def m0():
        maps[h] = pz[:, :128]
        for i in range(1, 8):
            si = take()
            cp = copy_of(pz.at[:, pl.ds(0, 128)], maps.at[h], (p, lax.rem(h + i, 8)), si, mr_sem + h)
            cp.start()
            map_copies.append(cp)

    def mw():
        for i in range(1, 8):
            o = lax.rem(h + i, 8)
            copy_of(maps.at[o], maps.at[o], sib, mr_sem, mr_sem + o).wait_recv()

    sc = {}
    axes = (((y, yp, ym), (z, zp, zm)), ((z, zp, zm), (y, yp, ym)))
    far2 = (dev(y, m4(z + 2), x, c), None)

    def pick(u, a, b):
        r = a * 4 + b if u == 0 else b * 4 + a
        idx = snap[r]
        v = pool[lax.rem(idx, 8), FIRST_ROW[u] : FIRST_ROW[u] + ROWS[u], :]
        return jnp.where(idx // 8 == p, v, jnp.zeros_like(v))

    def s_pick(u):
        if u == 1:
            loads[2].wait()
        a = axes[u][0][0]
        for b in range(4):
            f2[u][b] = pick(u, m4(a + 2), b)
        for b in (2, 3):
            f1[u][b] = pick(u, m4(a + 1), b)
        for b in (0, 1):
            f3[u][b] = pick(u, m4(a + 3), b)

    def s0(u):
        (a, ap, am), _ = axes[u]
        sc[u, "2a"] = send(f2[u].at[pl.ds(0, 2)], q2a[u], ap)
        sc[u, "2b"] = send(f2[u].at[pl.ds(2, 2)], q2b[u], am)
        sc[u, "1ah"] = send(f1[u].at[pl.ds(2, 2)], q1a[u].at[pl.ds(2, 2)], ap)
        sc[u, "1bl"] = send(f3[u].at[pl.ds(0, 2)], q1b[u].at[pl.ds(0, 2)], am)

    def s1(u):
        (a, ap, am), _ = axes[u]
        sc[u, "2a"].wait_recv()
        for b in (0, 1):
            f1[u][b] = pick(u, m4(a + 1), b) + q2a[u][b]
        sc[u, "1al"] = send(f1[u].at[pl.ds(0, 2)], q1a[u].at[pl.ds(0, 2)], ap)
        sc[u, "2b"].wait_recv()
        for b in (2, 3):
            f3[u][b] = pick(u, m4(a + 3), b) + q2b[u][b - 2]
        sc[u, "1bh"] = send(f3[u].at[pl.ds(2, 2)], q1b[u].at[pl.ds(2, 2)], am)

    def s2(u):
        (a, _, _), (b0, bp, bm) = axes[u]
        sc[u, "1ah"].wait_recv()
        sc[u, "1bl"].wait_recv()
        sc[u, "1al"].wait_recv()
        sc[u, "1bh"].wait_recv()
        for b in range(4):
            tt[u][b] = pick(u, a, b) + q1a[u][b] + q1b[u][b]
        far, nxt, prv = m4(b0 + 2), m4(b0 + 1), m4(b0 + 3)
        if far2[u] is not None:
            sc[u, "v2"] = send(tt[u].at[far], v2[u], far2[u])
            sc[u, "v1a"] = send(tt[u].at[nxt], v1a[u], bp)
            sc[u, "v1b"] = send(tt[u].at[prv], v1b[u], bm)
            return
        n = ROWS[u] // 2
        sc[u, "v2a"] = send(tt[u].at[far, pl.ds(0, n)], v2[u].at[pl.ds(0, n)], bp)
        sc[u, "v2b"] = send(tt[u].at[far, pl.ds(n, n)], v2[u].at[pl.ds(n, n)], bm)
        sc[u, "v1ah"] = send(tt[u].at[nxt, pl.ds(n, n)], v1a[u].at[pl.ds(n, n)], bp)
        sc[u, "v1bl"] = send(tt[u].at[prv, pl.ds(0, n)], v1b[u].at[pl.ds(0, n)], bm)

    def s3(u):
        _, (b0, bp, bm) = axes[u]
        nxt, prv = m4(b0 + 1), m4(b0 + 3)
        n = ROWS[u] // 2
        sc[u, "v2a"].wait_recv()
        g1[...] = tt[u][nxt, :n, :] + v2[u][:n]
        sc[u, "v1al"] = send(g1, v1a[u].at[pl.ds(0, n)], bp)
        sc[u, "v2b"].wait_recv()
        g3[...] = tt[u][prv, n:, :] + v2[u][n:]
        sc[u, "v1bh"] = send(g3, v1b[u].at[pl.ds(n, n)], bm)

    def s4(u):
        _, (b0, _, _) = axes[u]
        rows = slice(FIRST_ROW[u], FIRST_ROW[u] + ROWS[u])
        if far2[u] is not None:
            for k in ("v2", "v1a", "v1b"):
                sc[u, k].wait_recv()
            start[rows] = tt[u][b0] + v1a[u][...] + v1b[u][...] + v2[u][...]
            return
        for k in ("v1ah", "v1bl", "v1al", "v1bh"):
            sc[u, k].wait_recv()
        start[rows] = tt[u][b0] + v1a[u][...] + v1b[u][...]

    oc = {}
    half = pl.ds(mo(c * 128, 128), 128)

    def wo0():
        loads[4].wait()
        for k in range(4):
            wo[y, k, :, half] = wout_t[:, 128 * k : 128 * k + 128]
        blk = wo.at[y, :, :, half]
        oc["p"] = send(blk, blk, yp)
        oc["m"] = send(blk, blk, ym)
        oc["s0"] = send(blk, blk, sib)

    def wof():
        oc["p"].wait_recv()
        fw = wo.at[m4(y + 3), :, pl.ds(0, 160), half]
        oc["fp"] = send(fw, fw, yp)
        blk = wo.at[m4(y + 3), :, :, half]
        oc["s1"] = send(blk, blk, sib)
        oc["m"].wait_recv()
        fw = wo.at[m4(y + 1), :, pl.ds(160, 160), half]
        oc["fm"] = send(fw, fw, ym)
        blk = wo.at[m4(y + 1), :, :, half]
        oc["s2"] = send(blk, blk, sib)

    def wog():
        oc["fp"].wait_recv()
        oc["fm"].wait_recv()
        blk = wo.at[m4(y + 2), :, :, half]
        oc["s3"] = send(blk, blk, sib)

    def wow():
        for k in ("s0", "s1", "s2", "s3"):
            oc[k].wait_recv()

    nc = {}
    fa = {}
    stores = []

    def scan_a():
        lane1 = lax.broadcasted_iota(jnp.int32, (1, 128), 1)

        def row_of(ref):
            row = jnp.zeros((1, 128), F32)
            for q in range(8):
                row = jnp.where(lane1 == q, ref[q], row)
            return row

        dtile = pz[:, :128].astype(F32)
        dtile = jnp.where(c == 0, pltpu.roll(dtile, 64, 1), dtile)
        v = dtile + row_of(bias)
        dt = jnp.maximum(v, 0.0) + jnp.log1p(jnp.exp(-jnp.abs(v)))
        rowi = lax.broadcasted_iota(jnp.int32, (256, 256), 0)
        coli = lax.broadcasted_iota(jnp.int32, (256, 256), 1)
        lower = rowi >= coli
        tri = jnp.where(lower, 1.0, 0.0).astype(F32)
        cum = lax.dot_general(
            tri,
            -(row_of(rate) * dt),
            (((1,), (0,)), ((), ())),
            precision=lax.Precision.HIGHEST,
            preferred_element_type=F32,
        )
        ecum = jnp.exp(cum)
        tail = jnp.exp(cum[255:256, :] - cum) * dt
        cum_t = cum.T
        dt_t = dt.T
        first = lax.broadcasted_iota(jnp.int32, (256, 128), 1) < 64
        for i in range(2):
            bc[0, :, 128 * i : 128 * i + 128] = jnp.where(first, maps[2 * i], maps[2 * i + 1])
            bc[1, :, 128 * i : 128 * i + 128] = jnp.where(first, maps[4 + 2 * i], maps[5 + 2 * i])
        scores = dot_nt(bc[1], bc[0])
        for k in range(4):
            xv = pz[:, 128 + 128 * k : 256 + 128 * k]

            def within(q):
                spread = jnp.where(lower, cum[:, q : q + 1] - cum_t[q : q + 1, :], -1e30)
                mix = jnp.exp(spread) * dt_t[q : q + 1, :] * scores
                return dot_nn(mix.astype(BF16), xv)

            cols = slice(128 * k, 128 * k + 128)
            wi[:, cols] = jnp.where(first, within(2 * k), within(2 * k + 1))
            w = jnp.where(first, tail[:, 2 * k : 2 * k + 1], tail[:, 2 * k + 1 : 2 * k + 2])
            wt[:, cols] = (xv.astype(F32) * w).astype(BF16)
        fa["ecum"] = ecum

    def scan_b(k):
        ecum = fa["ecum"]
        lo, hi = 2 * k, 2 * k + 1
        cols = slice(128 * k, 128 * k + 128)
        first = lax.broadcasted_iota(jnp.int32, (256, 128), 1) < 64
        r128 = lax.broadcasted_iota(jnp.int32, (128, 128), 0) // 64
        c128 = lax.broadcasted_iota(jnp.int32, (128, 128), 1) // 64
        same = jnp.where(r128 == c128, 1.0 / 64.0, 0.0).astype(BF16)
        xf = pz[:, 128 + 128 * k : 256 + 128 * k].astype(F32)
        gate = pz[:, 640 + 128 * k : 768 + 128 * k].astype(F32)
        s_in = start[cols, :]
        decay = jnp.where(first, ecum[:, lo : lo + 1], ecum[:, hi : hi + 1])
        scanned = wi[:, cols] + decay * dot_nt(bc[1], s_in)
        skips = jnp.where(first, skip[lo], skip[hi])
        gated = (scanned + skips * xf) * (gate / (1.0 + jnp.exp(-gate)))
        sq = gated * gated
        sq_hi = sq.astype(BF16)
        sq_lo = (sq - sq_hi.astype(F32)).astype(BF16)
        meansq = dot_nn(sq_hi, same) + dot_nn(sq_lo, same)
        normed = (gated * lax.rsqrt(meansq + 1e-05) * gain[:, cols]).astype(BF16)
        upper, under = normed[:128], normed[128:]
        nbuf[z, k, :, half] = jnp.where(c == 0, upper, under)
        ns[k] = jnp.where(c == 0, under, upper)
        if k % 2 == 0:
            return
        j = k // 2
        both = pl.ds(2 * j, 2)
        dst = nbuf.at[z, both, :, half]
        nc[j, "pc"] = send(dst, dst, zp)
        nc[j, "mc"] = send(dst, dst, zm)
        nc[j, "pd"] = send(ns.at[both], dst, dev(y, m4(z + 1), x, 1 - c))
        nc[j, "md"] = send(ns.at[both], dst, dev(y, m4(z + 3), x, 1 - c))
        nc[j, "s"] = send(ns.at[both], dst, sib)

    def final():
        ecum = fa["ecum"]
        rows_first = lax.broadcasted_iota(jnp.int32, (128, 256), 0) < 64
        for k in range(4):
            cols = slice(128 * k, 128 * k + 128)
            lo, hi = 2 * k, 2 * k + 1
            last = jnp.where(rows_first, ecum[255:256, lo : lo + 1], ecum[255:256, hi : hi + 1])
            fin[cols, :] = last * start[cols, :].astype(F32) + dot_tn(wt[:, cols], bc[0])

        stores.append(pltpu.make_async_copy(fin, fin_out, ls.at[5]))
        stores[-1].start()

    def nf(j):
        nc[j, "pc"].wait_recv()
        nc[j, "pd"].wait_recv()
        fw = nbuf.at[m4(z + 3), pl.ds(2 * j, 2), pl.ds(0, 64)]
        nc[j, "fp"] = send(fw, fw, zp)
        nc[j, "mc"].wait_recv()
        nc[j, "md"].wait_recv()
        fw = nbuf.at[m4(z + 1), pl.ds(2 * j, 2), pl.ds(64, 64)]
        nc[j, "fm"] = send(fw, fw, zm)

    def ng():
        for j in range(2):
            nc[j, "fp"].wait_recv()
            nc[j, "fm"].wait_recv()

    def nw():
        for j in range(2):
            nc[j, "s"].wait_recv()

    xc = {}
    fr_sem = take(4)
    fin_copies = []

    def out_prod(zr, i):
        o = dot_nt(wo[i, 0], nbuf[zr, 0])
        for k in range(1, 4):
            o = o + dot_nt(wo[i, k], nbuf[zr, k])
        return o

    d_sem = take(8)
    direct = []

    def o_far():
        for ii in (2, 1, 3, 0):
            i = m4(x + ii)
            d2[ii] = out_prod(m4(z + 2), i).astype(BF16)
            cp = copy_of(d2.at[ii], h2.at[2 * ii + c], dev(y, m4(z + 2), i, zc), take(), d_sem + 2 * ii + c)
            cp.start()
            direct.append(cp)

    def far_in():
        @pl.when(c == m4(z + 2) // 2)
        def _():
            for cc in range(2):
                total = jnp.zeros((320, 128), F32)
                for ii in (0, 1, 3, 2):
                    q = 2 * ii + cc
                    copy_of(h2.at[q], h2.at[q], sib, hs_sem, d_sem + q).wait_recv()
                    total = total + h2[q].astype(F32)
                mt[pl.ds(mo(sz * 320, 64), 320), 128 * cc : 128 * cc + 128] = total.astype(BF16)

    def oa(rr):
        zr = m4(z + rr)

        def prod(ii):
            return out_prod(zr, m4(x + ii))

        o2[rr] = prod(2).astype(BF16)
        xc[rr, "2a"] = send(o2.at[rr, pl.ds(0, 160)], e2a.at[rr], xp)
        xc[rr, "2b"] = send(o2.at[rr, pl.ds(160, 160)], e2b.at[rr], xm)
        o = prod(1)
        k1[rr] = o[:160]
        o1[rr, 160:] = o[160:].astype(BF16)
        xc[rr, "1ah"] = send(o1.at[rr, pl.ds(160, 160)], e1a.at[rr, pl.ds(160, 160)], xp)
        o = prod(3)
        k3[rr] = o[160:]
        o3[rr, :160] = o[:160].astype(BF16)
        xc[rr, "1bl"] = send(o3.at[rr, pl.ds(0, 160)], e1b.at[rr, pl.ds(0, 160)], xm)
        k0[rr] = prod(0)

    def od(rr):
        xc[rr, "2a"].wait_recv()
        o1[rr, :160] = (k1[rr] + e2a[rr].astype(F32)).astype(BF16)
        xc[rr, "1al"] = send(o1.at[rr, pl.ds(0, 160)], e1a.at[rr, pl.ds(0, 160)], xp)
        xc[rr, "2b"].wait_recv()
        o3[rr, 160:] = (k3[rr] + e2b[rr].astype(F32)).astype(BF16)
        xc[rr, "1bh"] = send(o3.at[rr, pl.ds(160, 160)], e1b.at[rr, pl.ds(160, 160)], xm)

    def ox(rr):
        zr = m4(z + rr)
        o2[rr] = out_prod(zr, m4(x + 2)).astype(BF16)
        xc[rr, "2"] = send(o2.at[rr], e2.at[rr], dev(y, z, m4(x + 2), c))
        o1[rr] = out_prod(zr, m4(x + 1)).astype(BF16)
        xc[rr, "1a"] = send(o1.at[rr], e1a.at[rr], xp)
        o3[rr] = out_prod(zr, m4(x + 3)).astype(BF16)
        xc[rr, "1b"] = send(o3.at[rr], e1b.at[rr], xm)
        k0[rr] = out_prod(zr, x)

    def oxe(rr):
        for k in ("2", "1a", "1b"):
            xc[rr, k].wait_recv()
        home(rr, k0[rr] + e1a[rr].astype(F32) + e1b[rr].astype(F32) + e2[rr].astype(F32))

    def oe(rr):
        for k in ("1ah", "1bl", "1al", "1bh"):
            xc[rr, k].wait_recv()
        home(rr, k0[rr] + e1a[rr].astype(F32) + e1b[rr].astype(F32))

    def home(rr, total):
        fs[rr] = total.astype(BF16)
        dst = mt.at[pl.ds(mo(sz * 320, 64), 320), pl.ds(mo(c * 128, 128), 128)]
        cp = copy_of(fs.at[rr], dst, dev(y, m4(z + rr), x, zc), take(), fr_sem + 2 * sz + c)
        if rr == 0:

            @pl.when(c != zc)
            def _():
                cp.start()

            @pl.when(c == zc)
            def _():
                mt[pl.ds(mo(sz * 320, 64), 320), pl.ds(mo(c * 128, 128), 128)] = fs[0]
        else:
            cp.start()
        fin_copies.append((rr, cp))

    def of():
        for s in range(2):
            for cc in range(2):
                dst = mt.at[pl.ds(s * 320, 320), pl.ds(cc * 128, 128)]
                got = copy_of(dst, dst, sib, hs_sem, fr_sem + 2 * s + cc)
                local = ((z == 2 * c + s) & (c == cc)) | (m4(z + 2) == 2 * c + s)

                @pl.when(jnp.logical_not(local))
                def _(got=got):
                    got.wait_recv()

        stores.append(pltpu.make_async_copy(mt, mix_out, ls.at[6]))
        stores[-1].start()

    steps = dict(
        h0=h0,
        hf=hf,
        hg=hg,
        hs=hs,
        hw=hw,
        m0=m0,
        mw=mw,
        nf=nf,
        ng=ng,
        nw=nw,
        oa=oa,
        od=od,
        oe=oe,
        ox=ox,
        oxe=oxe,
        of=of,
        o_far=o_far,
        far_in=far_in,
        pa=pa,
        pb1=pb1,
        pb2=pb2,
        pd=pd,
        s0=s0,
        s1=s1,
        s2=s2,
        s3=s3,
        s4=s4,
        scan_a=scan_a,
        scan_b=scan_b,
        final=final,
        w0=w0,
        s_pick=s_pick,
        w_init=w_init,
        wf=wf,
        wg=wg,
        wo0=wo0,
        wof=wof,
        wog=wog,
        wow=wow,
    )
    loads[0].wait()
    loads[1].wait()
    w_cat()
    loads[3].wait()
    pl.semaphore_wait(barrier, len(peers))
    pl.semaphore_signal(tier, inc=1, device_id=zm, device_id_type=MESH)
    w0(0)
    h0_near()

    for step in ORDER:
        name, *args = step.split()
        steps[name](*map(int, args))

    for cp in sent:
        cp.finish()
    for cp in stores:
        cp.wait()
    for cp in map_copies + direct:
        cp.wait_send()
    for local, _, cp in h0_local:

        @pl.when(jnp.logical_not(local))
        def _(cp=cp):
            cp.wait_send()

    for rr, cp in fin_copies:
        if rr == 0:

            @pl.when(c != zc)
            def _(cp=cp):
                cp.wait_send()
        else:
            cp.wait_send()


def finish_body(mixed_t, final, mixed_out, final_out, mixed, sems):
    copies = [
        pltpu.make_async_copy(final, final_out, sems.at[0]),
        pltpu.make_async_copy(mixed, mixed_out, sems.at[1]),
    ]
    copies[0].start()
    mixed[...] = mixed_t[...].T
    copies[1].start()
    for cp in copies:
        cp.wait()


def shards(hidden, snap_map, pool_states, w_zx, w_bc, w_dt, dt_bias, decay_rate, skip, norm_gain, w_out):
    vm = pl.BlockSpec(memory_space=VMEM)
    sm = pl.BlockSpec(memory_space=pltpu.SMEM)
    hbm = pl.BlockSpec(memory_space=pl.ANY)
    scratch = [
        VMEM((256, 640), BF16),
        VMEM((320, 2, 512), BF16),
        VMEM((320, 512), BF16),
        VMEM((320, 512), BF16),
        VMEM((8, 512, 256), BF16),
        VMEM((320, 3 * CH), BF16),
        VMEM((1024, 1536), BF16),
        VMEM((1536, 3 * CH), BF16),
        *[VMEM((3, 256, CH), BF16)] * 3,
        *[VMEM((3, 128, CH), BF16)] * 2,
        *[VMEM((3, 256, CH), BF16)] * 2,
        *[VMEM((3, 128, CH), F32)] * 2,
        VMEM((256, 3 * CH), BF16),
        VMEM((8, 256, 128), BF16),
        *[tuple(VMEM((4, n, 256), BF16) for n in ROWS)] * 4,
        *[tuple(VMEM((2, n, 256), BF16) for n in ROWS)] * 2,
        *[tuple(VMEM((4, n, 256), BF16) for n in ROWS)] * 2,
        *[tuple(VMEM((n, 256), BF16) for n in ROWS)] * 3,
        *[VMEM((ROWS[1] // 2, 256), BF16)] * 2,
        VMEM((512, 256), BF16),
        VMEM((256, 512), F32),
        VMEM((256, 512), BF16),
        VMEM((2, 256, 256), BF16),
        VMEM((4, 128, 128), BF16),
        VMEM((4, 4, 128, 256), BF16),
        VMEM((4, 4, 320, 256), BF16),
        VMEM((4, 320, 128), BF16),
        VMEM((8, 320, 128), BF16),
        VMEM((4, 320, 128), F32),
        *[VMEM((4, 160, 128), F32)] * 2,
        *[VMEM((4, 320, 128), BF16)] * 3,
        *[VMEM((4, 160, 128), BF16)] * 2,
        *[VMEM((4, 320, 128), BF16)] * 4,
        VMEM((640, 256), BF16),
        VMEM((512, 256), F32),
        pltpu.SemaphoreType.DMA((N_SEM,)),
        pltpu.SemaphoreType.DMA((N_SEM,)),
        pltpu.SemaphoreType.DMA((7,)),
        pltpu.SemaphoreType.REGULAR,
    ]
    mixed_t, final = pl.pallas_call(
        body,
        out_shape=(jax.ShapeDtypeStruct((640, 256), BF16), jax.ShapeDtypeStruct((512, 256), F32)),
        in_specs=[sm] * 4 + [vm] * 2 + [hbm] * 5,
        out_specs=(hbm, hbm),
        scratch_shapes=scratch,
        compiler_params=pltpu.CompilerParams(
            collective_id=0, has_side_effects=True, vmem_limit_bytes=56 * 1024 * 1024
        ),
    )(
        snap_map,
        dt_bias,
        decay_rate,
        skip,
        norm_gain.reshape(1, 512),
        w_dt.T,
        hidden.reshape(256, 640),
        w_zx,
        w_bc,
        w_out.T,
        pool_states.reshape(8, 512, 256),
    )
    mixed, final = pl.pallas_call(
        finish_body,
        out_shape=(jax.ShapeDtypeStruct((256, 640), BF16), jax.ShapeDtypeStruct((512, 256), F32)),
        in_specs=[vm, vm],
        out_specs=(hbm, hbm),
        scratch_shapes=[VMEM((256, 640), BF16), pltpu.SemaphoreType.DMA((2,))],
    )(mixed_t, final)
    return mixed.reshape(1, 256, 640), final.reshape(1, 8, 64, 256)


def solution(mesh):
    in_specs = (
        P("pool", None, "head"),
        P(),
        P("pool", "head", None, None),
        P("pool", None, "head"),
        P("pool", None),
        P("pool", "head"),
        P("head"),
        P("head"),
        P("head"),
        P("head"),
        P("head", "pool"),
    )
    out_specs = (P("pool", None, "head"), P("pool", "head", None, None))
    return jax.shard_map(shards, mesh=mesh, in_specs=in_specs, out_specs=out_specs, check_vma=False)
```
